32 devices in a mesh: dom: 8 (over z, x), tile: 4 (over y, core).
Axes of the slice: x: 2, y: 2, z: 4, core: 2. Of those that a mesh axis runs over, the one named last changes fastest.
Arguments:
- krylov_block: float32 [96, 32, 128], P('dom'), may hold values from -6 to 6
- diag_block: float32 [96, 128, 128], P(('dom', 'tile')), may hold values from -0.031819805 to 4.03182
- inverse_prev: float32 [96, 128, 128], P(('dom', 'tile')), may hold values from -0.01767767 to 0.951011
- coupling_tiles: float32 [96, 8, 128, 128], P('dom', 'tile'), may hold values from -0.14142136 to 0.14142136
- slot_kind: int32 [96, 8], P('dom', 'tile'), may hold values from 0 to 2, as said below
- slot_link: int32 [96, 8], P('dom', 'tile'), may hold values from 0 to 31, as said below
- send_slots: int32 [8, 4, 4, 4], P('dom', 'tile'), may hold values from 0 to 23, as said below
Outputs:
- inverse_new: float32 [96, 128, 128], P(('dom', 'tile'))
- applied: float32 [96, 32, 128], P('dom')
The draws below stay inside these ranges and needn't reach their ends.
Inputs may be any that keep to these rules, and one draw needn't show every extreme that they name: `slot_kind`: every live slot has exactly one partner as stated, in the same tile group and in a partition at most two away; partners never lie outside the partitions 0 .. 7. `slot_link`: links of empty slots are 0. `send_slots`: entry [p, g, l, j] is a slot position of partition p in group g. Lists 0 and 1 name upper slots whose partners lie in partition p + 1 and p + 2, lists 2 and 3 lower slots whose partners lie in p - 1 and p - 2; the four lists and the partition's own pairs use distinct positions. Some list reaches 4 live entries in every draw.
All inputs are finite; a program needn't handle non-finite values.
Results may differ from the reference program's by a relative error of at most 0.0003.
Values sent between devices are 32-bit elements; how exact they have to be, the bound alone decides.
No kernel may reach another device: no remote copies, remote signals or barrier semaphores. Data moves between devices by JAX's collectives and lax.ppermute only.
A program may use at most 64 MiB of HBM per device.

```python
import jax
import jax.numpy as jnp
from jax import lax

BLK = 128
VECS = 32
RB = 12
KD = 2
FSWEEPS = 2
LSWEEPS = 3
USWEEPS = 3
NB = 96
N_DOM = 8
N_TILE = 4


def slot_pattern(key):
    base = jax.random.fold_in(key, 7151)
    slot_total = RB * KD
    capacity = RB * KD // 5
    local_pairs = (slot_total - 4 * capacity) // 2
    device_keys = jax.random.split(jax.random.fold_in(base, 1), N_DOM * N_TILE)
    orders = jax.vmap(lambda item: jax.random.permutation(item, slot_total))(device_keys)
    orders = orders.reshape(N_DOM, N_TILE, slot_total).astype(jnp.int32)
    coins = jax.random.randint(jax.random.fold_in(base, 2), (2, N_DOM, N_TILE, capacity), 0, 10)
    salt = jax.random.randint(jax.random.fold_in(base, 3), (), 0, 4)
    domain_ids = jnp.arange(N_DOM, dtype=jnp.int32)[:, None, None]
    group_ids = jnp.arange(N_TILE, dtype=jnp.int32)[None, :, None]
    filled = (domain_ids + group_ids + salt) % 4 == 0
    reach = jnp.stack([domain_ids + 1 < N_DOM, domain_ids + 2 < N_DOM])
    live = ((coins < 7) | filled[None]) & reach
    lower_near = jnp.concatenate([jnp.zeros_like(live[0, :1]), live[0, :-1]], 0)
    lower_far = jnp.concatenate([jnp.zeros_like(live[1, :2]), live[1, :-2]], 0)
    kinds = jnp.zeros((N_DOM, N_TILE, slot_total), jnp.int32)
    links = jnp.zeros((N_DOM, N_TILE, slot_total), jnp.int32)
    domain_index = jnp.broadcast_to(domain_ids, (N_DOM, N_TILE, capacity))
    group_index = jnp.broadcast_to(group_ids, (N_DOM, N_TILE, capacity))
    offsets = jnp.arange(capacity, dtype=jnp.int32)[None, None, :]
    plan = ((0, 2, live[0], 0), (1, 2, live[1], capacity), (2, 1, lower_near, 0), (3, 1, lower_far, capacity))
    for list_no, side_code, active, shift_by in plan:
        places = orders[:, :, list_no * capacity:(list_no + 1) * capacity]
        kinds = kinds.at[domain_index, group_index, places].set(side_code * active.astype(jnp.int32))
        links = links.at[domain_index, group_index, places].set(jnp.where(active, slot_total + shift_by + offsets, 0))
    pair_coins = jax.random.randint(jax.random.fold_in(base, 4), (N_DOM, N_TILE, local_pairs), 0, 10) < 8
    start = 4 * capacity
    first = orders[:, :, start:start + 2 * local_pairs:2]
    second = orders[:, :, start + 1:start + 2 * local_pairs:2]
    usable = pair_coins & (first // KD != second // KD)
    lower_place = jnp.where(first // KD > second // KD, first, second)
    upper_place = jnp.where(first // KD > second // KD, second, first)
    pair_domain = jnp.broadcast_to(domain_ids, (N_DOM, N_TILE, local_pairs))
    pair_group = jnp.broadcast_to(group_ids, (N_DOM, N_TILE, local_pairs))
    kinds = kinds.at[pair_domain, pair_group, lower_place].set(jnp.where(usable, 1, 0))
    links = links.at[pair_domain, pair_group, lower_place].set(jnp.where(usable, upper_place, 0))
    kinds = kinds.at[pair_domain, pair_group, upper_place].set(jnp.where(usable, 2, 0))
    links = links.at[pair_domain, pair_group, upper_place].set(jnp.where(usable, lower_place, 0))
    sending = jnp.stack([orders[:, :, j * capacity:(j + 1) * capacity] for j in range(4)], 2)
    kind_out = kinds.reshape(N_DOM, N_TILE, RB, KD).transpose(0, 2, 1, 3).reshape(RB * N_DOM, N_TILE * KD)
    link_out = links.reshape(N_DOM, N_TILE, RB, KD).transpose(0, 2, 1, 3).reshape(RB * N_DOM, N_TILE * KD)
    return (kind_out.astype(jnp.int32), link_out.astype(jnp.int32), sending.astype(jnp.int32))


def pivot_pattern(key):
    base = jax.random.fold_in(key, 3301)
    row_total = RB * N_DOM
    pivot_gains = jnp.exp(jax.random.uniform(jax.random.fold_in(base, 1), (row_total, BLK), minval=jnp.log(1.5), maxval=jnp.log(4.0)))
    identity = jnp.eye(BLK, dtype=jnp.float32)
    jitter = 0.09 * BLK ** (-0.5) * jax.random.truncated_normal(jax.random.fold_in(base, 2), -4.0, 4.0, (row_total, BLK, BLK))
    diagonal = pivot_gains[:, :, None] * identity + jitter
    wobble = 1.0 + 0.2 * jax.random.truncated_normal(jax.random.fold_in(base, 3), -2.0, 2.0, (row_total, BLK))
    scatter_part = 0.05 * BLK ** (-0.5) * jax.random.truncated_normal(jax.random.fold_in(base, 4), -4.0, 4.0, (row_total, BLK, BLK))
    inverse = (wobble / pivot_gains)[:, :, None] * identity + scatter_part
    return (diagonal.astype(jnp.float32), inverse.astype(jnp.float32))


def draw_slot_kind(key, part):
    return slot_pattern(key)[0]


def draw_slot_link(key, part):
    return slot_pattern(key)[1]


def draw_send_slots(key, part):
    return slot_pattern(key)[2]


def draw_diag_block(key, part):
    return pivot_pattern(key)[0]


def draw_inverse_prev(key, part):
    return pivot_pattern(key)[1]


def steps_of(own_key, shape, cuts, least, largest):
    gain, own = 1.0, jax.random.fold_in(own_key, 6)
    for dim, shards_of in cuts:
        steps = jnp.exp(jax.random.uniform(jax.random.fold_in(own, dim), (shards_of,), jnp.float32, least / len(cuts), largest / len(cuts)))
        gain = gain * jnp.repeat(steps, shape[dim] // shards_of).reshape([-1 if axis == dim else 1 for axis in range(len(shape))])
    return gain


def noise(own_key, shape, scale, bound, cuts=(), held_as=jnp.bfloat16):
    entries = jax.random.normal(own_key, shape, jnp.float32) * scale
    if len(cuts) > 0:
        entries = steps_of(own_key, shape, cuts, -0.22, 0.18) * entries
    return jnp.clip(entries, min=-bound, max=bound).astype(held_as)


def setup_inputs(seed: int = 0) -> dict:
    seeds = jax.random.split(jax.random.key(seed), 8)
    return {
        "krylov_block": noise(seeds[0], (NB, VECS, BLK), 1.0, 6.0, ((0, 8),), jnp.float32),
        "diag_block": draw_diag_block(jax.random.fold_in(seeds[7], 71), 0),
        "inverse_prev": draw_inverse_prev(jax.random.fold_in(seeds[7], 71), 0),
        "coupling_tiles": noise(seeds[3], (NB, N_TILE * KD, BLK, BLK), (0.6 * BLK ** -0.5), 0.14142136, ((0, 8), (1, 4)), jnp.float32),
        "slot_kind": draw_slot_kind(jax.random.fold_in(seeds[7], 71), 0),
        "slot_link": draw_slot_link(jax.random.fold_in(seeds[7], 71), 0),
        "send_slots": draw_send_slots(jax.random.fold_in(seeds[7], 71), 0),
    }


precise = lax.Precision.HIGHEST


def newton_step(inverse, pivot):
    product = jnp.matmul(inverse, pivot, precision=precise)
    return 2.0 * inverse - jnp.matmul(product, inverse, precision=precise)


def apply_inverse(inverse, vectors):
    return jnp.einsum("rvj,rij->rvi", vectors, inverse, precision=precise)


def reference(krylov_block, diag_block, inverse_prev, coupling_tiles, slot_kind, slot_link, send_slots):
    block_size = coupling_tiles.shape[2]
    vector_count = krylov_block.shape[1]
    slot_total = RB * KD
    group_tiles = coupling_tiles.reshape(N_DOM, RB, N_TILE, KD, block_size, block_size)
    group_kind = slot_kind.reshape(N_DOM, RB, N_TILE, KD).transpose(0, 2, 1, 3).reshape(N_DOM, N_TILE, slot_total)
    group_link = slot_link.reshape(N_DOM, RB, N_TILE, KD).transpose(0, 2, 1, 3).reshape(N_DOM, N_TILE, slot_total)
    row_source = jnp.where(group_link < slot_total, group_link // KD, group_link - slot_total + RB).astype(jnp.int32)
    send_rows = (send_slots // KD).astype(jnp.int32)
    domains = jnp.arange(N_DOM, dtype=jnp.int32)
    diag_rows = diag_block.reshape(N_DOM, RB, block_size, block_size)

    def tiles_of(domain, side_code):
        local_tiles = group_tiles[domain].transpose(1, 0, 2, 3, 4).reshape(N_TILE, slot_total, block_size, block_size)
        return local_tiles * (group_kind[domain] == side_code).astype(jnp.float32)[:, :, None, None]

    def sent_products(inverse_rows, domain, which):
        source = jnp.clip(domain, 0, N_DOM - 1)
        valid = ((domain >= 0) & (domain < N_DOM)).astype(jnp.float32)
        upper_tiles = tiles_of(source, 2)
        picked_slots = send_slots[source, :, which].astype(jnp.int32)
        picked = jnp.take_along_axis(upper_tiles, picked_slots[:, :, None, None], axis=1)
        picked_inverse = inverse_rows[source][picked_slots // KD]
        return valid * jnp.einsum("tcij,tcjk->tcik", picked_inverse, picked, precision=precise)

    def pivots_of(inverse_rows):
        def one_domain(domain):
            repeated = jnp.repeat(inverse_rows[domain], KD, axis=0)
            products = jnp.einsum("cij,tcjk->tcik", repeated, tiles_of(domain, 2), precision=precise)
            near_part = sent_products(inverse_rows, domain - 1, 0)
            far_part = sent_products(inverse_rows, domain - 2, 1)
            lookup = jnp.concatenate([products, near_part, far_part], axis=1)
            gathered = jnp.take_along_axis(lookup, group_link[domain][:, :, None, None], axis=1)
            terms = jnp.einsum("tcij,tcjk->tcik", tiles_of(domain, 1), gathered, precision=precise)
            sums = terms.reshape(N_TILE, RB, KD, block_size, block_size).sum(axis=(0, 2))
            return diag_rows[domain] - sums
        return lax.map(one_domain, domains).reshape(RB * N_DOM, block_size, block_size)

    def neighbour_sum(values, side_code, direction, list_pair):
        grouped = values.reshape(N_DOM, RB, vector_count, block_size)

        def one_domain(domain):
            local_vals = grouped[domain]
            pieces = [jnp.broadcast_to(local_vals, (N_TILE,) + local_vals.shape)]
            for step_no, list_no in ((1, list_pair[0]), (2, list_pair[1])):
                target = domain - direction * step_no
                source = jnp.clip(target, 0, N_DOM - 1)
                valid = ((target >= 0) & (target < N_DOM)).astype(jnp.float32)
                pieces.append(valid * grouped[source][send_rows[source, :, list_no]])
            lookup = jnp.concatenate(pieces, axis=1)
            gathered = jnp.take_along_axis(lookup, row_source[domain][:, :, None, None], axis=1)
            terms = jnp.einsum("tcvj,tcij->tcvi", gathered, tiles_of(domain, side_code), precision=precise)
            return terms.reshape(N_TILE, RB, KD, vector_count, block_size).sum(axis=(0, 2))
        return lax.map(one_domain, domains).reshape(RB * N_DOM, vector_count, block_size)

    inverse = inverse_prev
    for sweep_no in range(FSWEEPS):
        pivots = pivots_of(inverse.reshape(N_DOM, RB, block_size, block_size))
        inverse = newton_step(inverse, pivots)
    lower_y = krylov_block
    for sweep_no in range(LSWEEPS):
        scaled = apply_inverse(inverse, lower_y)
        lower_y = krylov_block - neighbour_sum(scaled, 1, 1, (0, 1))
    solved = apply_inverse(inverse, lower_y)
    for sweep_no in range(USWEEPS):
        solved = apply_inverse(inverse, lower_y - neighbour_sum(solved, 2, -1, (2, 3)))
    return inverse, solved
```

```python
import functools

import jax
import jax.numpy as jnp
from jax import lax
from jax.experimental import pallas as pl
from jax.experimental.pallas import tpu as pltpu
from jax.sharding import PartitionSpec as P

FSWEEPS = 2
LSWEEPS = 3
USWEEPS = 3
F32 = jnp.float32
BF16 = jnp.bfloat16


def split(a):
    hi = a.astype(BF16)
    return hi, (a - hi.astype(F32)).astype(BF16)


def matmul_parts(ah, al, bh, bl):
    lhs = jnp.concatenate([ah, al], 1)
    pair = jnp.concatenate([bh, bl], 1)
    rhs = jnp.concatenate([pair, pair], 0)
    out = jnp.dot(lhs, rhs, preferred_element_type=F32)
    n = bh.shape[1]
    return out[:, :n] + out[:, n:]


def matmul(a, b):
    return matmul_parts(*split(a), *split(b))


def times_tile(x, wide):
    v, n = x.shape
    stacked = jnp.concatenate(split(x), 0)
    out = lax.dot_general(stacked, wide, (((1,), (1,)), ((), ())), preferred_element_type=F32)
    return out[:v, :n] + (out[v:, :n] + out[:v, n:])


def widen(a):
    return jnp.concatenate(split(a), 0)


class Layout:
    def __init__(self, rows, width, cap, n_tile):
        self.rows, self.width, self.cap, self.n_tile = rows, width, cap, n_tile
        self.slots = rows * width
        self.own_rows = rows // n_tile
        self.n_link = self.slots
        self.n_send = 2 * self.slots

    def kind(self, meta, s):
        return meta[s]

    def link(self, meta, s):
        return meta[self.n_link + s]

    def listed(self, meta, which, j):
        return meta[self.n_send + which * self.cap + j]

    def place(self, r, me):
        far = (r // self.own_rows) ^ me
        return ((far & 1) * (self.n_tile // 2) + (far >> 1)) * self.own_rows + r % self.own_rows

    def lookup(self, meta, role, base_list, side, j):
        s = self.listed(meta, base_list + role, j)
        v = self.link(meta, s) - self.slots - role * self.cap
        live = (self.kind(meta, s) == side) & (v >= 0) & (v < self.cap)
        return s, s // self.width, live, jnp.clip(v, 0, self.cap - 1)


def smem():
    return pl.BlockSpec(memory_space=pltpu.SMEM)


def vmem():
    return pl.BlockSpec(memory_space=pltpu.VMEM)


def call(body, outs, scalars, arrays, flops=0, scratch=()):
    moved = sum(a.size * a.dtype.itemsize for a in arrays) + sum(o.size * o.dtype.itemsize for o in outs)
    return pl.pallas_call(
        body,
        out_shape=outs,
        in_specs=[smem()] * len(scalars) + [vmem()] * len(arrays),
        out_specs=[vmem()] * len(outs),
        scratch_shapes=list(scratch),
        compiler_params=pltpu.CompilerParams(vmem_limit_bytes=24 << 20),
        cost_estimate=pl.CostEstimate(flops=flops, bytes_accessed=moved, transcendentals=0),
    )(*scalars, *arrays)


def pack_kernel(lay, me, mine, mates, tiles, mate_tiles, lower, upper):
    role = me[0] % 2
    for base, side, out in ((2, 1, lower), (0, 2, upper)):
        for g, (meta, source) in enumerate(((mine, tiles), (mates, mate_tiles))):
            for j in range(lay.cap):
                s, _, live, _ = lay.lookup(meta, role, base, side, j)
                out[g * lay.cap + j] = widen(jnp.where(live, source[s], 0.0))


def outgoing_kernel(lay, me, mine, mates, inverse, upper, out):
    role = me[0] % 2
    n = inverse.shape[1]
    for g, meta in enumerate((mine, mates)):
        for j in range(lay.cap):
            _, r, _, _ = lay.lookup(meta, role, 0, 2, j)
            k = g * lay.cap + j
            out[k] = matmul_parts(*split(inverse[lay.place(r, me[0])]), upper[k, :n], upper[k, n:])


def local_pivot_kernel(lay, me, mine, inverse, tiles, out):
    out[...] = jnp.zeros_like(out)

    @pl.loop(0, lay.slots)
    def _(s):
        v = lay.link(mine, s)

        @pl.when((lay.kind(mine, s) == 1) & (v < lay.slots))
        def _():
            q = matmul(inverse[lay.place(v // lay.width, me[0])], tiles[v])
            out[lay.place(s // lay.width, me[0])] += matmul(tiles[s], q)


def incoming_kernel(lay, me, mine, mates, local, lower, arrived, keep, give, total):
    role = me[0] % 2
    n = lower.shape[2]
    total[...] = local[...]
    for g, meta in enumerate((mine, mates)):
        for j in range(lay.cap):
            _, r, _, v = lay.lookup(meta, role, 2, 1, j)
            k = g * lay.cap + j
            total[lay.place(r, me[0])] += matmul_parts(
                lower[k, :n], lower[k, n:], *split(arrived[g * lay.cap + v])
            )
    half = keep.shape[0]
    keep[...] = total[:half]
    give[...] = total[half:]


def newton_kernel(inverse, diag, sums, out):
    for i in range(out.shape[0]):
        x = inverse[i]
        xh, xl = split(x)
        product = matmul_parts(xh, xl, *split(diag[i] - sums[i]))
        out[i] = 2.0 * x - matmul_parts(*split(product), xh, xl)


def apply_kernel(lay, list_base, n_sums, me, mine, mates, base, *refs):
    sums, (inverse, out, send, rest) = refs[:n_sums], refs[n_sums:]
    role = me[0] % 2
    for r in range(lay.rows):
        u = base[r]
        if sums:
            u = u - sum(s[r] for s in sums)
        rest[r] = u
        out[r] = times_tile(u, widen(inverse[lay.place(r, me[0])]))
    if send is not None:
        for g, meta in enumerate((mine, mates)):
            for j in range(lay.cap):
                r = lay.listed(meta, list_base + role, j) // lay.width
                send[g * lay.cap + j] = out[r]


def last_apply_kernel(lay, n_sums, me, base, *refs):
    sums, (inverse, out) = refs[:n_sums], refs[n_sums:]
    for r in range(lay.rows):
        u = base[r] - sum(s[r] for s in sums)
        out[r] = times_tile(u, widen(inverse[lay.place(r, me[0])]))


def local_vector_kernel(lay, side, mine, x, tiles, out):
    out[...] = jnp.zeros_like(out)

    @pl.loop(0, lay.slots)
    def _(s):
        v = lay.link(mine, s)

        @pl.when((lay.kind(mine, s) == side) & (v < lay.slots))
        def _():
            out[s // lay.width] += times_tile(x[v // lay.width], widen(tiles[s]))


def arrived_vector_kernel(lay, list_base, side, me, mine, mates, local, tiles, arrived, out):
    role = me[0] % 2
    out[...] = local[...]
    for g, meta in enumerate((mine, mates)):
        for j in range(lay.cap):
            _, r, _, v = lay.lookup(meta, role, list_base, side, j)
            k = g * lay.cap + j
            out[r] += times_tile(arrived[g * lay.cap + v], tiles[k])


def local(krylov_block, diag_block, inverse_prev, coupling_tiles, slot_kind, slot_link, send_slots):
    rows, width, n, _ = coupling_tiles.shape
    cap = send_slots.shape[3]
    n_dom, n_tile = lax.axis_size("dom"), lax.axis_size("tile")
    lay = Layout(rows, width, cap, n_tile)
    vectors = krylov_block.shape[1]
    upper_bits = [1 << b for b in range(1, n_tile.bit_length() - 1)]

    me = lax.axis_index("tile").astype(jnp.int32).reshape(1)
    mine = jnp.concatenate([slot_kind.reshape(-1), slot_link.reshape(-1), send_slots.reshape(-1)])
    tiles = coupling_tiles.reshape(lay.slots, n, n)

    def swap(x, bit):
        return lax.ppermute(x, "tile", [(i, i ^ bit) for i in range(n_tile)])

    def along(x, sign):
        route = []
        for d in range(n_dom):
            for t in range(n_tile):
                to = d + sign * (1 + t % 2)
                if 0 <= to < n_dom:
                    route.append((d * n_tile + t, to * n_tile + t))
        return lax.ppermute(x, ("dom", "tile"), route)

    def spread(x):
        for bit in upper_bits:
            x = jnp.concatenate([x, swap(x, bit)], 0)
        return x

    def summed(x, chunked):
        for bit in upper_bits:
            got = swap(x, bit)
            if chunked:
                near = bit // 2
                got = got.reshape((n_tile // 2 // (2 * near), 2, near * lay.own_rows) + x.shape[1:])
                got = jnp.concatenate([got[:, 1:], got[:, :1]], 1).reshape(x.shape)
            x = x + got
        return x

    def shape(*dims, dtype=F32):
        return jax.ShapeDtypeStruct(dims, dtype)

    kernel = lambda body, *bound: functools.partial(body, lay, *bound)

    mates = swap(mine, 1)
    mate_tiles = swap(tiles, 1)
    kept = spread(inverse_prev)
    diag = spread(diag_block)
    lower, upper = call(
        kernel(pack_kernel),
        [shape(2 * cap, 2 * n, n, dtype=BF16)] * 2,
        (me, mine, mates),
        (tiles, mate_tiles),
    )
    half = rows // 2
    for _ in range(FSWEEPS):
        inverse = jnp.concatenate([kept, swap(kept, 1)], 0)
        (out,) = call(kernel(outgoing_kernel), [shape(2 * cap, n, n)], (me, mine, mates), (inverse, upper))
        arrived = along(out, 1)
        (here,) = call(
            kernel(local_pivot_kernel), [shape(rows, n, n)], (me, mine), (inverse, tiles), flops=8 * 2 * n**3 * rows
        )
        keep, give = call(
            kernel(incoming_kernel),
            [shape(half, n, n)] * 2,
            (me, mine, mates),
            (here, lower, arrived),
            scratch=(pltpu.VMEM((rows, n, n), F32),),
        )
        sums = summed(keep + swap(give, 1), True)
        (kept,) = call(newton_kernel, [shape(half, n, n)], (), (kept, diag, sums))
    inverse = jnp.concatenate([kept, swap(kept, 1)], 0)

    block = shape(rows, vectors, n)
    sent = shape(2 * cap, vectors, n)

    def apply(base, sums, list_base):
        return call(
            kernel(apply_kernel, list_base, len(sums)),
            [block, sent, block],
            (me, mine, mates),
            (base, *sums, inverse),
        )

    def neighbour_sum(x, send, side):
        arrived = along(send, 1 if side == 1 else -1)
        (here,) = call(
            kernel(local_vector_kernel, side), [block], (mine,), (x, tiles), flops=4 * 2 * n**2 * vectors * rows
        )
        (part,) = call(
            kernel(arrived_vector_kernel, 2 if side == 1 else 0, side),
            [block],
            (me, mine, mates),
            (here, lower if side == 1 else upper, arrived),
        )
        part = part + swap(part, 1)
        for bit in upper_bits[:-1]:
            part = part + swap(part, bit)
        return part, swap(part, upper_bits[-1])

    x, send, _ = apply(krylov_block, (), 0)
    for sweep in range(LSWEEPS):
        sums = neighbour_sum(x, send, 1)
        x, send, y = apply(krylov_block, sums, 0 if sweep < LSWEEPS - 1 else 2)
    for sweep in range(USWEEPS):
        sums = neighbour_sum(x, send, 2)
        if sweep < USWEEPS - 1:
            x, send, _ = apply(y, sums, 2)
        else:
            (x,) = call(kernel(last_apply_kernel, len(sums)), [block], (me,), (y, *sums, inverse))
    return (kept[: lay.own_rows], x)


def solution(mesh):
    placed = (
        P("dom", None, None),
        P(("dom", "tile"), None, None),
        P(("dom", "tile"), None, None),
        P("dom", "tile", None, None),
        P("dom", "tile"),
        P("dom", "tile"),
        P("dom", "tile", None, None),
    )
    return jax.shard_map(
        local,
        mesh=mesh,
        in_specs=placed,
        out_specs=(P(("dom", "tile"), None, None), P("dom", None, None)),
        check_vma=False,
    )
```

```python
import functools

import jax
import jax.numpy as jnp
from jax import lax
from jax.experimental import pallas as pl
from jax.experimental.pallas import tpu as pltpu
from jax.sharding import PartitionSpec as P

FSWEEPS = 2
LSWEEPS = 3
USWEEPS = 3
F32 = jnp.float32
BF16 = jnp.bfloat16


def split(a):
    hi = a.astype(BF16)
    return hi, (a - hi.astype(F32)).astype(BF16)


def matmul_parts(ah, al, bh, bl):
    lhs = jnp.concatenate([ah, al], 1)
    pair = jnp.concatenate([bh, bl], 1)
    rhs = jnp.concatenate([pair, pair], 0)
    out = jnp.dot(lhs, rhs, preferred_element_type=F32)
    n = bh.shape[1]
    return out[:, :n] + out[:, n:]


def matmul(a, b):
    return matmul_parts(*split(a), *split(b))


def times_tile(x, wide):
    v, n = x.shape
    stacked = jnp.concatenate(split(x), 0)
    out = lax.dot_general(stacked, wide, (((1,), (1,)), ((), ())), preferred_element_type=F32)
    return out[:v, :n] + (out[v:, :n] + out[:v, n:])


def widen(a):
    return jnp.concatenate(split(a), 0)


class Layout:
    def __init__(self, rows, width, cap, n_tile):
        self.rows, self.width, self.cap, self.n_tile = rows, width, cap, n_tile
        self.slots = rows * width
        self.own_rows = rows // n_tile
        self.n_link = self.slots
        self.n_send = 2 * self.slots
        self.listed_slots = n_tile * cap
        self.pairs = self.slots // 2
        self.usual = min(self.pairs, max(1, (self.slots - 4 * cap) // 2))
        self.table = 3 * self.listed_slots + n_tile * self.pairs + n_tile // 2

    def kind(self, meta, s):
        return meta[s]

    def link(self, meta, s):
        return meta[self.n_link + s]

    def listed(self, meta, which, j):
        return meta[self.n_send + which * self.cap + j]

    def place(self, r, me):
        far = (r // self.own_rows) ^ me
        return ((far & 1) * (self.n_tile // 2) + (far >> 1)) * self.own_rows + r % self.own_rows

    def lookup(self, meta, role, base_list, side, j):
        s = self.listed(meta, base_list + role, j)
        v = self.link(meta, s) - self.slots - role * self.cap
        live = (self.kind(meta, s) == side) & (v >= 0) & (v < self.cap)
        return s, s // self.width, live, jnp.clip(v, 0, self.cap - 1)


def smem():
    return pl.BlockSpec(memory_space=pltpu.SMEM)


def vmem():
    return pl.BlockSpec(memory_space=pltpu.VMEM)


def call(body, outs, scalars, arrays, flops=0, scratch=(), early=()):
    moved = sum(a.size * a.dtype.itemsize for a in arrays) + sum(o.size * o.dtype.itemsize for o in outs)
    return pl.pallas_call(
        body if not early else lambda *refs: body(*refs[len(early) :]),
        out_shape=outs,
        in_specs=[pl.BlockSpec(memory_space=pl.ANY)] * len(early) + [smem()] * len(scalars) + [vmem()] * len(arrays),
        out_specs=[vmem()] * len(outs),
        scratch_shapes=list(scratch),
        compiler_params=pltpu.CompilerParams(vmem_limit_bytes=8 << 20),
        cost_estimate=pl.CostEstimate(flops=flops, bytes_accessed=moved, transcendentals=0),
    )(*early, *scalars, *arrays)


def outgoing_kernel(lay, me, mine, mates, inverse, tiles, mate_tiles, out):
    role = me[0] % 2
    for g, (meta, source) in enumerate(((mine, tiles), (mates, mate_tiles))):
        for j in range(lay.cap):
            s, r, live, _ = lay.lookup(meta, role, 0, 2, j)
            out[g * lay.cap + j] = matmul(inverse[lay.place(r, me[0])], jnp.where(live, source[s], 0.0))


def local_pivot_kernel(lay, me, mine, inverse, diag, tiles, out):
    out[: lay.own_rows] = -diag[...]
    out[lay.own_rows :] = jnp.zeros((lay.rows - lay.own_rows,) + diag.shape[1:], F32)

    @pl.loop(0, lay.slots)
    def _(s):
        v = lay.link(mine, s)

        @pl.when((lay.kind(mine, s) == 1) & (v < lay.slots))
        def _():
            q = matmul(inverse[lay.place(v // lay.width, me[0])], tiles[v])
            out[lay.place(s // lay.width, me[0])] += matmul(tiles[s], q)


def incoming_kernel(lay, me, mine, mates, local, tiles, mate_tiles, arrived, keep, give, total):
    role = me[0] % 2
    places, terms = [], []
    for g, (meta, source) in enumerate(((mine, tiles), (mates, mate_tiles))):
        for j in range(lay.cap):
            s, r, live, v = lay.lookup(meta, role, 2, 1, j)
            places.append(lay.place(r, me[0]))
            terms.append(matmul(jnp.where(live, source[s], 0.0), arrived[g * lay.cap + v]))
    total[...] = local[...]
    for place, term in zip(places, terms):
        total[place] += term
    half = keep.shape[0]
    keep[...] = total[:half]
    give[...] = total[half:]


def newton_kernel(inverse, sums, out):
    for i in range(out.shape[0]):
        x = inverse[i]
        xh, xl = split(x)
        product = matmul_parts(xh, xl, *split(sums[i]))
        out[i] = 2.0 * x + matmul_parts(*split(product), xh, xl)


def table_kernel(lay, me, metas, peers_below, peers_above, out):
    role = me[0] % 2
    for side in (1, 2):
        start = (side - 1) * lay.table
        base, peers = ((2, peers_below), (0, peers_above))[side - 1]
        for q in range(lay.n_tile):
            a, meta, peer = q ^ me[0], metas.at[q], peers.at[q]
            for j in range(lay.cap):
                s, _, live, v = lay.lookup(meta, role, base, side, j)
                k = start + a * lay.cap + j
                out[k] = s
                out[lay.listed_slots + k] = live.astype(jnp.int32)
                out[2 * lay.listed_slots + k] = lay.listed(peer, 2 - base + role, v) // lay.width
        for q in range(0, lay.n_tile, 2):
            meta, a = metas.at[q], (q ^ me[0]) >> 1
            begin = start + 3 * lay.listed_slots + a * (2 * lay.pairs)
            for i in range(2 * lay.pairs):
                out[begin + i] = 0

            def step(s, count, meta=meta, begin=begin, side=side):
                v = lay.link(meta, s)
                found = (lay.kind(meta, s) == side) & (v < lay.slots)

                @pl.when(found)
                def _():
                    out[begin + count] = s
                    out[begin + lay.pairs + count] = v // lay.width

                return count + found.astype(jnp.int32)

            out[start + 3 * lay.listed_slots + lay.n_tile * lay.pairs + a] = lax.fori_loop(0, lay.slots, step, 0)


def scaled_kernel(lay, side, pieces, me, table, inverse, *refs):
    sources, (listed, local) = refs[:-2], refs[-2:]
    groups, at = [], 0
    for count in pieces:
        groups.append(sources[at : at + count])
        at += count
    start = (side - 1) * lay.table

    def scaled(q, s, live):
        tile = jnp.concatenate([ref[s] for ref in groups[q]], 0)
        return widen(matmul(inverse[lay.place(s // lay.width, me[0])], jnp.where(live, tile, 0.0)))

    for q in range(lay.n_tile):
        for j in range(lay.cap):
            k = (q ^ me[0]) * lay.cap + j
            listed[k] = scaled(q, table[start + k], table[start + lay.listed_slots + k] != 0)
    for q in range(0, lay.n_tile, 2):
        a = (q ^ me[0]) >> 1
        begin = start + 3 * lay.listed_slots + a * (2 * lay.pairs)
        count = table[start + 3 * lay.listed_slots + lay.n_tile * lay.pairs + a]
        for i in range(lay.usual):
            local[a * lay.pairs + i] = scaled(q, table[begin + i], i < count)

        @pl.loop(lay.usual, count)
        def _(i, q=q, a=a, begin=begin):
            local[a * lay.pairs + i] = scaled(q, table[begin + i], True)


def first_kernel(lay, me, base, inverse, out):
    for r in range(lay.rows):
        out[r] = times_tile(base[r], widen(inverse[lay.place(r, me[0])]))


def local_sum_kernel(lay, side, table, x, tiles, out):
    start = (side - 1) * lay.table + 3 * lay.listed_slots
    groups = lay.n_tile // 2

    def term(a, i):
        return times_tile(x[table[start + a * (2 * lay.pairs) + lay.pairs + i]], tiles[a * lay.pairs + i])

    def row(a, i):
        return table[start + a * (2 * lay.pairs) + i] // lay.width

    usual = [(a, i) for a in range(groups) for i in range(lay.usual)]
    terms = [term(a, i) for a, i in usual]
    out[...] = jnp.zeros_like(out)
    for (a, i), value in zip(usual, terms):
        out[row(a, i)] += value
    for a in range(groups):

        @pl.loop(lay.usual, table[start + lay.n_tile * lay.pairs + a])
        def _(i, a=a):
            out[row(a, i)] += term(a, i)


def listed_sum_kernel(lay, side, table, local, tiles, arrived, out):
    start = (side - 1) * lay.table
    terms = [
        times_tile(arrived[table[start + 2 * lay.listed_slots + k]], tiles[k]) for k in range(lay.listed_slots)
    ]
    out[...] = local[...]
    for k, value in enumerate(terms):
        out[table[start + k] // lay.width] += value


def local(krylov_block, diag_block, inverse_prev, coupling_tiles, slot_kind, slot_link, send_slots):
    rows, width, n, _ = coupling_tiles.shape
    cap = send_slots.shape[3]
    n_dom, n_tile = lax.axis_size("dom"), lax.axis_size("tile")
    lay = Layout(rows, width, cap, n_tile)
    vectors = krylov_block.shape[1]
    upper_bits = [1 << b for b in range(1, n_tile.bit_length() - 1)]

    me = lax.axis_index("tile").astype(jnp.int32).reshape(1)
    mine = jnp.concatenate([slot_kind.reshape(-1), slot_link.reshape(-1), send_slots.reshape(-1)])
    tiles = coupling_tiles.reshape(lay.slots, n, n)

    def swap(x, bit):
        return lax.ppermute(x, "tile", [(i, i ^ bit) for i in range(n_tile)])

    def along(x, sign):
        route = []
        for d in range(n_dom):
            for t in range(n_tile):
                to = d + sign * (1 + t % 2)
                if 0 <= to < n_dom:
                    route.append((d * n_tile + t, to * n_tile + t))
        return lax.ppermute(x, ("dom", "tile"), route)

    def spread(x):
        for bit in upper_bits:
            x = jnp.concatenate([x, swap(x, bit)], 0)
        return x

    def summed(x):
        for bit in upper_bits:
            got = swap(x, bit)
            near = bit // 2
            got = got.reshape((n_tile // 2 // (2 * near), 2, near * lay.own_rows) + x.shape[1:])
            x = x + jnp.concatenate([got[:, 1:], got[:, :1]], 1).reshape(x.shape)
        return x

    def after(x, *others):
        return lax.optimization_barrier((x, others))[0]

    def shape(*dims, dtype=F32):
        return jax.ShapeDtypeStruct(dims, dtype)

    kernel = lambda body, *bound: functools.partial(body, lay, *bound)
    product = 8 * n**3

    mate_tiles = swap(tiles, 1)
    arriving = spread(inverse_prev)
    mates = swap(mine, 1)
    kept, mine, mates = lax.optimization_barrier((arriving, mine, mates))
    half = rows // 2
    cuts = [slice(i * n // FSWEEPS, (i + 1) * n // FSWEEPS) for i in range(FSWEEPS)]
    metas = jnp.stack([mine, mates])
    far_tiles, far_mate_tiles = [], []
    for sweep in range(FSWEEPS):
        inverse = jnp.concatenate([kept, swap(kept, 1)], 0)
        (out,) = call(
            kernel(outgoing_kernel), [shape(2 * cap, n, n)], (me, mine, mates), (inverse, tiles, mate_tiles)
        )
        arrived = along(out, 1)
        (here,) = call(
            kernel(local_pivot_kernel),
            [shape(rows, n, n)],
            (me, mine),
            (inverse, diag_block, tiles),
            flops=product * rows,
        )
        part = [tiles[:, cuts[sweep]]]
        for bit in upper_bits:
            part += [swap(x, bit) for x in part]
        far_tiles.append(part[1:])
        early = list(part[1:])
        if sweep == 0:
            for bit in upper_bits:
                metas = jnp.concatenate([metas, swap(metas, bit)], 0)
            early.append(metas)
        if sweep == FSWEEPS - 1:
            below, above = along(metas, 1), along(metas, -1)
            table = pl.pallas_call(
                kernel(table_kernel),
                out_shape=shape(2 * lay.table, dtype=jnp.int32),
                in_specs=[smem()] * 4,
                out_specs=smem(),
            )(me, metas, below, above)
            early.append(table)
        keep, give = call(
            kernel(incoming_kernel),
            [shape(half, n, n)] * 2,
            (me, mine, mates),
            (here, tiles, mate_tiles, arrived),
            scratch=(pltpu.VMEM((rows, n, n), F32),),
            early=early,
        )
        sums = summed(keep + swap(give, 1))
        far_mate_tiles.append([swap(x, 1) for x in part[1:]])
        (kept,) = call(newton_kernel, [shape(half, n, n)], (), (kept, sums), early=far_mate_tiles[-1])
    inverse = jnp.concatenate([kept, swap(kept, 1)], 0)

    groups = [[tiles], [mate_tiles]]
    for i in range(n_tile // 2 - 1):
        groups += [[part[i] for part in far_tiles], [part[i] for part in far_mate_tiles]]
    flat = [x for group in groups for x in group]

    def scale(side):
        return call(
            kernel(scaled_kernel, side, [len(group) for group in groups]),
            [
                shape(lay.listed_slots, 2 * n, n, dtype=BF16),
                shape(n_tile // 2 * lay.pairs, 2 * n, n, dtype=BF16),
            ],
            (me, table),
            (inverse, *flat),
            flops=product * 24,
        )

    block = shape(rows, vectors, n)
    (first,) = call(kernel(first_kernel), [block], (me,), (krylov_block, inverse))

    def sweeps(x, side, count, listed, local):
        base = x
        for _ in range(count):
            arrived = along(x, 1 if side == 1 else -1)
            (here,) = call(
                kernel(local_sum_kernel, side), [block], (table,), (x, local), flops=8 * n**2 * vectors * rows
            )
            (part,) = call(kernel(listed_sum_kernel, side), [block], (table,), (here, listed, arrived))
            x = base - (part + swap(part, 1))
        return x

    lower, upper = scale(1), scale(2)
    solved = sweeps(sweeps(first, 1, LSWEEPS, *lower), 2, USWEEPS, *upper)
    return (kept[: lay.own_rows], solved)


def solution(mesh):
    placed = (
        P("dom", None, None),
        P(("dom", "tile"), None, None),
        P(("dom", "tile"), None, None),
        P("dom", "tile", None, None),
        P("dom", "tile"),
        P("dom", "tile"),
        P("dom", "tile", None, None),
    )
    return jax.shard_map(
        local,
        mesh=mesh,
        in_specs=placed,
        out_specs=(P(("dom", "tile"), None, None), P("dom", None, None)),
        check_vma=False,
    )
```

```python
import functools

import jax
import jax.numpy as jnp
from jax import lax
from jax.experimental import pallas as pl
from jax.experimental.pallas import tpu as pltpu
from jax.sharding import PartitionSpec as P

FSWEEPS = 2
LSWEEPS = 3
USWEEPS = 3
F32 = jnp.float32
BF16 = jnp.bfloat16


def split(a):
    hi = a.astype(BF16)
    return hi, (a - hi.astype(F32)).astype(BF16)


def matmul_parts(ah, al, bh, bl):
    lhs = jnp.concatenate([ah, al], 1)
    pair = jnp.concatenate([bh, bl], 1)
    rhs = jnp.concatenate([pair, pair], 0)
    out = jnp.dot(lhs, rhs, preferred_element_type=F32)
    n = bh.shape[1]
    return out[:, :n] + out[:, n:]


def matmul(a, b):
    return matmul_parts(*split(a), *split(b))


def times_tile(x, wide):
    v, n = x.shape
    stacked = jnp.concatenate(split(x), 0)
    out = lax.dot_general(stacked, wide, (((1,), (1,)), ((), ())), preferred_element_type=F32)
    return out[:v, :n] + (out[v:, :n] + out[:v, n:])


def widen(a):
    return jnp.concatenate(split(a), 0)


class Layout:
    def __init__(self, rows, width, cap, n_tile):
        self.rows, self.width, self.cap, self.n_tile = rows, width, cap, n_tile
        self.slots = rows * width
        self.own_rows = rows // n_tile
        self.pairs = max(1, (self.slots - 4 * cap) // 2)
        self.listed_slots = n_tile * cap
        self.local_slots = n_tile // 2 * self.pairs
        self.table = 2 * (self.listed_slots + self.local_slots)

    def kind(self, meta, s):
        return meta[s]

    def link(self, meta, s):
        return meta[self.slots + s]

    def listed(self, meta, which, j):
        return meta[2 * self.slots + which * self.cap + j]

    def place(self, r, me):
        far = (r // self.own_rows) ^ me
        return ((far & 1) * (self.n_tile // 2) + (far >> 1)) * self.own_rows + r % self.own_rows

    def lookup(self, meta, which, side, j):
        s = self.listed(meta, which, j)
        v = self.link(meta, s) - self.slots - (which % 2) * self.cap
        live = (self.kind(meta, s) == side) & (v >= 0) & (v < self.cap)
        return s, live, jnp.clip(v, 0, self.cap - 1)

    def is_local(self, meta, s, side):
        return (self.kind(meta, s) == side) & (self.link(meta, s) < self.slots)

    def scan(self, meta, side, found):
        def step(s, count):
            hit = self.is_local(meta, s, side)

            @pl.when(hit & (count < self.pairs))
            def _():
                found(s, count)

            return count + hit.astype(jnp.int32)

        return lax.fori_loop(0, self.slots, step, 0)


def smem():
    return pl.BlockSpec(memory_space=pltpu.SMEM)


def vmem():
    return pl.BlockSpec(memory_space=pltpu.VMEM)


def call(body, outs, scalars, arrays, flops=0, scratch=(), early=()):
    moved = sum(a.size * a.dtype.itemsize for a in arrays) + sum(o.size * o.dtype.itemsize for o in outs)
    return pl.pallas_call(
        body if not early else lambda *refs: body(*refs[len(early) :]),
        out_shape=outs,
        in_specs=[pl.BlockSpec(memory_space=pl.ANY)] * len(early) + [smem()] * len(scalars) + [vmem()] * len(arrays),
        out_specs=[vmem()] * len(outs),
        scratch_shapes=list(scratch),
        compiler_params=pltpu.CompilerParams(vmem_limit_bytes=8 << 20),
        cost_estimate=pl.CostEstimate(flops=flops, bytes_accessed=moved, transcendentals=0),
    )(*early, *scalars, *arrays)


def gather_kernel(lay, mine, tiles, lower, lower_local, upper, places):
    for side, base, out in ((1, 2, lower), (2, 0, upper)):
        for which in range(2):
            for j in range(lay.cap):
                s, live, _ = lay.lookup(mine, base + which, side, j)
                out[which * lay.cap + j] = jnp.where(live, tiles[s], 0.0)
    for side, out, start in ((1, lower_local, 0), (2, upper, 2 * lay.cap)):
        for i in range(lay.pairs):
            places[i] = 0

        def found(s, i):
            places[i] = s

        count = lay.scan(mine, side, found)
        for i in range(lay.pairs):
            out[start + i] = jnp.where(i < count, tiles[places[i]], 0.0)


def outgoing_kernel(lay, me, mine, mates, inverse, upper, mate_upper, out):
    role = me[0] % 2
    for g, (meta, source) in enumerate(((mine, upper), (mates, mate_upper))):
        for j in range(lay.cap):
            r = lay.listed(meta, role, j) // lay.width
            out[g * lay.cap + j] = matmul(inverse[lay.place(r, me[0])], source[role * lay.cap + j])


def local_pivot_kernel(lay, me, mine, inverse, diag, tiles, out):
    out[: lay.own_rows] = -diag[...]
    out[lay.own_rows :] = jnp.zeros((lay.rows - lay.own_rows,) + diag.shape[1:], F32)

    @pl.loop(0, lay.slots)
    def _(s):
        @pl.when(lay.is_local(mine, s, 1))
        def _():
            v = lay.link(mine, s)
            q = matmul(inverse[lay.place(v // lay.width, me[0])], tiles[v])
            out[lay.place(s // lay.width, me[0])] += matmul(tiles[s], q)


def incoming_kernel(lay, me, mine, mates, local, lower, mate_lower, arrived, keep, give, total):
    role = me[0] % 2
    places, terms = [], []
    for g, (meta, source) in enumerate(((mine, lower), (mates, mate_lower))):
        for j in range(lay.cap):
            s, _, v = lay.lookup(meta, 2 + role, 1, j)
            places.append(lay.place(s // lay.width, me[0]))
            terms.append(matmul(source[role * lay.cap + j], arrived[g * lay.cap + v]))
    total[...] = local[...]
    for place, term in zip(places, terms):
        total[place] += term
    half = keep.shape[0]
    keep[...] = total[:half]
    give[...] = total[half:]


def newton_kernel(inverse, sums, out):
    for i in range(out.shape[0]):
        x = inverse[i]
        xh, xl = split(x)
        product = matmul_parts(xh, xl, *split(sums[i]))
        out[i] = 2.0 * x + matmul_parts(*split(product), xh, xl)


def table_kernel(lay, me, metas, peers_below, peers_above, out):
    role = me[0] % 2
    for side in (1, 2):
        start = (side - 1) * lay.table
        base, peers = ((2, peers_below), (0, peers_above))[side - 1]
        for q in range(lay.n_tile):
            a, meta, peer = q ^ me[0], metas.at[q], peers.at[q]
            for j in range(lay.cap):
                s, _, v = lay.lookup(meta, base + role, side, j)
                k = start + a * lay.cap + j
                out[k] = s // lay.width
                out[lay.listed_slots + k] = lay.listed(peer, 2 - base + role, v) // lay.width
        for q in range(0, lay.n_tile, 2):
            meta = metas.at[q]
            begin = start + 2 * lay.listed_slots + ((q ^ me[0]) >> 1) * lay.pairs
            for i in range(lay.pairs):
                out[begin + i] = 0
                out[begin + lay.local_slots + i] = 0

            def found(s, i, meta=meta, begin=begin):
                out[begin + i] = s // lay.width
                out[begin + lay.local_slots + i] = lay.link(meta, s) // lay.width

            lay.scan(meta, side, found)


def scaled_kernel(lay, side, me, table, inverse, *refs):
    sources, (listed, local) = refs[:-2], refs[-2:]
    role = me[0] % 2
    start = (side - 1) * lay.table

    def scaled(row, tile):
        return widen(matmul(inverse[lay.place(row, me[0])], tile))

    at = 0
    for q in range(lay.n_tile):
        lists = sources[at]
        for j in range(lay.cap):
            k = (q ^ me[0]) * lay.cap + j
            listed[k] = scaled(table[start + k], lists[role * lay.cap + j])
        at += 1
        if q % 2 == 0:
            pairs, first = (lists, 2 * lay.cap) if side == 2 else (sources[at], 0)
            at += side == 1
            for i in range(lay.pairs):
                k = ((q ^ me[0]) >> 1) * lay.pairs + i
                local[k] = scaled(table[start + 2 * lay.listed_slots + k], pairs[first + i])


def first_kernel(lay, me, base, inverse, out):
    count = out.shape[1]
    mine = pl.ds(pl.multiple_of((me[0] >> 1) * count, count), count)
    for r in range(lay.rows):
        out[r] = times_tile(base[r, mine], widen(inverse[lay.place(r, me[0])]))


def local_sum_kernel(lay, side, table, x, tiles, out):
    start = (side - 1) * lay.table + 2 * lay.listed_slots
    terms = [times_tile(x[table[start + lay.local_slots + k]], tiles[k]) for k in range(lay.local_slots)]
    out[...] = jnp.zeros_like(out)
    for k, value in enumerate(terms):
        out[table[start + k]] += value


def listed_sum_kernel(lay, side, table, local, tiles, arrived, out):
    start = (side - 1) * lay.table
    terms = [times_tile(arrived[table[start + lay.listed_slots + k]], tiles[k]) for k in range(lay.listed_slots)]
    out[...] = local[...]
    for k, value in enumerate(terms):
        out[table[start + k]] += value


def local(krylov_block, diag_block, inverse_prev, coupling_tiles, slot_kind, slot_link, send_slots):
    rows, width, n, _ = coupling_tiles.shape
    cap = send_slots.shape[3]
    n_dom, n_tile = lax.axis_size("dom"), lax.axis_size("tile")
    lay = Layout(rows, width, cap, n_tile)
    vectors = krylov_block.shape[1]
    upper_bits = [1 << b for b in range(1, n_tile.bit_length() - 1)]

    me = lax.axis_index("tile").astype(jnp.int32).reshape(1)
    mine = jnp.concatenate([slot_kind.reshape(-1), slot_link.reshape(-1), send_slots.reshape(-1)])
    tiles = coupling_tiles.reshape(lay.slots, n, n)

    def swap(x, bit):
        return lax.ppermute(x, "tile", [(i, i ^ bit) for i in range(n_tile)])

    def along(x, sign):
        route = []
        for d in range(n_dom):
            for t in range(n_tile):
                to = d + sign * (1 + t % 2)
                if 0 <= to < n_dom:
                    route.append((d * n_tile + t, to * n_tile + t))
        return lax.ppermute(x, ("dom", "tile"), route)

    def summed(x):
        for bit in upper_bits:
            got = swap(x, bit)
            near = bit // 2
            got = got.reshape((n_tile // 2 // (2 * near), 2, near * lay.own_rows) + x.shape[1:])
            x = x + jnp.concatenate([got[:, 1:], got[:, :1]], 1).reshape(x.shape)
        return x

    def shape(*dims, dtype=F32):
        return jax.ShapeDtypeStruct(dims, dtype)

    kernel = lambda body, *bound: functools.partial(body, lay, *bound)
    product = 8 * n**3

    def over_chips(x):
        held = [x]
        for bit in upper_bits:
            held += [swap(one, bit) for one in held]
        return held

    arriving = over_chips(inverse_prev)
    held = over_chips(mine)
    both = [swap(x, 1) for x in held]
    lower, lower_local, upper = call(
        kernel(gather_kernel),
        [shape(2 * cap, n, n), shape(lay.pairs, n, n), shape(2 * cap + lay.pairs, n, n)],
        (mine,),
        (tiles,),
        scratch=(pltpu.SMEM((lay.pairs,), jnp.int32),),
    )
    mate_lower, mate_upper = swap(lower, 1), swap(upper, 1)
    arriving, held, both, lower, lower_local, upper = lax.optimization_barrier(
        (arriving, held, both, lower, lower_local, upper)
    )
    mates = both[0]
    metas = jnp.stack([one for pair in zip(held, both) for one in pair])
    kept = jnp.concatenate(arriving, 0)
    mated = jnp.concatenate([swap(x, 1) for x in arriving], 0)
    half = rows // 2
    for sweep in range(FSWEEPS):
        inverse = jnp.concatenate([kept, mated], 0)
        (out,) = call(
            kernel(outgoing_kernel), [shape(2 * cap, n, n)], (me, mine, mates), (inverse, upper, mate_upper)
        )
        arrived = along(out, 1)
        (here,) = call(
            kernel(local_pivot_kernel),
            [shape(rows, n, n)],
            (me, mine),
            (inverse, diag_block, tiles),
            flops=product * rows,
        )
        early = []
        if sweep == 0:
            lowers = over_chips(lower)
            below, above = along(metas, 1), along(metas, -1)
            early += [*lowers[1:], below, above]
        if sweep == FSWEEPS - 1:
            lower_locals = over_chips(lower_local)
            mate_lowers = [mate_lower] + [swap(x, 1) for x in lowers[1:]]
            table = pl.pallas_call(
                kernel(table_kernel),
                out_shape=shape(2 * lay.table, dtype=jnp.int32),
                in_specs=[smem()] * 4,
                out_specs=smem(),
            )(me, metas, below, above)
            early += [*lower_locals[1:], *mate_lowers[1:], table]
        keep, give = call(
            kernel(incoming_kernel),
            [shape(half, n, n)] * 2,
            (me, mine, mates),
            (here, lower, mate_lower, arrived),
            scratch=(pltpu.VMEM((rows, n, n), F32),),
            early=early,
        )
        sums = summed(keep + swap(give, 1))
        (kept,) = call(newton_kernel, [shape(half, n, n)], (), (kept, sums))
        mated = swap(kept, 1)
    inverse = jnp.concatenate([kept, mated], 0)

    def scale(side, sources):
        return call(
            kernel(scaled_kernel, side),
            [
                shape(lay.listed_slots, 2 * n, n, dtype=BF16),
                shape(lay.local_slots, 2 * n, n, dtype=BF16),
            ],
            (me, table),
            (inverse, *sources),
            flops=product * 24,
        )

    share = vectors // (n_tile // 2)
    block = shape(rows, share, n)
    (first,) = call(kernel(first_kernel), [block], (me,), (krylov_block, inverse))

    def sweeps(x, side, count, listed, local, early=()):
        base = x
        for sweep in range(count):
            arrived = along(x, 1 if side == 1 else -1)
            (here,) = call(
                kernel(local_sum_kernel, side), [block], (table,), (x, local), flops=8 * n**2 * vectors * rows
            )
            (part,) = call(
                kernel(listed_sum_kernel, side),
                [block],
                (table,),
                (here, listed, arrived),
                early=early if sweep == count - 1 else (),
            )
            x = base - (part + swap(part, 1))
        return x

    uppers = over_chips(upper)
    mate_uppers = [mate_upper] + [swap(x, 1) for x in uppers[1:]]
    low = [x for three in zip(lowers, lower_locals, mate_lowers) for x in three]
    up = [x for pair in zip(uppers, mate_uppers) for x in pair]
    solved = sweeps(first, 1, LSWEEPS, *scale(1, low), early=uppers[1:])
    solved = sweeps(solved, 2, USWEEPS, *scale(2, up))
    for bit in upper_bits:
        got = swap(solved, bit)
        solved = jnp.where(
            (me[0] & bit) == 0, jnp.concatenate([solved, got], 1), jnp.concatenate([got, solved], 1)
        )
    return (kept[: lay.own_rows], solved)


def solution(mesh):
    placed = (
        P("dom", None, None),
        P(("dom", "tile"), None, None),
        P(("dom", "tile"), None, None),
        P("dom", "tile", None, None),
        P("dom", "tile"),
        P("dom", "tile"),
        P("dom", "tile", None, None),
    )
    return jax.shard_map(
        local,
        mesh=mesh,
        in_specs=placed,
        out_specs=(P(("dom", "tile"), None, None), P("dom", None, None)),
        check_vma=False,
    )
```

```python
import functools

import jax
import jax.numpy as jnp
from jax import lax
from jax.experimental import pallas as pl
from jax.experimental.pallas import tpu as pltpu
from jax.sharding import PartitionSpec as P

FSWEEPS = 2
LSWEEPS = 3
USWEEPS = 3
F32 = jnp.float32
BF16 = jnp.bfloat16


def split(a):
    hi = a.astype(BF16)
    return hi, (a - hi.astype(F32)).astype(BF16)


def matmul_parts(ah, al, bh, bl):
    lhs = jnp.concatenate([ah, al], 1)
    pair = jnp.concatenate([bh, bl], 1)
    rhs = jnp.concatenate([pair, pair], 0)
    out = jnp.dot(lhs, rhs, preferred_element_type=F32)
    n = bh.shape[1]
    return out[:, :n] + out[:, n:]


def matmul(a, b):
    return matmul_parts(*split(a), *split(b))


def times_tile(x, wide):
    v, n = x.shape
    stacked = jnp.concatenate(split(x), 0)
    out = lax.dot_general(stacked, wide, (((1,), (1,)), ((), ())), preferred_element_type=F32)
    return out[:v, :n] + (out[v:, :n] + out[:v, n:])


def widen(a):
    return jnp.concatenate(split(a), 0)


class Layout:
    def __init__(self, rows, width, cap, n_tile):
        self.rows, self.width, self.cap, self.n_tile = rows, width, cap, n_tile
        self.slots = rows * width
        self.own_rows = rows // n_tile
        self.pairs = max(1, (self.slots - 4 * cap) // 2)
        self.listed_slots = n_tile * cap
        self.local_slots = n_tile // 2 * self.pairs
        self.table = 2 * (self.listed_slots + self.local_slots)

    def kind(self, meta, s):
        return meta[s]

    def link(self, meta, s):
        return meta[self.slots + s]

    def listed(self, meta, which, j):
        return meta[2 * self.slots + which * self.cap + j]

    def place(self, r, me):
        far = (r // self.own_rows) ^ me
        return ((far & 1) * (self.n_tile // 2) + (far >> 1)) * self.own_rows + r % self.own_rows

    def lookup(self, meta, which, side, j):
        s = self.listed(meta, which, j)
        v = self.link(meta, s) - self.slots - (which % 2) * self.cap
        live = (self.kind(meta, s) == side) & (v >= 0) & (v < self.cap)
        return s, live, jnp.clip(v, 0, self.cap - 1)

    def is_local(self, meta, s, side):
        return (self.kind(meta, s) == side) & (self.link(meta, s) < self.slots)

    def scan(self, meta, side, places):
        count = jnp.int32(0)
        for s in range(self.slots):
            places[count] = s
            count = count + self.is_local(meta, s, side).astype(jnp.int32)
        return count


def smem():
    return pl.BlockSpec(memory_space=pltpu.SMEM)


def vmem():
    return pl.BlockSpec(memory_space=pltpu.VMEM)


def call(body, outs, scalars, arrays, flops=0, scratch=(), early=(), to_smem=False):
    moved = sum(a.size * a.dtype.itemsize for a in arrays) + sum(o.size * o.dtype.itemsize for o in outs)
    return pl.pallas_call(
        body if not early else lambda *refs: body(*refs[len(early) :]),
        out_shape=outs,
        in_specs=[pl.BlockSpec(memory_space=pl.ANY)] * len(early) + [smem()] * len(scalars) + [vmem()] * len(arrays),
        out_specs=[smem() if to_smem else vmem()] * len(outs),
        scratch_shapes=list(scratch),
        compiler_params=pltpu.CompilerParams(vmem_limit_bytes=8 << 20),
        cost_estimate=pl.CostEstimate(flops=flops, bytes_accessed=moved, transcendentals=0),
    )(*early, *scalars, *arrays)


def listed_tiles(lay, meta, side, tiles, out):
    for which in range(2):
        for j in range(lay.cap):
            s, live, _ = lay.lookup(meta, 4 - 2 * side + which, side, j)
            out[which * lay.cap + j] = jnp.where(live, tiles[s], 0.0)


def outgoing_kernel(lay, me, mine, mates, inverse, tiles, mate_tiles, out, lower):
    role = me[0] % 2
    for g, (meta, source) in enumerate(((mine, tiles), (mates, mate_tiles))):
        for j in range(lay.cap):
            s, live, _ = lay.lookup(meta, role, 2, j)
            tile = jnp.where(live, source[s], 0.0)
            out[g * lay.cap + j] = matmul(inverse[lay.place(s // lay.width, me[0])], tile)
    listed_tiles(lay, mine, 1, tiles, lower)


def next_outgoing_kernel(lay, me, mine, mates, inverse, upper, mate_upper, out):
    role = me[0] % 2
    for g, (meta, source) in enumerate(((mine, upper), (mates, mate_upper))):
        for j in range(lay.cap):
            r = lay.listed(meta, role, j) // lay.width
            out[g * lay.cap + j] = matmul(inverse[lay.place(r, me[0])], source[role * lay.cap + j])


def local_terms(lay, me, mine, inverse, diag, tiles, out):
    out[: lay.own_rows] = -diag[...]
    out[lay.own_rows :] = jnp.zeros((lay.rows - lay.own_rows,) + diag.shape[1:], F32)

    @pl.loop(0, lay.slots)
    def _(s):
        @pl.when(lay.is_local(mine, s, 1))
        def _():
            v = lay.link(mine, s)
            q = matmul(inverse[lay.place(v // lay.width, me[0])], tiles[v])
            out[lay.place(s // lay.width, me[0])] += matmul(tiles[s], q)


def local_pivot_kernel(
    lay, me, mine, mates, inverse, diag, tiles, mate_tiles, out, mate_lower, lower_local, upper, mate_upper, places
):
    local_terms(lay, me, mine, inverse, diag, tiles, out)
    listed_tiles(lay, mates, 1, mate_tiles, mate_lower)
    listed_tiles(lay, mates, 2, mate_tiles, mate_upper)
    listed_tiles(lay, mine, 2, tiles, upper)
    for side, target, start in ((1, lower_local, 0), (2, upper, 2 * lay.cap)):
        count = lay.scan(mine, side, places)
        for i in range(lay.pairs):
            live = i < count
            target[start + i] = jnp.where(live, tiles[jnp.where(live, places[i], 0)], 0.0)


def next_local_pivot_kernel(lay, me, mine, inverse, diag, tiles, out):
    local_terms(lay, me, mine, inverse, diag, tiles, out)


def incoming_kernel(lay, me, mine, mates, local, lower, mate_lower, arrived, keep, give, total):
    role = me[0] % 2
    places, terms = [], []
    for g, (meta, source) in enumerate(((mine, lower), (mates, mate_lower))):
        for j in range(lay.cap):
            s, _, v = lay.lookup(meta, 2 + role, 1, j)
            places.append(lay.place(s // lay.width, me[0]))
            terms.append(matmul(source[role * lay.cap + j], arrived[g * lay.cap + v]))
    total[...] = local[...]
    for place, term in zip(places, terms):
        total[place] += term
    half = keep.shape[0]
    keep[...] = total[:half]
    give[...] = total[half:]


def newton_kernel(inverse, sums, out):
    for i in range(out.shape[0]):
        x = inverse[i]
        xh, xl = split(x)
        product = matmul_parts(xh, xl, *split(sums[i]))
        out[i] = 2.0 * x + matmul_parts(*split(product), xh, xl)


def table_kernel(lay, me, metas, peers_below, peers_above, out, places):
    role = me[0] % 2
    for side in (1, 2):
        start = (side - 1) * lay.table
        base, peers = ((2, peers_below), (0, peers_above))[side - 1]
        for q in range(lay.n_tile):
            a, meta, peer = q ^ me[0], metas.at[q], peers.at[q]
            for j in range(lay.cap):
                s, _, v = lay.lookup(meta, base + role, side, j)
                k = start + a * lay.cap + j
                out[k] = s // lay.width
                out[lay.listed_slots + k] = lay.listed(peer, 2 - base + role, v) // lay.width
        for q in range(0, lay.n_tile, 2):
            meta = metas.at[q]
            begin = start + 2 * lay.listed_slots + ((q ^ me[0]) >> 1) * lay.pairs
            count = lay.scan(meta, side, places)
            for i in range(lay.pairs):
                s = jnp.where(i < count, places[i], 0)
                out[begin + i] = s // lay.width
                v = jnp.where(i < count, lay.link(meta, s), 0)
                out[begin + lay.local_slots + i] = v // lay.width


def scaled_kernel(lay, side, me, table, inverse, *refs):
    sources, (listed, local) = refs[:-2], refs[-2:]
    role = me[0] % 2
    start = (side - 1) * lay.table

    def scaled(row, tile):
        return widen(matmul(inverse[lay.place(row, me[0])], tile))

    at = 0
    for q in range(lay.n_tile):
        lists = sources[at]
        for j in range(lay.cap):
            k = (q ^ me[0]) * lay.cap + j
            listed[k] = scaled(table[start + k], lists[role * lay.cap + j])
        at += 1
        if q % 2 == 0:
            pairs, first = (lists, 2 * lay.cap) if side == 2 else (sources[at], 0)
            at += side == 1
            for i in range(lay.pairs):
                k = ((q ^ me[0]) >> 1) * lay.pairs + i
                local[k] = scaled(table[start + 2 * lay.listed_slots + k], pairs[first + i])


def first_kernel(lay, me, base, inverse, out):
    count = out.shape[1]
    mine = pl.ds(pl.multiple_of((me[0] >> 1) * count, count), count)
    for r in range(lay.rows):
        out[r] = times_tile(base[r, mine], widen(inverse[lay.place(r, me[0])]))


def local_sum_kernel(lay, side, table, x, tiles, out):
    start = (side - 1) * lay.table + 2 * lay.listed_slots
    terms = [times_tile(x[table[start + lay.local_slots + k]], tiles[k]) for k in range(lay.local_slots)]
    out[...] = jnp.zeros_like(out)
    for k, value in enumerate(terms):
        out[table[start + k]] += value


def listed_sum_kernel(lay, side, table, local, tiles, arrived, out):
    start = (side - 1) * lay.table
    terms = [times_tile(arrived[table[start + lay.listed_slots + k]], tiles[k]) for k in range(lay.listed_slots)]
    out[...] = local[...]
    for k, value in enumerate(terms):
        out[table[start + k]] += value


def local(krylov_block, diag_block, inverse_prev, coupling_tiles, slot_kind, slot_link, send_slots):
    rows, width, n, _ = coupling_tiles.shape
    cap = send_slots.shape[3]
    n_dom, n_tile = lax.axis_size("dom"), lax.axis_size("tile")
    lay = Layout(rows, width, cap, n_tile)
    vectors = krylov_block.shape[1]
    upper_bits = [1 << b for b in range(1, n_tile.bit_length() - 1)]

    me = lax.axis_index("tile").astype(jnp.int32).reshape(1)
    mine = jnp.concatenate([slot_kind.reshape(-1), slot_link.reshape(-1), send_slots.reshape(-1)])
    tiles = coupling_tiles.reshape(lay.slots, n, n)

    def swap(x, bit):
        return lax.ppermute(x, "tile", [(i, i ^ bit) for i in range(n_tile)])

    def along(x, sign):
        route = []
        for d in range(n_dom):
            for t in range(n_tile):
                to = d + sign * (1 + t % 2)
                if 0 <= to < n_dom:
                    route.append((d * n_tile + t, to * n_tile + t))
        return lax.ppermute(x, ("dom", "tile"), route)

    def summed(x):
        for bit in upper_bits:
            got = swap(x, bit)
            near = bit // 2
            got = got.reshape((n_tile // 2 // (2 * near), 2, near * lay.own_rows) + x.shape[1:])
            x = x + jnp.concatenate([got[:, 1:], got[:, :1]], 1).reshape(x.shape)
        return x

    def shape(*dims, dtype=F32):
        return jax.ShapeDtypeStruct(dims, dtype)

    kernel = lambda body, *bound: functools.partial(body, lay, *bound)
    product = 8 * n**3

    def over_chips(x):
        held = [x]
        for bit in upper_bits:
            held += [swap(one, bit) for one in held]
        return held

    mate_tiles = swap(tiles, 1)
    arriving = over_chips(inverse_prev)
    held = over_chips(mine)
    both = [swap(x, 1) for x in held]
    arriving, held, both = lax.optimization_barrier((arriving, held, both))
    mates = both[0]
    metas = jnp.stack([one for pair in zip(held, both) for one in pair])
    kept = jnp.concatenate(arriving, 0)
    mated = jnp.concatenate([swap(x, 1) for x in arriving], 0)
    half = rows // 2
    lists, local_list = shape(2 * cap, n, n), shape(lay.pairs, n, n)
    places = pltpu.SMEM((lay.slots + 1,), jnp.int32)
    for sweep in range(FSWEEPS):
        inverse = jnp.concatenate([kept, mated], 0)
        early, later = [], []
        if sweep == 0:
            out, lower = call(
                kernel(outgoing_kernel), [lists] * 2, (me, mine, mates), (inverse, tiles, mate_tiles)
            )
            arrived = along(out, 1)
            lowers = over_chips(lower)
            here, mate_lower, lower_local, upper, mate_upper = call(
                kernel(local_pivot_kernel),
                [shape(rows, n, n), lists, local_list, shape(2 * cap + lay.pairs, n, n), lists],
                (me, mine, mates),
                (inverse, diag_block, tiles, mate_tiles),
                flops=product * rows,
                scratch=(places,),
            )
            early += lowers[1:]
        else:
            (out,) = call(
                kernel(next_outgoing_kernel), [lists], (me, mine, mates), (inverse, upper, mate_upper)
            )
            arrived = along(out, 1)
            (here,) = call(
                kernel(next_local_pivot_kernel),
                [shape(rows, n, n)],
                (me, mine),
                (inverse, diag_block, tiles),
                flops=product * rows,
            )
        if sweep == FSWEEPS - 1:
            lower_locals = over_chips(lower_local)
            mate_lowers = [mate_lower] + [swap(x, 1) for x in lowers[1:]]
            below, above = along(metas, 1), along(metas, -1)
            (table,) = call(
                kernel(table_kernel),
                [shape(2 * lay.table, dtype=jnp.int32)],
                (me, metas, below, above),
                (),
                scratch=(places,),
                to_smem=True,
            )
            early += [*lower_locals[1:], *mate_lowers[1:], below, above]
            later += [table]
        keep, give = call(
            kernel(incoming_kernel),
            [shape(half, n, n)] * 2,
            (me, mine, mates),
            (here, lower, mate_lower, arrived),
            scratch=(pltpu.VMEM((rows, n, n), F32),),
            early=early,
        )
        sums = summed(keep + swap(give, 1))
        (kept,) = call(newton_kernel, [shape(half, n, n)], (), (kept, sums), early=later)
        mated = swap(kept, 1)
    inverse = jnp.concatenate([kept, mated], 0)

    def scale(side, sources):
        return call(
            kernel(scaled_kernel, side),
            [
                shape(lay.listed_slots, 2 * n, n, dtype=BF16),
                shape(lay.local_slots, 2 * n, n, dtype=BF16),
            ],
            (me, table),
            (inverse, *sources),
            flops=product * 24,
        )

    share = vectors // (n_tile // 2)
    block = shape(rows, share, n)
    (first,) = call(kernel(first_kernel), [block], (me,), (krylov_block, inverse))

    def sweeps(x, side, count, listed, local, early=()):
        base = x
        for sweep in range(count):
            arrived = along(x, 1 if side == 1 else -1)
            (here,) = call(
                kernel(local_sum_kernel, side), [block], (table,), (x, local), flops=8 * n**2 * vectors * rows
            )
            (part,) = call(
                kernel(listed_sum_kernel, side),
                [block],
                (table,),
                (here, listed, arrived),
                early=early if sweep == count - 1 else (),
            )
            x = base - (part + swap(part, 1))
        return x

    uppers = over_chips(upper)
    mate_uppers = [mate_upper] + [swap(x, 1) for x in uppers[1:]]
    low = [x for three in zip(lowers, lower_locals, mate_lowers) for x in three]
    up = [x for pair in zip(uppers, mate_uppers) for x in pair]
    solved = sweeps(first, 1, LSWEEPS, *scale(1, low), early=uppers[1:])
    solved = sweeps(solved, 2, USWEEPS, *scale(2, up))
    for bit in upper_bits:
        got = swap(solved, bit)
        solved = jnp.where(
            (me[0] & bit) == 0, jnp.concatenate([solved, got], 1), jnp.concatenate([got, solved], 1)
        )
    return (kept[: lay.own_rows], solved)


def solution(mesh):
    placed = (
        P("dom", None, None),
        P(("dom", "tile"), None, None),
        P(("dom", "tile"), None, None),
        P("dom", "tile", None, None),
        P("dom", "tile"),
        P("dom", "tile"),
        P("dom", "tile", None, None),
    )
    return jax.shard_map(
        local,
        mesh=mesh,
        in_specs=placed,
        out_specs=(P(("dom", "tile"), None, None), P("dom", None, None)),
        check_vma=False,
    )
```

```python
import functools

import jax
import jax.numpy as jnp
from jax import lax
from jax.experimental import pallas as pl
from jax.experimental.pallas import tpu as pltpu
from jax.sharding import PartitionSpec as P

FSWEEPS = 2
LSWEEPS = 3
USWEEPS = 3
PARTS = 2
F32 = jnp.float32
BF16 = jnp.bfloat16


def split(a):
    hi = a.astype(BF16)
    return hi, (a - hi.astype(F32)).astype(BF16)


def matmul_parts(ah, al, bh, bl):
    lhs = jnp.concatenate([ah, al], 1)
    pair = jnp.concatenate([bh, bl], 1)
    rhs = jnp.concatenate([pair, pair], 0)
    out = jnp.dot(lhs, rhs, preferred_element_type=F32)
    n = bh.shape[1]
    return out[:, :n] + out[:, n:]


def matmul(a, b):
    return matmul_parts(*split(a), *split(b))


def matmul_nt_parts(ah, al, bh, bl):
    lhs = jnp.concatenate([ah, al], 1)
    rhs = jnp.concatenate([jnp.concatenate([bh, bh], 1), jnp.concatenate([bl, bl], 1)], 0)
    out = lax.dot_general(lhs, rhs, (((1,), (1,)), ((), ())), preferred_element_type=F32)
    n = bh.shape[0]
    return out[:, :n] + out[:, n:]


def matmul_nt(a, b):
    return matmul_nt_parts(*split(a), *split(b))


def times_tile(x, wide):
    v, n = x.shape
    stacked = jnp.concatenate(split(x), 0)
    out = lax.dot_general(stacked, wide, (((1,), (1,)), ((), ())), preferred_element_type=F32)
    return out[:v, :n] + (out[v:, :n] + out[:v, n:])


def widen(a):
    return jnp.concatenate(split(a), 0)


class Layout:
    def __init__(self, rows, width, cap, n_tile):
        self.rows, self.width, self.cap, self.n_tile = rows, width, cap, n_tile
        self.slots = rows * width
        self.own_rows = rows // n_tile
        self.pairs = max(1, (self.slots - 4 * cap) // 2)
        self.listed_slots = n_tile * cap
        self.local_slots = n_tile // 2 * self.pairs
        self.table = self.listed_slots + 2 * self.local_slots

    def kind(self, meta, s):
        return meta[s]

    def link(self, meta, s):
        return meta[self.slots + s]

    def listed(self, meta, which, j):
        return meta[2 * self.slots + which * self.cap + j]

    def place(self, r, me):
        far = (r // self.own_rows) ^ me
        return ((far & 1) * (self.n_tile // 2) + (far >> 1)) * self.own_rows + r % self.own_rows

    def lookup(self, meta, which, side, j):
        s = self.listed(meta, which, j)
        v = self.link(meta, s) - self.slots - (which % 2) * self.cap
        live = (self.kind(meta, s) == side) & (v >= 0) & (v < self.cap)
        return s, live, jnp.clip(v, 0, self.cap - 1)

    def is_local(self, meta, s, side):
        return (self.kind(meta, s) == side) & (self.link(meta, s) < self.slots)

    def scan(self, meta, side, places):
        count = jnp.int32(0)
        for s in range(self.slots):
            places[count] = s
            count = count + self.is_local(meta, s, side).astype(jnp.int32)
        return count


def smem():
    return pl.BlockSpec(memory_space=pltpu.SMEM)


def vmem():
    return pl.BlockSpec(memory_space=pltpu.VMEM)


def call(body, outs, scalars, arrays, flops=0, scratch=(), early=(), to_smem=0):
    moved = sum(a.size * a.dtype.itemsize for a in arrays) + sum(o.size * o.dtype.itemsize for o in outs)
    return pl.pallas_call(
        body if not early else lambda *refs: body(*refs[len(early) :]),
        out_shape=outs,
        in_specs=[pl.BlockSpec(memory_space=pl.ANY)] * len(early) + [smem()] * len(scalars) + [vmem()] * len(arrays),
        out_specs=[smem()] * to_smem + [vmem()] * (len(outs) - to_smem),
        scratch_shapes=list(scratch),
        compiler_params=pltpu.CompilerParams(vmem_limit_bytes=8 << 20),
        cost_estimate=pl.CostEstimate(flops=flops, bytes_accessed=moved, transcendentals=0),
    )(*early, *scalars, *arrays)


def listed_tiles(lay, meta, side, tiles, out):
    for which in range(2):
        for j in range(lay.cap):
            s, live, _ = lay.lookup(meta, 4 - 2 * side + which, side, j)
            tile = jnp.where(live, tiles[s], 0.0)
            out[which * lay.cap + j] = tile if side == 1 else tile.T


def outgoing_kernel(lay, near, inverse, tiles, mate_tiles, *refs):
    outs, lower = refs[:-1], refs[-1]
    me, mine, mates = near.at[0], near.at[1], near.at[2]
    role = me[0] % 2
    for g, (meta, source) in enumerate(((mine, tiles), (mates, mate_tiles))):
        for j in range(lay.cap):
            s, live, _ = lay.lookup(meta, role, 2, j)
            tile = jnp.where(live, source[s], 0.0)
            product = matmul(inverse[lay.place(s // lay.width, me[0])], tile).T
            for h, out in enumerate(outs):
                out[g * lay.cap + j] = product[h * out.shape[1] : (h + 1) * out.shape[1]]
    listed_tiles(lay, mine, 1, tiles, lower)


def next_outgoing_kernel(lay, near, inverse, upper, mate_upper, *outs):
    me, mine, mates = near.at[0], near.at[1], near.at[2]
    role = me[0] % 2
    for g, (meta, source) in enumerate(((mine, upper), (mates, mate_upper))):
        for j in range(lay.cap):
            r = lay.listed(meta, role, j) // lay.width
            product = matmul_nt(source[role * lay.cap + j], inverse[lay.place(r, me[0])])
            for h, out in enumerate(outs):
                out[g * lay.cap + j] = product[h * out.shape[1] : (h + 1) * out.shape[1]]


def local_terms(lay, me, mine, inverse, diag, tiles, outs, total):
    total[: lay.own_rows] = -diag[...]
    total[lay.own_rows :] = jnp.zeros((lay.rows - lay.own_rows,) + diag.shape[1:], F32)

    @pl.loop(0, lay.slots)
    def _(s):
        @pl.when(lay.is_local(mine, s, 1))
        def _():
            v = lay.link(mine, s)
            q = matmul(inverse[lay.place(v // lay.width, me[0])], tiles[v])
            total[lay.place(s // lay.width, me[0])] += matmul(tiles[s], q)

    for r in range(lay.rows):
        turned = total[r].T
        for h, out in enumerate(outs):
            out[r] = turned[h * out.shape[1] : (h + 1) * out.shape[1]]


def local_pivot_kernel(lay, parts, near, inverse, diag, tiles, mate_tiles, *refs):
    outs, (mate_lower, lower_local, upper, mate_upper, total, places) = refs[:parts], refs[parts:]
    me, mine, mates = near.at[0], near.at[1], near.at[2]
    local_terms(lay, me, mine, inverse, diag, tiles, outs, total)
    listed_tiles(lay, mates, 1, mate_tiles, mate_lower)
    listed_tiles(lay, mates, 2, mate_tiles, mate_upper)
    listed_tiles(lay, mine, 2, tiles, upper)
    for side, target, start in ((1, lower_local, 0), (2, upper, 2 * lay.cap)):
        count = lay.scan(mine, side, places)
        for i in range(lay.pairs):
            live = i < count
            tile = jnp.where(live, tiles[jnp.where(live, places[i], 0)], 0.0)
            target[start + i] = tile if side == 1 else tile.T


def next_local_pivot_kernel(lay, near, inverse, diag, tiles, *refs):
    local_terms(lay, near.at[0], near.at[1], inverse, diag, tiles, refs[:-1], refs[-1])


def incoming_kernel(lay, near, local, lower, mate_lower, arrived, keep, give, total):
    me, mine, mates = near.at[0], near.at[1], near.at[2]
    role = me[0] % 2
    places, terms = [], []
    for g, (meta, source) in enumerate(((mine, lower), (mates, mate_lower))):
        for j in range(lay.cap):
            s, _, v = lay.lookup(meta, 2 + role, 1, j)
            places.append(lay.place(s // lay.width, me[0]))
            terms.append(matmul_nt(arrived[g * lay.cap + v], source[role * lay.cap + j]))
    total[...] = local[...]
    for place, term in zip(places, terms):
        total[place] += term
    half = keep.shape[0]
    keep[...] = total[:half]
    give[...] = total[half:]


def newton_kernel(inverse, *refs):
    sums, out = refs[:-1], refs[-1]
    for i in range(out.shape[0]):
        x = inverse[i]
        xh, xl = split(x)
        product = matmul_nt_parts(xh, xl, *split(jnp.concatenate([part[i] for part in sums], 0)))
        out[i] = 2.0 * x + matmul_parts(*split(product), xh, xl)


def table_kernel(lay, me, metas, peers_below, peers_above, out, *refs):
    masks, places = refs[:4], refs[4]
    role = me[0] % 2
    out[2 * lay.table] = me[0]
    row = lax.broadcasted_iota(jnp.int32, masks[0].shape[1:], 0)
    for side in (1, 2):
        start = (side - 1) * lay.table
        base, peers = ((2, peers_below), (0, peers_above))[side - 1]
        for q in range(lay.n_tile):
            a, meta, peer = q ^ me[0], metas.at[q], peers.at[q]
            for j in range(lay.cap):
                s, _, v = lay.lookup(meta, base + role, side, j)
                out[start + a * lay.cap + j] = s // lay.width
                source = lay.listed(peer, 2 - base + role, v) // lay.width
                masks[2 * side - 2][a * lay.cap + j] = (row == s // lay.width).astype(F32)
                masks[2 * side - 1][a * lay.cap + j] = (row == source).astype(F32)
        for q in range(0, lay.n_tile, 2):
            meta = metas.at[q]
            begin = start + lay.listed_slots + ((q ^ me[0]) >> 1) * lay.pairs
            count = lay.scan(meta, side, places)
            for i in range(lay.pairs):
                s = jnp.where(i < count, places[i], 0)
                out[begin + i] = s // lay.width
                v = jnp.where(i < count, lay.link(meta, s), 0)
                out[begin + lay.local_slots + i] = v // lay.width


def scaled_kernel(lay, side, table, inverse, *refs):
    sources, (listed, local) = refs[:-2], refs[-2:]
    me = table[2 * lay.table]
    role = me % 2
    start = (side - 1) * lay.table

    def scaled(row, tile):
        x = inverse[lay.place(row, me)]
        return widen(matmul(x, tile) if side == 1 else matmul_nt(x, tile))

    at = 0
    for q in range(lay.n_tile):
        lists = sources[at]
        for j in range(lay.cap):
            k = (q ^ me) * lay.cap + j
            listed[k] = scaled(table[start + k], lists[role * lay.cap + j])
        at += 1
        if q % 2 == 0:
            pairs, first = (lists, 2 * lay.cap) if side == 2 else (sources[at], 0)
            at += side == 1
            for i in range(lay.pairs):
                k = ((q ^ me) >> 1) * lay.pairs + i
                local[k] = scaled(table[start + lay.listed_slots + k], pairs[first + i])


def first_kernel(lay, me, base, inverse, out):
    count = out.shape[1]
    mine = pl.ds(pl.multiple_of((me[0] >> 1) * count, count), count)
    for r in range(lay.rows):
        out[r] = times_tile(base[r, mine], widen(inverse[lay.place(r, me[0])]))


def local_sum_kernel(lay, side, table, x, tiles, out):
    start = (side - 1) * lay.table + lay.listed_slots
    terms = [times_tile(x[table[start + lay.local_slots + k]], tiles[k]) for k in range(lay.local_slots)]
    out[...] = jnp.zeros_like(out)
    for k, value in enumerate(terms):
        out[table[start + k]] += value


def listed_sum_kernel(lay, tiles, picks, sources, local, arrived, out):
    rows = [arrived[r] for r in range(lay.rows)]
    terms = []
    for k in range(lay.listed_slots):
        x = sum(sources[k, r : r + 1] * rows[r] for r in range(lay.rows))
        terms.append(times_tile(x, tiles[k]))
    for r in range(lay.rows):
        out[r] = local[r] + sum(picks[k, r : r + 1] * terms[k] for k in range(lay.listed_slots))


def local(krylov_block, diag_block, inverse_prev, coupling_tiles, slot_kind, slot_link, send_slots):
    rows, width, n, _ = coupling_tiles.shape
    cap = send_slots.shape[3]
    n_dom, n_tile = lax.axis_size("dom"), lax.axis_size("tile")
    lay = Layout(rows, width, cap, n_tile)
    vectors = krylov_block.shape[1]
    upper_bits = [1 << b for b in range(1, n_tile.bit_length() - 1)]

    me = lax.axis_index("tile").astype(jnp.int32).reshape(1)
    mine = jnp.concatenate([slot_kind.reshape(-1), slot_link.reshape(-1), send_slots.reshape(-1)])
    tiles = coupling_tiles.reshape(lay.slots, n, n)

    def swap(x, bit):
        return lax.ppermute(x, "tile", [(i, i ^ bit) for i in range(n_tile)])

    def along(x, sign):
        route = []
        for d in range(n_dom):
            for t in range(n_tile):
                to = d + sign * (1 + t % 2)
                if 0 <= to < n_dom:
                    route.append((d * n_tile + t, to * n_tile + t))
        return lax.ppermute(x, ("dom", "tile"), route)

    def summed(x):
        for bit in upper_bits:
            got = swap(x, bit)
            near = bit // 2
            got = got.reshape((n_tile // 2 // (2 * near), 2, near * lay.own_rows) + x.shape[1:])
            x = x + jnp.concatenate([got[:, 1:], got[:, :1]], 1).reshape(x.shape)
        return x

    def shape(*dims, dtype=F32):
        return jax.ShapeDtypeStruct(dims, dtype)

    kernel = lambda body, *bound: functools.partial(body, lay, *bound)
    product = 8 * n**3

    def over_chips(x):
        held = [x]
        for bit in upper_bits:
            held += [swap(one, bit) for one in held]
        return held

    mate_tiles = swap(tiles, 1)
    arriving = over_chips(inverse_prev)
    held = over_chips(mine)
    both = [swap(x, 1) for x in held]
    arriving, held, both = lax.optimization_barrier((arriving, held, both))
    mates = both[0]
    metas = jnp.stack([one for pair in zip(held, both) for one in pair])
    near = jnp.stack([jnp.broadcast_to(me, mine.shape), mine, mates])
    kept = jnp.concatenate(arriving, 0)
    mated = jnp.concatenate([swap(x, 1) for x in arriving], 0)
    half = rows // 2
    lists, local_list = shape(2 * cap, n, n), shape(lay.pairs, n, n)
    sent, summands = [shape(2 * cap, n // PARTS, n)] * PARTS, [shape(rows, n // PARTS, n)] * PARTS
    places = pltpu.SMEM((lay.slots + 1,), jnp.int32)
    total = pltpu.VMEM((rows, n, n), F32)
    for sweep in range(FSWEEPS):
        inverse = jnp.concatenate([kept, mated], 0)
        early, later = [], []
        if sweep == 0:
            *out, lower = call(kernel(outgoing_kernel), sent + [lists], (near,), (inverse, tiles, mate_tiles))
            arrived = [along(part, 1) for part in out]
            lowers = over_chips(lower)
            *here, mate_lower, lower_local, upper, mate_upper = call(
                kernel(local_pivot_kernel, PARTS),
                summands + [lists, local_list, shape(2 * cap + lay.pairs, n, n), lists],
                (near,),
                (inverse, diag_block, tiles, mate_tiles),
                flops=product * rows,
                scratch=(total, places),
            )
            early += lowers[1:]
        else:
            out = call(kernel(next_outgoing_kernel), sent, (near,), (inverse, upper, mate_upper))
            arrived = [along(part, 1) for part in out]
            here = call(
                kernel(next_local_pivot_kernel),
                summands,
                (near,),
                (inverse, diag_block, tiles),
                flops=product * rows,
                scratch=(total,),
            )
        if sweep == FSWEEPS - 1:
            lower_locals = over_chips(lower_local)
            mate_lowers = [mate_lower] + [swap(x, 1) for x in lowers[1:]]
            below, above = along(metas, 1), along(metas, -1)
            mask = shape(lay.listed_slots, rows, n)
            table, *masks = call(
                kernel(table_kernel),
                [shape(2 * lay.table + 1, dtype=jnp.int32)] + [mask] * 4,
                (me, metas, below, above),
                (),
                scratch=(places,),
                to_smem=1,
            )
            early += [*lower_locals[1:], *mate_lowers[1:], below, above]
            later += [table]
        sums = []
        for part in range(PARTS):
            keep, give = call(
                kernel(incoming_kernel),
                [shape(half, n // PARTS, n)] * 2,
                (near,),
                (here[part], lower, mate_lower, arrived[part]),
                scratch=(pltpu.VMEM((rows, n // PARTS, n), F32),),
                early=early if part == PARTS - 1 else (),
            )
            sums.append(summed(keep + swap(give, 1)))
        (kept,) = call(newton_kernel, [shape(half, n, n)], (), (kept, *sums), early=later)
        mated = swap(kept, 1)
    inverse = jnp.concatenate([kept, mated], 0)

    def scale(side, sources):
        return call(
            kernel(scaled_kernel, side),
            [
                shape(lay.listed_slots, 2 * n, n, dtype=BF16),
                shape(lay.local_slots, 2 * n, n, dtype=BF16),
            ],
            (table,),
            (inverse, *sources),
            flops=product * 24,
        )

    share = vectors // (n_tile // 2)
    block = shape(rows, share, n)
    (first,) = call(kernel(first_kernel), [block], (me,), (krylov_block, inverse))

    def sweeps(x, side, count, listed, local, early=()):
        base = x
        for sweep in range(count):
            arrived = along(x, 1 if side == 1 else -1)
            (here,) = call(
                kernel(local_sum_kernel, side), [block], (table,), (x, local), flops=8 * n**2 * vectors * rows
            )
            (part,) = call(
                kernel(listed_sum_kernel),
                [block],
                (),
                (listed, *masks[2 * side - 2 : 2 * side], here, arrived),
                early=early if sweep == count - 1 else (),
            )
            x = base - (part + swap(part, 1))
        return x

    uppers = over_chips(upper)
    mate_uppers = [mate_upper] + [swap(x, 1) for x in uppers[1:]]
    low = [x for three in zip(lowers, lower_locals, mate_lowers) for x in three]
    up = [x for pair in zip(uppers, mate_uppers) for x in pair]
    solved = sweeps(first, 1, LSWEEPS, *scale(1, low), early=uppers[1:])
    solved = sweeps(solved, 2, USWEEPS, *scale(2, up))
    for bit in upper_bits:
        got = swap(solved, bit)
        solved = jnp.where(
            (me[0] & bit) == 0, jnp.concatenate([solved, got], 1), jnp.concatenate([got, solved], 1)
        )
    return (kept[: lay.own_rows], solved)


def solution(mesh):
    placed = (
        P("dom", None, None),
        P(("dom", "tile"), None, None),
        P(("dom", "tile"), None, None),
        P("dom", "tile", None, None),
        P("dom", "tile"),
        P("dom", "tile"),
        P("dom", "tile", None, None),
    )
    return jax.shard_map(
        local,
        mesh=mesh,
        in_specs=placed,
        out_specs=(P(("dom", "tile"), None, None), P("dom", None, None)),
        check_vma=False,
    )
```

```python
import functools

import jax
import jax.numpy as jnp
from jax import lax
from jax.experimental import pallas as pl
from jax.experimental.pallas import tpu as pltpu
from jax.sharding import PartitionSpec as P

FSWEEPS = 2
LSWEEPS = 3
USWEEPS = 3
F32 = jnp.float32
BF16 = jnp.bfloat16


def split(a):
    hi = a.astype(BF16)
    return hi, (a - hi.astype(F32)).astype(BF16)


def matmul_parts(ah, al, bh, bl):
    lhs = jnp.concatenate([ah, al], 1)
    pair = jnp.concatenate([bh, bl], 1)
    rhs = jnp.concatenate([pair, pair], 0)
    out = jnp.dot(lhs, rhs, preferred_element_type=F32)
    n = bh.shape[1]
    return out[:, :n] + out[:, n:]


def matmul(a, b):
    return matmul_parts(*split(a), *split(b))


def times_tile(x, wide):
    v, n = x.shape
    stacked = jnp.concatenate(split(x), 0)
    out = lax.dot_general(stacked, wide, (((1,), (1,)), ((), ())), preferred_element_type=F32)
    return out[:v, :n] + (out[v:, :n] + out[:v, n:])


def widen(a):
    return jnp.concatenate(split(a), 0)


class Layout:
    def __init__(self, rows, width, cap, n_tile):
        self.rows, self.width, self.cap, self.n_tile = rows, width, cap, n_tile
        self.slots = rows * width
        self.own_rows = rows // n_tile
        self.pairs = max(1, (self.slots - 4 * cap) // 2)
        self.listed_slots = n_tile * cap
        self.local_slots = n_tile // 2 * self.pairs
        self.table = self.listed_slots + 2 * self.local_slots

    def kind(self, meta, s):
        return meta[s]

    def link(self, meta, s):
        return meta[self.slots + s]

    def listed(self, meta, which, j):
        return meta[2 * self.slots + which * self.cap + j]

    def place(self, r, me):
        far = (r // self.own_rows) ^ me
        return ((far & 1) * (self.n_tile // 2) + (far >> 1)) * self.own_rows + r % self.own_rows

    def lookup(self, meta, which, side, j):
        s = self.listed(meta, which, j)
        v = self.link(meta, s) - self.slots - (which % 2) * self.cap
        live = (self.kind(meta, s) == side) & (v >= 0) & (v < self.cap)
        return s, live, jnp.clip(v, 0, self.cap - 1)

    def is_local(self, meta, s, side):
        return (self.kind(meta, s) == side) & (self.link(meta, s) < self.slots)

    def scan(self, meta, side, places):
        count = jnp.int32(0)
        for s in range(self.slots):
            places[count] = s
            count = count + self.is_local(meta, s, side).astype(jnp.int32)
        return count


def smem():
    return pl.BlockSpec(memory_space=pltpu.SMEM)


def vmem():
    return pl.BlockSpec(memory_space=pltpu.VMEM)


def call(body, outs, scalars, arrays, flops=0, scratch=(), early=(), to_smem=0):
    moved = sum(a.size * a.dtype.itemsize for a in arrays) + sum(o.size * o.dtype.itemsize for o in outs)
    return pl.pallas_call(
        body if not early else lambda *refs: body(*refs[len(early) :]),
        out_shape=outs,
        in_specs=[pl.BlockSpec(memory_space=pl.ANY)] * len(early) + [smem()] * len(scalars) + [vmem()] * len(arrays),
        out_specs=[smem()] * to_smem + [vmem()] * (len(outs) - to_smem),
        scratch_shapes=list(scratch),
        compiler_params=pltpu.CompilerParams(vmem_limit_bytes=8 << 20),
        cost_estimate=pl.CostEstimate(flops=flops, bytes_accessed=moved, transcendentals=0),
    )(*early, *scalars, *arrays)


def listed_tiles(lay, meta, side, tiles, out):
    for which in range(2):
        for j in range(lay.cap):
            s, live, _ = lay.lookup(meta, 4 - 2 * side + which, side, j)
            out[which * lay.cap + j] = jnp.where(live, tiles[s], 0.0)


def outgoing_kernel(lay, near, inverse, tiles, mate_tiles, out, lower):
    me, mine, mates = near.at[0], near.at[1], near.at[2]
    role = me[0] % 2
    for g, (meta, source) in enumerate(((mine, tiles), (mates, mate_tiles))):
        for j in range(lay.cap):
            s, live, _ = lay.lookup(meta, role, 2, j)
            tile = jnp.where(live, source[s], 0.0)
            out[g * lay.cap + j] = matmul(inverse[lay.place(s // lay.width, me[0])], tile)
    listed_tiles(lay, mine, 1, tiles, lower)


def next_outgoing_kernel(lay, near, inverse, upper, mate_upper, out):
    me, mine, mates = near.at[0], near.at[1], near.at[2]
    role = me[0] % 2
    for g, (meta, source) in enumerate(((mine, upper), (mates, mate_upper))):
        for j in range(lay.cap):
            r = lay.listed(meta, role, j) // lay.width
            out[g * lay.cap + j] = matmul(inverse[lay.place(r, me[0])], source[role * lay.cap + j])


def local_terms(lay, me, mine, inverse, diag, tiles, out):
    out[: lay.own_rows] = -diag[...]
    out[lay.own_rows :] = jnp.zeros((lay.rows - lay.own_rows,) + diag.shape[1:], F32)

    @pl.loop(0, lay.slots)
    def _(s):
        @pl.when(lay.is_local(mine, s, 1))
        def _():
            v = lay.link(mine, s)
            q = matmul(inverse[lay.place(v // lay.width, me[0])], tiles[v])
            out[lay.place(s // lay.width, me[0])] += matmul(tiles[s], q)


def local_pivot_kernel(
    lay, near, inverse, diag, tiles, mate_tiles, out, mate_lower, lower_local, upper, mate_upper, places
):
    me, mine, mates = near.at[0], near.at[1], near.at[2]
    local_terms(lay, me, mine, inverse, diag, tiles, out)
    listed_tiles(lay, mates, 1, mate_tiles, mate_lower)
    listed_tiles(lay, mates, 2, mate_tiles, mate_upper)
    listed_tiles(lay, mine, 2, tiles, upper)
    for side, target, start in ((1, lower_local, 0), (2, upper, 2 * lay.cap)):
        count = lay.scan(mine, side, places)
        for i in range(lay.pairs):
            live = i < count
            target[start + i] = jnp.where(live, tiles[jnp.where(live, places[i], 0)], 0.0)


def next_local_pivot_kernel(lay, near, inverse, diag, tiles, out):
    local_terms(lay, near.at[0], near.at[1], inverse, diag, tiles, out)


def incoming_kernel(lay, near, local, lower, mate_lower, arrived, keep, give, total):
    me, mine, mates = near.at[0], near.at[1], near.at[2]
    role = me[0] % 2
    places, terms = [], []
    for g, (meta, source) in enumerate(((mine, lower), (mates, mate_lower))):
        for j in range(lay.cap):
            s, _, v = lay.lookup(meta, 2 + role, 1, j)
            places.append(lay.place(s // lay.width, me[0]))
            terms.append(matmul(source[role * lay.cap + j], arrived[g * lay.cap + v]))
    total[...] = local[...]
    for place, term in zip(places, terms):
        total[place] += term
    half = keep.shape[0]
    keep[...] = total[:half]
    give[...] = total[half:]


def newton_kernel(inverse, sums, out):
    for i in range(out.shape[0]):
        x = inverse[i]
        xh, xl = split(x)
        product = matmul_parts(xh, xl, *split(sums[i]))
        out[i] = 2.0 * x + matmul_parts(*split(product), xh, xl)


def table_kernel(lay, me, metas, peers_below, peers_above, out, *refs):
    masks, places = refs[:4], refs[4]
    role = me[0] % 2
    out[2 * lay.table] = me[0]
    row = lax.broadcasted_iota(jnp.int32, masks[0].shape[1:], 0)
    for side in (1, 2):
        start = (side - 1) * lay.table
        base, peers = ((2, peers_below), (0, peers_above))[side - 1]
        for q in range(lay.n_tile):
            a, meta, peer = q ^ me[0], metas.at[q], peers.at[q]
            for j in range(lay.cap):
                s, _, v = lay.lookup(meta, base + role, side, j)
                out[start + a * lay.cap + j] = s // lay.width
                source = lay.listed(peer, 2 - base + role, v) // lay.width
                masks[2 * side - 2][a * lay.cap + j] = (row == s // lay.width).astype(F32)
                masks[2 * side - 1][a * lay.cap + j] = (row == source).astype(F32)
        for q in range(0, lay.n_tile, 2):
            meta = metas.at[q]
            begin = start + lay.listed_slots + ((q ^ me[0]) >> 1) * lay.pairs
            count = lay.scan(meta, side, places)
            for i in range(lay.pairs):
                s = jnp.where(i < count, places[i], 0)
                out[begin + i] = s // lay.width
                v = jnp.where(i < count, lay.link(meta, s), 0)
                out[begin + lay.local_slots + i] = v // lay.width


def scaled_kernel(lay, side, table, inverse, *refs):
    sources, (listed, local) = refs[:-2], refs[-2:]
    me = table[2 * lay.table]
    role = me % 2
    start = (side - 1) * lay.table

    def scaled(row, tile):
        return widen(matmul(inverse[lay.place(row, me)], tile))

    at = 0
    for q in range(lay.n_tile):
        lists = sources[at]
        for j in range(lay.cap):
            k = (q ^ me) * lay.cap + j
            listed[k] = scaled(table[start + k], lists[role * lay.cap + j])
        at += 1
        if q % 2 == 0:
            pairs, first = (lists, 2 * lay.cap) if side == 2 else (sources[at], 0)
            at += side == 1
            for i in range(lay.pairs):
                k = ((q ^ me) >> 1) * lay.pairs + i
                local[k] = scaled(table[start + lay.listed_slots + k], pairs[first + i])


def first_kernel(lay, me, base, inverse, out):
    count = out.shape[1]
    mine = pl.ds(pl.multiple_of((me[0] >> 1) * count, count), count)
    for r in range(lay.rows):
        out[r] = times_tile(base[r, mine], widen(inverse[lay.place(r, me[0])]))


def local_sum_kernel(lay, side, table, x, tiles, out):
    start = (side - 1) * lay.table + lay.listed_slots
    terms = [times_tile(x[table[start + lay.local_slots + k]], tiles[k]) for k in range(lay.local_slots)]
    out[...] = jnp.zeros_like(out)
    for k, value in enumerate(terms):
        out[table[start + k]] += value


def listed_sum_kernel(lay, tiles, picks, sources, local, arrived, out):
    rows = [arrived[r] for r in range(lay.rows)]
    terms = []
    for k in range(lay.listed_slots):
        x = sum(sources[k, r : r + 1] * rows[r] for r in range(lay.rows))
        terms.append(times_tile(x, tiles[k]))
    for r in range(lay.rows):
        out[r] = local[r] + sum(picks[k, r : r + 1] * terms[k] for k in range(lay.listed_slots))


def local(krylov_block, diag_block, inverse_prev, coupling_tiles, slot_kind, slot_link, send_slots):
    rows, width, n, _ = coupling_tiles.shape
    cap = send_slots.shape[3]
    n_dom, n_tile = lax.axis_size("dom"), lax.axis_size("tile")
    lay = Layout(rows, width, cap, n_tile)
    vectors = krylov_block.shape[1]
    upper_bits = [1 << b for b in range(1, n_tile.bit_length() - 1)]

    me = lax.axis_index("tile").astype(jnp.int32).reshape(1)
    mine = jnp.concatenate([slot_kind.reshape(-1), slot_link.reshape(-1), send_slots.reshape(-1)])
    tiles = coupling_tiles.reshape(lay.slots, n, n)

    def swap(x, bit):
        return lax.ppermute(x, "tile", [(i, i ^ bit) for i in range(n_tile)])

    def along(x, sign):
        route = []
        for d in range(n_dom):
            for t in range(n_tile):
                to = d + sign * (1 + t % 2)
                if 0 <= to < n_dom:
                    route.append((d * n_tile + t, to * n_tile + t))
        return lax.ppermute(x, ("dom", "tile"), route)

    def summed(x):
        for bit in upper_bits:
            got = swap(x, bit)
            near = bit // 2
            got = got.reshape((n_tile // 2 // (2 * near), 2, near * lay.own_rows) + x.shape[1:])
            x = x + jnp.concatenate([got[:, 1:], got[:, :1]], 1).reshape(x.shape)
        return x

    def shape(*dims, dtype=F32):
        return jax.ShapeDtypeStruct(dims, dtype)

    kernel = lambda body, *bound: functools.partial(body, lay, *bound)
    product = 8 * n**3

    def over_chips(x):
        held = [x]
        for bit in upper_bits:
            held += [swap(one, bit) for one in held]
        return held

    mate_tiles = swap(tiles, 1)
    arriving = over_chips(inverse_prev)
    mates = swap(mine, 1)
    arriving, mine, mates = lax.optimization_barrier((arriving, mine, mates))
    near = jnp.stack([jnp.broadcast_to(me, mine.shape), mine, mates])
    kept = jnp.concatenate(arriving, 0)
    mated = jnp.concatenate([swap(x, 1) for x in arriving], 0)
    half = rows // 2
    lists, local_list = shape(2 * cap, n, n), shape(lay.pairs, n, n)
    places = pltpu.SMEM((lay.slots + 1,), jnp.int32)
    for sweep in range(FSWEEPS):
        inverse = jnp.concatenate([kept, mated], 0)
        early, later = [], []
        if sweep == 0:
            out, lower = call(
                kernel(outgoing_kernel), [lists] * 2, (near,), (inverse, tiles, mate_tiles)
            )
            arrived = along(out, 1)
            lowers = over_chips(lower)
            here, mate_lower, lower_local, upper, mate_upper = call(
                kernel(local_pivot_kernel),
                [shape(rows, n, n), lists, local_list, shape(2 * cap + lay.pairs, n, n), lists],
                (near,),
                (inverse, diag_block, tiles, mate_tiles),
                flops=product * rows,
                scratch=(places,),
            )
            early += lowers[1:]
            metas = jnp.concatenate(over_chips(near[1:]), 0)
            later += [metas]
        else:
            (out,) = call(
                kernel(next_outgoing_kernel), [lists], (near,), (inverse, upper, mate_upper)
            )
            arrived = along(out, 1)
            (here,) = call(
                kernel(next_local_pivot_kernel),
                [shape(rows, n, n)],
                (near,),
                (inverse, diag_block, tiles),
                flops=product * rows,
            )
        if sweep == FSWEEPS - 1:
            lower_locals = over_chips(lower_local)
            mate_lowers = [mate_lower] + [swap(x, 1) for x in lowers[1:]]
            below, above = along(metas, 1), along(metas, -1)
            mask = shape(lay.listed_slots, rows, n)
            table, *masks = call(
                kernel(table_kernel),
                [shape(2 * lay.table + 1, dtype=jnp.int32)] + [mask] * 4,
                (me, metas, below, above),
                (),
                scratch=(places,),
                to_smem=1,
            )
            early += [*lower_locals[1:], *mate_lowers[1:], below, above]
            later += [table]
        keep, give = call(
            kernel(incoming_kernel),
            [shape(half, n, n)] * 2,
            (near,),
            (here, lower, mate_lower, arrived),
            scratch=(pltpu.VMEM((rows, n, n), F32),),
            early=early,
        )
        sums = summed(keep + swap(give, 1))
        (kept,) = call(newton_kernel, [shape(half, n, n)], (), (kept, sums), early=later)
        mated = swap(kept, 1)
    inverse = jnp.concatenate([kept, mated], 0)

    def scale(side, sources):
        return call(
            kernel(scaled_kernel, side),
            [
                shape(lay.listed_slots, 2 * n, n, dtype=BF16),
                shape(lay.local_slots, 2 * n, n, dtype=BF16),
            ],
            (table,),
            (inverse, *sources),
            flops=product * 24,
        )

    share = vectors // (n_tile // 2)
    block = shape(rows, share, n)
    (first,) = call(kernel(first_kernel), [block], (me,), (krylov_block, inverse))

    def sweeps(x, side, count, listed, local, early=()):
        base = x
        for sweep in range(count):
            arrived = along(x, 1 if side == 1 else -1)
            (here,) = call(
                kernel(local_sum_kernel, side), [block], (table,), (x, local), flops=8 * n**2 * vectors * rows
            )
            (part,) = call(
                kernel(listed_sum_kernel),
                [block],
                (),
                (listed, *masks[2 * side - 2 : 2 * side], here, arrived),
                early=early if sweep == count - 1 else (),
            )
            x = base - (part + swap(part, 1))
        return x

    uppers = over_chips(upper)
    mate_uppers = [mate_upper] + [swap(x, 1) for x in uppers[1:]]
    low = [x for three in zip(lowers, lower_locals, mate_lowers) for x in three]
    up = [x for pair in zip(uppers, mate_uppers) for x in pair]
    solved = sweeps(first, 1, LSWEEPS, *scale(1, low), early=uppers[1:])
    solved = sweeps(solved, 2, USWEEPS, *scale(2, up))
    for bit in upper_bits:
        got = swap(solved, bit)
        solved = jnp.where(
            (me[0] & bit) == 0, jnp.concatenate([solved, got], 1), jnp.concatenate([got, solved], 1)
        )
    return (kept[: lay.own_rows], solved)


def solution(mesh):
    placed = (
        P("dom", None, None),
        P(("dom", "tile"), None, None),
        P(("dom", "tile"), None, None),
        P("dom", "tile", None, None),
        P("dom", "tile"),
        P("dom", "tile"),
        P("dom", "tile", None, None),
    )
    return jax.shard_map(
        local,
        mesh=mesh,
        in_specs=placed,
        out_specs=(P(("dom", "tile"), None, None), P("dom", None, None)),
        check_vma=False,
    )
```

```python
import functools

import jax
import jax.numpy as jnp
from jax import lax
from jax.experimental import pallas as pl
from jax.experimental.pallas import tpu as pltpu
from jax.sharding import PartitionSpec as P

FSWEEPS = 2
LSWEEPS = 3
USWEEPS = 3
F32 = jnp.float32
BF16 = jnp.bfloat16


def split(a):
    hi = a.astype(BF16)
    return hi, (a - hi.astype(F32)).astype(BF16)


def beside(a):
    return jnp.concatenate(split(a), 1)


def matmul_beside(lhs, pair):
    out = jnp.dot(lhs, jnp.concatenate([pair, pair], 0), preferred_element_type=F32)
    n = pair.shape[1] // 2
    return out[:, :n] + out[:, n:]


def matmul_parts(ah, al, bh, bl):
    return matmul_beside(jnp.concatenate([ah, al], 1), jnp.concatenate([bh, bl], 1))


def matmul(a, b):
    return matmul_parts(*split(a), *split(b))


def times_tile(x, wide):
    v, n = x.shape
    stacked = jnp.concatenate(split(x), 0)
    out = lax.dot_general(stacked, wide, (((1,), (1,)), ((), ())), preferred_element_type=F32)
    return out[:v, :n] + (out[v:, :n] + out[:v, n:])


def widen(a):
    return jnp.concatenate(split(a), 0)


class Layout:
    def __init__(self, rows, width, cap, n_tile):
        self.rows, self.width, self.cap, self.n_tile = rows, width, cap, n_tile
        self.slots = rows * width
        self.own_rows = rows // n_tile
        self.pairs = max(1, (self.slots - 4 * cap) // 2)
        self.listed_slots = n_tile * cap
        self.local_slots = n_tile // 2 * self.pairs
        self.table = self.listed_slots + 2 * self.local_slots

    def kind(self, meta, s):
        return meta[s]

    def link(self, meta, s):
        return meta[self.slots + s]

    def listed(self, meta, which, j):
        return meta[2 * self.slots + which * self.cap + j]

    def place(self, r, me):
        far = (r // self.own_rows) ^ me
        return ((far & 1) * (self.n_tile // 2) + (far >> 1)) * self.own_rows + r % self.own_rows

    def lookup(self, meta, which, side, j):
        s = self.listed(meta, which, j)
        v = self.link(meta, s) - self.slots - (which % 2) * self.cap
        live = (self.kind(meta, s) == side) & (v >= 0) & (v < self.cap)
        return s, live, jnp.clip(v, 0, self.cap - 1)

    def is_local(self, meta, s, side):
        return (self.kind(meta, s) == side) & (self.link(meta, s) < self.slots)

    def scan(self, meta, side, places):
        count = jnp.int32(0)
        for s in range(self.slots):
            places[count] = s
            count = count + self.is_local(meta, s, side).astype(jnp.int32)
        return count


def smem():
    return pl.BlockSpec(memory_space=pltpu.SMEM)


def vmem():
    return pl.BlockSpec(memory_space=pltpu.VMEM)


def call(body, outs, scalars, arrays, flops=0, scratch=(), early=(), to_smem=0, fetched=()):
    moved = sum(a.size * a.dtype.itemsize for a in arrays) + sum(o.size * o.dtype.itemsize for o in outs)
    return pl.pallas_call(
        body if not early else lambda *refs: body(*refs[len(early) :]),
        out_shape=outs,
        in_specs=[pl.BlockSpec(memory_space=pl.ANY)] * (len(early) + len(fetched)) + [smem()] * len(scalars) + [vmem()] * len(arrays),
        out_specs=[smem()] * to_smem + [vmem()] * (len(outs) - to_smem),
        scratch_shapes=list(scratch),
        compiler_params=pltpu.CompilerParams(vmem_limit_bytes=8 << 20),
        cost_estimate=pl.CostEstimate(flops=flops, bytes_accessed=moved, transcendentals=0),
    )(*early, *fetched, *scalars, *arrays)


def listed_tiles(lay, meta, side, tiles, out):
    for which in range(2):
        for j in range(lay.cap):
            s, live, _ = lay.lookup(meta, 4 - 2 * side + which, side, j)
            out[which * lay.cap + j] = jnp.where(live, tiles[s], 0.0)


def outgoing_products(lay, inverse, near_source, near, done, halves, tile_of, out):
    fetch = pltpu.make_async_copy(near_source, near, done)
    fetch.start()
    for r in range(lay.rows):
        halves[r] = beside(inverse[r])
    fetch.wait()
    me, metas = near.at[0], (near.at[1], near.at[2])
    for g, meta in enumerate(metas):
        for j in range(lay.cap):
            s, live, _ = lay.lookup(meta, me[0] % 2, 2, j)
            tile = tile_of(g, me[0] % 2 * lay.cap + j, s, live)
            out[g * lay.cap + j] = matmul_beside(halves[lay.place(s // lay.width, me[0])], beside(tile))


def outgoing_kernel(lay, near_source, inverse, tiles, mate_tiles, out, lower, halves, near, done):
    held = (tiles, mate_tiles)
    outgoing_products(
        lay, inverse, near_source, near, done, halves, lambda g, k, s, live: jnp.where(live, held[g][s], 0.0), out
    )
    listed_tiles(lay, near.at[1], 1, tiles, lower)


def next_outgoing_kernel(lay, near_source, inverse, upper, mate_upper, out, halves, near, done):
    held = (upper, mate_upper)
    outgoing_products(lay, inverse, near_source, near, done, halves, lambda g, k, s, live: held[g][k], out)


def local_terms(lay, me, mine, inverse, diag, tiles, out):
    out[: lay.own_rows] = -diag[...]
    out[lay.own_rows :] = jnp.zeros((lay.rows - lay.own_rows,) + diag.shape[1:], F32)

    @pl.loop(0, lay.slots)
    def _(s):
        @pl.when(lay.is_local(mine, s, 1))
        def _():
            v = lay.link(mine, s)
            q = matmul(inverse[lay.place(v // lay.width, me[0])], tiles[v])
            out[lay.place(s // lay.width, me[0])] += matmul(tiles[s], q)


def local_pivot_kernel(
    lay, near, inverse, diag, tiles, mate_tiles, out, mate_lower, lower_local, upper, mate_upper, places
):
    me, mine, mates = near.at[0], near.at[1], near.at[2]
    local_terms(lay, me, mine, inverse, diag, tiles, out)
    listed_tiles(lay, mates, 1, mate_tiles, mate_lower)
    listed_tiles(lay, mates, 2, mate_tiles, mate_upper)
    listed_tiles(lay, mine, 2, tiles, upper)
    for side, target, start in ((1, lower_local, 0), (2, upper, 2 * lay.cap)):
        count = lay.scan(mine, side, places)
        for i in range(lay.pairs):
            live = i < count
            target[start + i] = jnp.where(live, tiles[jnp.where(live, places[i], 0)], 0.0)


def next_local_pivot_kernel(lay, near, inverse, diag, tiles, out):
    local_terms(lay, near.at[0], near.at[1], inverse, diag, tiles, out)


def incoming_kernel(lay, near_source, local, lower, mate_lower, arrived, keep, give, total, halves, near, done):
    fetch = pltpu.make_async_copy(near_source, near, done)
    fetch.start()
    total[...] = local[...]
    for k in range(2 * lay.cap):
        halves[k] = beside(arrived[k])
    fetch.wait()
    me, mine, mates = near.at[0], near.at[1], near.at[2]
    role = me[0] % 2
    places, terms = [], []
    for g, (meta, source) in enumerate(((mine, lower), (mates, mate_lower))):
        for j in range(lay.cap):
            s, _, v = lay.lookup(meta, 2 + role, 1, j)
            places.append(lay.place(s // lay.width, me[0]))
            terms.append(matmul_beside(beside(source[role * lay.cap + j]), halves[g * lay.cap + v]))
    for place, term in zip(places, terms):
        total[place] += term
    half = keep.shape[0]
    keep[...] = total[:half]
    give[...] = total[half:]


def newton_kernel(inverse, sums, out):
    for i in range(out.shape[0]):
        x = inverse[i]
        xh, xl = split(x)
        product = matmul_parts(xh, xl, *split(sums[i]))
        out[i] = 2.0 * x + matmul_parts(*split(product), xh, xl)


def table_kernel(lay, me, metas, peers_below, peers_above, out, *refs):
    masks, places = refs[:4], refs[4]
    role = me[0] % 2
    out[2 * lay.table] = me[0]
    row = lax.broadcasted_iota(jnp.int32, masks[0].shape[1:], 0)
    for side in (1, 2):
        start = (side - 1) * lay.table
        base, peers = ((2, peers_below), (0, peers_above))[side - 1]
        for q in range(lay.n_tile):
            a, meta, peer = q ^ me[0], metas.at[q], peers.at[q]
            for j in range(lay.cap):
                s, _, v = lay.lookup(meta, base + role, side, j)
                out[start + a * lay.cap + j] = s // lay.width
                source = lay.listed(peer, 2 - base + role, v) // lay.width
                masks[2 * side - 2][a * lay.cap + j] = (row == s // lay.width).astype(F32)
                masks[2 * side - 1][a * lay.cap + j] = (row == source).astype(F32)
        for q in range(0, lay.n_tile, 2):
            meta = metas.at[q]
            begin = start + lay.listed_slots + ((q ^ me[0]) >> 1) * lay.pairs
            count = lay.scan(meta, side, places)
            for i in range(lay.pairs):
                s = jnp.where(i < count, places[i], 0)
                out[begin + i] = s // lay.width
                v = jnp.where(i < count, lay.link(meta, s), 0)
                out[begin + lay.local_slots + i] = v // lay.width


def scaled_kernel(lay, side, table, inverse, *refs):
    sources, (listed, local) = refs[:-2], refs[-2:]
    me = table[2 * lay.table]
    role = me % 2
    start = (side - 1) * lay.table

    def scaled(row, tile):
        return widen(matmul(inverse[lay.place(row, me)], tile))

    at = 0
    for q in range(lay.n_tile):
        lists = sources[at]
        for j in range(lay.cap):
            k = (q ^ me) * lay.cap + j
            listed[k] = scaled(table[start + k], lists[role * lay.cap + j])
        at += 1
        if q % 2 == 0:
            pairs, first = (lists, 2 * lay.cap) if side == 2 else (sources[at], 0)
            at += side == 1
            for i in range(lay.pairs):
                k = ((q ^ me) >> 1) * lay.pairs + i
                local[k] = scaled(table[start + lay.listed_slots + k], pairs[first + i])


def first_kernel(lay, me, base, inverse, out):
    count = out.shape[1]
    mine = pl.ds(pl.multiple_of((me[0] >> 1) * count, count), count)
    for r in range(lay.rows):
        out[r] = times_tile(base[r, mine], widen(inverse[lay.place(r, me[0])]))


def local_sum_kernel(lay, side, table, x, tiles, out):
    start = (side - 1) * lay.table + lay.listed_slots
    terms = [times_tile(x[table[start + lay.local_slots + k]], tiles[k]) for k in range(lay.local_slots)]
    out[...] = jnp.zeros_like(out)
    for k, value in enumerate(terms):
        out[table[start + k]] += value


def listed_sum_kernel(lay, tiles, picks, sources, local, arrived, out):
    rows = [arrived[r] for r in range(lay.rows)]
    terms = []
    for k in range(lay.listed_slots):
        x = sum(sources[k, r : r + 1] * rows[r] for r in range(lay.rows))
        terms.append(times_tile(x, tiles[k]))
    for r in range(lay.rows):
        out[r] = local[r] + sum(picks[k, r : r + 1] * terms[k] for k in range(lay.listed_slots))


def local(krylov_block, diag_block, inverse_prev, coupling_tiles, slot_kind, slot_link, send_slots):
    rows, width, n, _ = coupling_tiles.shape
    cap = send_slots.shape[3]
    n_dom, n_tile = lax.axis_size("dom"), lax.axis_size("tile")
    lay = Layout(rows, width, cap, n_tile)
    vectors = krylov_block.shape[1]
    upper_bits = [1 << b for b in range(1, n_tile.bit_length() - 1)]

    me = lax.axis_index("tile").astype(jnp.int32).reshape(1)
    mine = jnp.concatenate([slot_kind.reshape(-1), slot_link.reshape(-1), send_slots.reshape(-1)])
    tiles = coupling_tiles.reshape(lay.slots, n, n)

    def swap(x, bit):
        return lax.ppermute(x, "tile", [(i, i ^ bit) for i in range(n_tile)])

    def along(x, sign):
        route = []
        for d in range(n_dom):
            for t in range(n_tile):
                to = d + sign * (1 + t % 2)
                if 0 <= to < n_dom:
                    route.append((d * n_tile + t, to * n_tile + t))
        return lax.ppermute(x, ("dom", "tile"), route)

    def summed(x):
        for bit in upper_bits:
            got = swap(x, bit)
            near = bit // 2
            got = got.reshape((n_tile // 2 // (2 * near), 2, near * lay.own_rows) + x.shape[1:])
            x = x + jnp.concatenate([got[:, 1:], got[:, :1]], 1).reshape(x.shape)
        return x

    def shape(*dims, dtype=F32):
        return jax.ShapeDtypeStruct(dims, dtype)

    kernel = lambda body, *bound: functools.partial(body, lay, *bound)
    product = 8 * n**3

    def over_chips(x):
        held = [x]
        for bit in upper_bits:
            held += [swap(one, bit) for one in held]
        return held

    mate_tiles = swap(tiles, 1)
    arriving = over_chips(inverse_prev)
    mates = swap(mine, 1)
    arriving, mine, mates = lax.optimization_barrier((arriving, mine, mates))
    near = jnp.stack([jnp.broadcast_to(me, mine.shape), mine, mates])
    kept = jnp.concatenate(arriving, 0)
    mated = jnp.concatenate([swap(x, 1) for x in arriving], 0)
    half = rows // 2
    lists, local_list = shape(2 * cap, n, n), shape(lay.pairs, n, n)
    places = pltpu.SMEM((lay.slots + 1,), jnp.int32)
    fetching = (pltpu.SMEM(near.shape, jnp.int32), pltpu.SemaphoreType.DMA)
    split_rows, whole_rows = pltpu.VMEM((rows, n, 2 * n), BF16), pltpu.VMEM((rows, n, n), F32)
    for sweep in range(FSWEEPS):
        inverse = jnp.concatenate([kept, mated], 0)
        early, later = [], []
        if sweep == 0:
            out, lower = call(
                kernel(outgoing_kernel),
                [lists] * 2,
                (),
                (inverse, tiles, mate_tiles),
                scratch=(split_rows, *fetching),
                fetched=(near,),
            )
            arrived = along(out, 1)
            lowers = over_chips(lower)
            here, mate_lower, lower_local, upper, mate_upper = call(
                kernel(local_pivot_kernel),
                [shape(rows, n, n), lists, local_list, shape(2 * cap + lay.pairs, n, n), lists],
                (near,),
                (inverse, diag_block, tiles, mate_tiles),
                flops=product * rows,
                scratch=(places,),
            )
            early += lowers[1:]
            metas = jnp.concatenate(over_chips(near[1:]), 0)
            later += [metas]
        else:
            (out,) = call(
                kernel(next_outgoing_kernel),
                [lists],
                (),
                (inverse, upper, mate_upper),
                scratch=(split_rows, *fetching),
                fetched=(near,),
            )
            arrived = along(out, 1)
            (here,) = call(
                kernel(next_local_pivot_kernel),
                [shape(rows, n, n)],
                (near,),
                (inverse, diag_block, tiles),
                flops=product * rows,
            )
        if sweep == FSWEEPS - 1:
            lower_locals = over_chips(lower_local)
            mate_lowers = [mate_lower] + [swap(x, 1) for x in lowers[1:]]
            below, above = along(metas, 1), along(metas, -1)
            mask = shape(lay.listed_slots, rows, n)
            table, *masks = call(
                kernel(table_kernel),
                [shape(2 * lay.table + 1, dtype=jnp.int32)] + [mask] * 4,
                (me, metas, below, above),
                (),
                scratch=(places,),
                to_smem=1,
            )
            early += [*lower_locals[1:], *mate_lowers[1:], below, above]
            later += [table]
        keep, give = call(
            kernel(incoming_kernel),
            [shape(half, n, n)] * 2,
            (),
            (here, lower, mate_lower, arrived),
            scratch=(whole_rows, pltpu.VMEM((2 * cap, n, 2 * n), BF16), *fetching),
            fetched=(near,),
            early=early,
        )
        sums = summed(keep + swap(give, 1))
        (kept,) = call(newton_kernel, [shape(half, n, n)], (), (kept, sums), early=later)
        mated = swap(kept, 1)
    inverse = jnp.concatenate([kept, mated], 0)

    def scale(side, sources):
        return call(
            kernel(scaled_kernel, side),
            [
                shape(lay.listed_slots, 2 * n, n, dtype=BF16),
                shape(lay.local_slots, 2 * n, n, dtype=BF16),
            ],
            (table,),
            (inverse, *sources),
            flops=product * 24,
        )

    share = vectors // (n_tile // 2)
    block = shape(rows, share, n)
    (first,) = call(kernel(first_kernel), [block], (me,), (krylov_block, inverse))

    def sweeps(x, side, count, listed, local, early=()):
        base = x
        for sweep in range(count):
            arrived = along(x, 1 if side == 1 else -1)
            (here,) = call(
                kernel(local_sum_kernel, side), [block], (table,), (x, local), flops=8 * n**2 * vectors * rows
            )
            (part,) = call(
                kernel(listed_sum_kernel),
                [block],
                (),
                (listed, *masks[2 * side - 2 : 2 * side], here, arrived),
                early=early if sweep == count - 1 else (),
            )
            x = base - (part + swap(part, 1))
        return x

    uppers = over_chips(upper)
    mate_uppers = [mate_upper] + [swap(x, 1) for x in uppers[1:]]
    low = [x for three in zip(lowers, lower_locals, mate_lowers) for x in three]
    up = [x for pair in zip(uppers, mate_uppers) for x in pair]
    solved = sweeps(first, 1, LSWEEPS, *scale(1, low), early=uppers[1:])
    solved = sweeps(solved, 2, USWEEPS, *scale(2, up))
    for bit in upper_bits:
        got = swap(solved, bit)
        solved = jnp.where(
            (me[0] & bit) == 0, jnp.concatenate([solved, got], 1), jnp.concatenate([got, solved], 1)
        )
    return (kept[: lay.own_rows], solved)


def solution(mesh):
    placed = (
        P("dom", None, None),
        P(("dom", "tile"), None, None),
        P(("dom", "tile"), None, None),
        P("dom", "tile", None, None),
        P("dom", "tile"),
        P("dom", "tile"),
        P("dom", "tile", None, None),
    )
    return jax.shard_map(
        local,
        mesh=mesh,
        in_specs=placed,
        out_specs=(P(("dom", "tile"), None, None), P("dom", None, None)),
        check_vma=False,
    )
```

```python
import functools

import jax
import jax.numpy as jnp
from jax import lax
from jax.experimental import pallas as pl
from jax.experimental.pallas import tpu as pltpu
from jax.sharding import PartitionSpec as P

FSWEEPS = 2
LSWEEPS = 3
USWEEPS = 3
F32 = jnp.float32
BF16 = jnp.bfloat16


def split(a):
    hi = a.astype(BF16)
    return hi, (a - hi.astype(F32)).astype(BF16)


def beside(a):
    return jnp.concatenate(split(a), 1)


def matmul_beside(lhs, pair):
    out = jnp.dot(lhs, jnp.concatenate([pair, pair], 0), preferred_element_type=F32)
    n = pair.shape[1] // 2
    return out[:, :n] + out[:, n:]


def matmul_parts(ah, al, bh, bl):
    return matmul_beside(jnp.concatenate([ah, al], 1), jnp.concatenate([bh, bl], 1))


def matmul(a, b):
    return matmul_parts(*split(a), *split(b))


def times_tile(x, wide):
    v, n = x.shape
    stacked = jnp.concatenate(split(x), 0)
    out = lax.dot_general(stacked, wide, (((1,), (1,)), ((), ())), preferred_element_type=F32)
    return out[:v, :n] + (out[v:, :n] + out[:v, n:])


def widen(a):
    return jnp.concatenate(split(a), 0)


class Layout:
    def __init__(self, rows, width, cap, n_tile):
        self.rows, self.width, self.cap, self.n_tile = rows, width, cap, n_tile
        self.slots = rows * width
        self.own_rows = rows // n_tile
        self.pairs = max(1, (self.slots - 4 * cap) // 2)
        self.listed_slots = n_tile * cap
        self.local_slots = n_tile // 2 * self.pairs
        self.table = self.listed_slots + 2 * self.local_slots

    def kind(self, meta, s):
        return meta[s]

    def link(self, meta, s):
        return meta[self.slots + s]

    def listed(self, meta, which, j):
        return meta[2 * self.slots + which * self.cap + j]

    def place(self, r, me):
        far = (r // self.own_rows) ^ me
        return ((far & 1) * (self.n_tile // 2) + (far >> 1)) * self.own_rows + r % self.own_rows

    def lookup(self, meta, which, side, j):
        s = self.listed(meta, which, j)
        v = self.link(meta, s) - self.slots - (which % 2) * self.cap
        live = (self.kind(meta, s) == side) & (v >= 0) & (v < self.cap)
        return s, live, jnp.clip(v, 0, self.cap - 1)

    def is_local(self, meta, s, side):
        return (self.kind(meta, s) == side) & (self.link(meta, s) < self.slots)

    def scan(self, meta, side, places):
        count = jnp.int32(0)
        for s in range(self.slots):
            places[count] = s
            count = count + self.is_local(meta, s, side).astype(jnp.int32)
        return count


def smem():
    return pl.BlockSpec(memory_space=pltpu.SMEM)


def vmem():
    return pl.BlockSpec(memory_space=pltpu.VMEM)


def call(body, outs, scalars, arrays, flops=0, scratch=(), early=(), to_smem=0, fetched=()):
    moved = sum(a.size * a.dtype.itemsize for a in arrays) + sum(o.size * o.dtype.itemsize for o in outs)
    return pl.pallas_call(
        body if not early else lambda *refs: body(*refs[len(early) :]),
        out_shape=outs,
        in_specs=[pl.BlockSpec(memory_space=pl.ANY)] * (len(early) + len(fetched)) + [smem()] * len(scalars) + [vmem()] * len(arrays),
        out_specs=[smem()] * to_smem + [vmem()] * (len(outs) - to_smem),
        scratch_shapes=list(scratch),
        compiler_params=pltpu.CompilerParams(vmem_limit_bytes=8 << 20),
        cost_estimate=pl.CostEstimate(flops=flops, bytes_accessed=moved, transcendentals=0),
    )(*early, *fetched, *scalars, *arrays)


def listed_tiles(lay, meta, side, tiles, out):
    for which in range(2):
        for j in range(lay.cap):
            s, live, _ = lay.lookup(meta, 4 - 2 * side + which, side, j)
            out[which * lay.cap + j] = jnp.where(live, tiles[s], 0.0)


def outgoing_products(lay, inverse, near_source, near, done, halves, tile_of, out):
    fetch = pltpu.make_async_copy(near_source, near, done)
    fetch.start()
    for r in range(lay.rows):
        halves[r] = beside(inverse[r])
    fetch.wait()
    me, metas = near.at[0], (near.at[1], near.at[2])
    for g, meta in enumerate(metas):
        for j in range(lay.cap):
            s, live, _ = lay.lookup(meta, me[0] % 2, 2, j)
            tile = tile_of(g, me[0] % 2 * lay.cap + j, s, live)
            out[g * lay.cap + j] = matmul_beside(halves[lay.place(s // lay.width, me[0])], beside(tile))


def outgoing_kernel(lay, near_source, inverse, tiles, mate_tiles, out, lower, halves, near, done):
    held = (tiles, mate_tiles)
    outgoing_products(
        lay, inverse, near_source, near, done, halves, lambda g, k, s, live: jnp.where(live, held[g][s], 0.0), out
    )
    listed_tiles(lay, near.at[1], 1, tiles, lower)


def next_outgoing_kernel(lay, near_source, inverse, upper, mate_upper, out, halves, near, done):
    held = (upper, mate_upper)
    outgoing_products(lay, inverse, near_source, near, done, halves, lambda g, k, s, live: held[g][k], out)


def local_terms(lay, me, mine, inverse, diag, tiles, out):
    out[: lay.own_rows] = -diag[...]
    out[lay.own_rows :] = jnp.zeros((lay.rows - lay.own_rows,) + diag.shape[1:], F32)

    @pl.loop(0, lay.slots)
    def _(s):
        @pl.when(lay.is_local(mine, s, 1))
        def _():
            v = lay.link(mine, s)
            q = matmul(inverse[lay.place(v // lay.width, me[0])], tiles[v])
            out[lay.place(s // lay.width, me[0])] += matmul(tiles[s], q)


def local_pivot_kernel(
    lay, near, inverse, diag, tiles, mate_tiles, out, mate_lower, lower_local, upper, mate_upper, places
):
    me, mine, mates = near.at[0], near.at[1], near.at[2]
    local_terms(lay, me, mine, inverse, diag, tiles, out)
    listed_tiles(lay, mates, 1, mate_tiles, mate_lower)
    listed_tiles(lay, mates, 2, mate_tiles, mate_upper)
    listed_tiles(lay, mine, 2, tiles, upper)
    for side, target, start in ((1, lower_local, 0), (2, upper, 2 * lay.cap)):
        count = lay.scan(mine, side, places)
        for i in range(lay.pairs):
            live = i < count
            target[start + i] = jnp.where(live, tiles[jnp.where(live, places[i], 0)], 0.0)


def next_local_pivot_kernel(lay, near, inverse, diag, tiles, out):
    local_terms(lay, near.at[0], near.at[1], inverse, diag, tiles, out)


def incoming_kernel(lay, near_source, local, lower, mate_lower, arrived, keep, give, total, halves, near, done):
    fetch = pltpu.make_async_copy(near_source, near, done)
    fetch.start()
    total[...] = local[...]
    for k in range(2 * lay.cap):
        halves[k] = beside(arrived[k])
    fetch.wait()
    me, mine, mates = near.at[0], near.at[1], near.at[2]
    role = me[0] % 2
    places, terms = [], []
    for g, (meta, source) in enumerate(((mine, lower), (mates, mate_lower))):
        for j in range(lay.cap):
            s, _, v = lay.lookup(meta, 2 + role, 1, j)
            places.append(lay.place(s // lay.width, me[0]))
            terms.append(matmul_beside(beside(source[role * lay.cap + j]), halves[g * lay.cap + v]))
    for place, term in zip(places, terms):
        total[place] += term
    half = keep.shape[0]
    keep[...] = total[:half]
    give[...] = total[half:]


def newton_kernel(inverse, sums, out):
    for i in range(out.shape[0]):
        x = inverse[i]
        xh, xl = split(x)
        product = matmul_parts(xh, xl, *split(sums[i]))
        out[i] = 2.0 * x + matmul_parts(*split(product), xh, xl)


def table_kernel(lay, me, metas, peers_below, peers_above, out, *refs):
    masks, places = refs[:4], refs[4]
    role = 1 - me[0] % 2
    out[2 * lay.table] = me[0]
    row = lax.broadcasted_iota(jnp.int32, masks[0].shape[1:], 0)
    for side in (1, 2):
        start = (side - 1) * lay.table
        base, peers = ((2, peers_below), (0, peers_above))[side - 1]
        for q in range(lay.n_tile):
            a, meta, peer = q ^ me[0], metas.at[q], peers.at[q]
            for j in range(lay.cap):
                s, _, v = lay.lookup(meta, base + role, side, j)
                out[start + a * lay.cap + j] = s // lay.width
                source = lay.listed(peer, 2 - base + role, v) // lay.width
                masks[2 * side - 2][a * lay.cap + j] = (row == s // lay.width).astype(F32)
                masks[2 * side - 1][a * lay.cap + j] = (row == source).astype(F32)
        for q in range(0, lay.n_tile, 2):
            meta = metas.at[q]
            begin = start + lay.listed_slots + ((q ^ me[0]) >> 1) * lay.pairs
            count = lay.scan(meta, side, places)
            for i in range(lay.pairs):
                s = jnp.where(i < count, places[i], 0)
                out[begin + i] = s // lay.width
                v = jnp.where(i < count, lay.link(meta, s), 0)
                out[begin + lay.local_slots + i] = v // lay.width


def scaled_kernel(lay, side, table, inverse, *refs):
    sources, (listed, local) = refs[:-2], refs[-2:]
    me = table[2 * lay.table]
    role = 1 - me % 2
    start = (side - 1) * lay.table

    def scaled(row, tile):
        return widen(matmul(inverse[lay.place(row, me)], tile))

    at = 0
    for q in range(lay.n_tile):
        lists = sources[at]
        for j in range(lay.cap):
            k = (q ^ me) * lay.cap + j
            listed[k] = scaled(table[start + k], lists[role * lay.cap + j])
        at += 1
        if q % 2 == 0:
            pairs, first = (lists, 2 * lay.cap) if side == 2 else (sources[at], 0)
            at += side == 1
            for i in range(lay.pairs):
                k = ((q ^ me) >> 1) * lay.pairs + i
                local[k] = scaled(table[start + lay.listed_slots + k], pairs[first + i])


def first_kernel(lay, me, base, inverse, out):
    count = out.shape[1]
    mine = pl.ds(pl.multiple_of((me[0] >> 1) * count, count), count)
    for r in range(lay.rows):
        out[r] = times_tile(base[r, mine], widen(inverse[lay.place(r, me[0])]))


def local_sum_kernel(lay, side, table, x, tiles, out):
    start = (side - 1) * lay.table + lay.listed_slots
    terms = [times_tile(x[table[start + lay.local_slots + k]], tiles[k]) for k in range(lay.local_slots)]
    out[...] = jnp.zeros_like(out)
    for k, value in enumerate(terms):
        out[table[start + k]] += value


def listed_sum_kernel(lay, tiles, picks, sources, local, arrived, out):
    rows = [arrived[r] for r in range(lay.rows)]
    terms = []
    for k in range(lay.listed_slots):
        x = sum(sources[k, r : r + 1] * rows[r] for r in range(lay.rows))
        terms.append(times_tile(x, tiles[k]))
    for r in range(lay.rows):
        out[r] = local[r] + sum(picks[k, r : r + 1] * terms[k] for k in range(lay.listed_slots))


def local(krylov_block, diag_block, inverse_prev, coupling_tiles, slot_kind, slot_link, send_slots):
    rows, width, n, _ = coupling_tiles.shape
    cap = send_slots.shape[3]
    n_dom, n_tile = lax.axis_size("dom"), lax.axis_size("tile")
    lay = Layout(rows, width, cap, n_tile)
    vectors = krylov_block.shape[1]
    upper_bits = [1 << b for b in range(1, n_tile.bit_length() - 1)]

    me = lax.axis_index("tile").astype(jnp.int32).reshape(1)
    mine = jnp.concatenate([slot_kind.reshape(-1), slot_link.reshape(-1), send_slots.reshape(-1)])
    tiles = coupling_tiles.reshape(lay.slots, n, n)

    def swap(x, bit):
        return lax.ppermute(x, "tile", [(i, i ^ bit) for i in range(n_tile)])

    def along(x, sign, swapped=0):
        route = []
        for d in range(n_dom):
            for t in range(n_tile):
                to = d + sign * (1 + (t + swapped) % 2)
                if 0 <= to < n_dom:
                    route.append((d * n_tile + t, to * n_tile + t))
        return lax.ppermute(x, ("dom", "tile"), route)

    def summed(x):
        for bit in upper_bits:
            got = swap(x, bit)
            near = bit // 2
            got = got.reshape((n_tile // 2 // (2 * near), 2, near * lay.own_rows) + x.shape[1:])
            x = x + jnp.concatenate([got[:, 1:], got[:, :1]], 1).reshape(x.shape)
        return x

    def shape(*dims, dtype=F32):
        return jax.ShapeDtypeStruct(dims, dtype)

    kernel = lambda body, *bound: functools.partial(body, lay, *bound)
    product = 8 * n**3

    def over_chips(x):
        held = [x]
        for bit in upper_bits:
            held += [swap(one, bit) for one in held]
        return held

    mate_tiles = swap(tiles, 1)
    arriving = over_chips(inverse_prev)
    mates = swap(mine, 1)
    given = swap(inverse_prev, 1)
    arriving, mine, mates, given = lax.optimization_barrier((arriving, mine, mates, given))
    near = jnp.stack([jnp.broadcast_to(me, mine.shape), mine, mates])
    kept = jnp.concatenate(arriving, 0)
    mated = jnp.concatenate([given] + [swap(x, 1) for x in arriving[1:]], 0)
    half = rows // 2
    lists, local_list = shape(2 * cap, n, n), shape(lay.pairs, n, n)
    places = pltpu.SMEM((lay.slots + 1,), jnp.int32)
    fetching = (pltpu.SMEM(near.shape, jnp.int32), pltpu.SemaphoreType.DMA)
    split_rows, whole_rows = pltpu.VMEM((rows, n, 2 * n), BF16), pltpu.VMEM((rows, n, n), F32)
    for sweep in range(FSWEEPS):
        inverse = jnp.concatenate([kept, mated], 0)
        early, later = [], []
        if sweep == 0:
            out, lower = call(
                kernel(outgoing_kernel),
                [lists] * 2,
                (),
                (inverse, tiles, mate_tiles),
                scratch=(split_rows, *fetching),
                fetched=(near,),
            )
            arrived = along(out, 1)
            lowers = over_chips(lower)
            here, mate_lower, lower_local, upper, mate_upper = call(
                kernel(local_pivot_kernel),
                [shape(rows, n, n), lists, local_list, shape(2 * cap + lay.pairs, n, n), lists],
                (near,),
                (inverse, diag_block, tiles, mate_tiles),
                flops=product * rows,
                scratch=(places,),
            )
            early += lowers[1:]
            metas = jnp.concatenate(over_chips(near[1:]), 0)
            later += [metas]
        else:
            (out,) = call(
                kernel(next_outgoing_kernel),
                [lists],
                (),
                (inverse, upper, mate_upper),
                scratch=(split_rows, *fetching),
                fetched=(near,),
            )
            arrived = along(out, 1)
            (here,) = call(
                kernel(next_local_pivot_kernel),
                [shape(rows, n, n)],
                (near,),
                (inverse, diag_block, tiles),
                flops=product * rows,
            )
        if sweep == FSWEEPS - 1:
            lower_locals = over_chips(lower_local)
            mate_lowers = [mate_lower] + [swap(x, 1) for x in lowers[1:]]
            below, above = along(metas, 1, 1), along(metas, -1, 1)
            mask = shape(lay.listed_slots, rows, n)
            table, *masks = call(
                kernel(table_kernel),
                [shape(2 * lay.table + 1, dtype=jnp.int32)] + [mask] * 4,
                (me, metas, below, above),
                (),
                scratch=(places,),
                to_smem=1,
            )
            early += [*lower_locals[1:], *mate_lowers[1:], below, above]
            later += [table]
        keep, give = call(
            kernel(incoming_kernel),
            [shape(half, n, n)] * 2,
            (),
            (here, lower, mate_lower, arrived),
            scratch=(whole_rows, pltpu.VMEM((2 * cap, n, 2 * n), BF16), *fetching),
            fetched=(near,),
            early=early,
        )
        sums = summed(keep + swap(give, 1))
        (kept,) = call(newton_kernel, [shape(half, n, n)], (), (kept, sums), early=later)
        mated = swap(kept, 1)
    inverse = jnp.concatenate([kept, mated], 0)

    def scale(side, sources):
        return call(
            kernel(scaled_kernel, side),
            [
                shape(lay.listed_slots, 2 * n, n, dtype=BF16),
                shape(lay.local_slots, 2 * n, n, dtype=BF16),
            ],
            (table,),
            (inverse, *sources),
            flops=product * 24,
        )

    share = vectors // (n_tile // 2)
    block = shape(rows, share, n)
    (first,) = call(kernel(first_kernel), [block], (me,), (krylov_block, inverse))

    def sweeps(x, side, count, listed, local, early=()):
        base = x
        for sweep in range(count):
            arrived = along(x, 1 if side == 1 else -1, 1)
            (here,) = call(
                kernel(local_sum_kernel, side), [block], (table,), (x, local), flops=8 * n**2 * vectors * rows
            )
            (part,) = call(
                kernel(listed_sum_kernel),
                [block],
                (),
                (listed, *masks[2 * side - 2 : 2 * side], here, arrived),
                early=early if sweep == count - 1 else (),
            )
            x = base - (part + swap(part, 1))
        return x

    uppers = over_chips(upper)
    mate_uppers = [mate_upper] + [swap(x, 1) for x in uppers[1:]]
    low = [x for three in zip(lowers, lower_locals, mate_lowers) for x in three]
    up = [x for pair in zip(uppers, mate_uppers) for x in pair]
    solved = sweeps(first, 1, LSWEEPS, *scale(1, low), early=uppers[1:])
    solved = sweeps(solved, 2, USWEEPS, *scale(2, up))
    for bit in upper_bits:
        got = swap(solved, bit)
        solved = jnp.where(
            (me[0] & bit) == 0, jnp.concatenate([solved, got], 1), jnp.concatenate([got, solved], 1)
        )
    return (kept[: lay.own_rows], solved)


def solution(mesh):
    placed = (
        P("dom", None, None),
        P(("dom", "tile"), None, None),
        P(("dom", "tile"), None, None),
        P("dom", "tile", None, None),
        P("dom", "tile"),
        P("dom", "tile"),
        P("dom", "tile", None, None),
    )
    return jax.shard_map(
        local,
        mesh=mesh,
        in_specs=placed,
        out_specs=(P(("dom", "tile"), None, None), P("dom", None, None)),
        check_vma=False,
    )
```

```python
import functools

import jax
import jax.numpy as jnp
from jax import lax
from jax.experimental import pallas as pl
from jax.experimental.pallas import tpu as pltpu
from jax.sharding import PartitionSpec as P

FSWEEPS = 2
LSWEEPS = 3
USWEEPS = 3
F32 = jnp.float32
BF16 = jnp.bfloat16


def split(a):
    hi = a.astype(BF16)
    return hi, (a - hi.astype(F32)).astype(BF16)


def beside(a):
    return jnp.concatenate(split(a), 1)


def matmul_beside(lhs, pair):
    out = jnp.dot(lhs, jnp.concatenate([pair, pair], 0), preferred_element_type=F32)
    n = pair.shape[1] // 2
    return out[:, :n] + out[:, n:]


def matmul_parts(ah, al, bh, bl):
    return matmul_beside(jnp.concatenate([ah, al], 1), jnp.concatenate([bh, bl], 1))


def matmul(a, b):
    return matmul_parts(*split(a), *split(b))


def times_tile(x, wide):
    v, n = x.shape
    stacked = jnp.concatenate(split(x), 0)
    out = lax.dot_general(stacked, wide, (((1,), (1,)), ((), ())), preferred_element_type=F32)
    return out[:v, :n] + (out[v:, :n] + out[:v, n:])


def widen(a):
    return jnp.concatenate(split(a), 0)


class Layout:
    def __init__(self, rows, width, cap, n_tile):
        self.rows, self.width, self.cap, self.n_tile = rows, width, cap, n_tile
        self.slots = rows * width
        self.own_rows = rows // n_tile
        self.pairs = max(1, (self.slots - 4 * cap) // 2)
        self.listed_slots = n_tile * cap
        self.local_slots = n_tile // 2 * self.pairs
        self.table = self.listed_slots + 2 * self.local_slots

    def kind(self, meta, s):
        return meta[s]

    def link(self, meta, s):
        return meta[self.slots + s]

    def listed(self, meta, which, j):
        return meta[2 * self.slots + which * self.cap + j]

    def place(self, r, me):
        far = (r // self.own_rows) ^ me
        return ((far & 1) * (self.n_tile // 2) + (far >> 1)) * self.own_rows + r % self.own_rows

    def lookup(self, meta, which, side, j):
        s = self.listed(meta, which, j)
        v = self.link(meta, s) - self.slots - (which % 2) * self.cap
        live = (self.kind(meta, s) == side) & (v >= 0) & (v < self.cap)
        return s, live, jnp.clip(v, 0, self.cap - 1)

    def is_local(self, meta, s, side):
        return (self.kind(meta, s) == side) & (self.link(meta, s) < self.slots)

    def scan(self, meta, side, places):
        count = jnp.int32(0)
        for s in range(self.slots):
            places[count] = s
            count = count + self.is_local(meta, s, side).astype(jnp.int32)
        return count


def smem():
    return pl.BlockSpec(memory_space=pltpu.SMEM)


def vmem():
    return pl.BlockSpec(memory_space=pltpu.VMEM)


def call(body, outs, scalars, arrays, flops=0, scratch=(), early=(), to_smem=0, fetched=()):
    moved = sum(a.size * a.dtype.itemsize for a in arrays) + sum(o.size * o.dtype.itemsize for o in outs)
    return pl.pallas_call(
        body if not early else lambda *refs: body(*refs[len(early) :]),
        out_shape=outs,
        in_specs=[pl.BlockSpec(memory_space=pl.ANY)] * (len(early) + len(fetched)) + [smem()] * len(scalars) + [vmem()] * len(arrays),
        out_specs=[smem()] * to_smem + [vmem()] * (len(outs) - to_smem),
        scratch_shapes=list(scratch),
        compiler_params=pltpu.CompilerParams(vmem_limit_bytes=8 << 20),
        cost_estimate=pl.CostEstimate(flops=flops, bytes_accessed=moved, transcendentals=0),
    )(*early, *fetched, *scalars, *arrays)


def listed_tiles(lay, meta, side, tiles, out):
    for which in range(2):
        for j in range(lay.cap):
            s, live, _ = lay.lookup(meta, 4 - 2 * side + which, side, j)
            out[which * lay.cap + j] = jnp.where(live, tiles[s], 0.0)


def outgoing_products(lay, inverse, near_source, near, done, halves, tile_of, out):
    fetch = pltpu.make_async_copy(near_source, near, done)
    fetch.start()
    for r in range(lay.rows):
        halves[r] = beside(inverse[r])
    fetch.wait()
    me, metas = near.at[0], (near.at[1], near.at[2])
    for g, meta in enumerate(metas):
        for j in range(lay.cap):
            s, live, _ = lay.lookup(meta, me[0] % 2, 2, j)
            tile = tile_of(g, me[0] % 2 * lay.cap + j, s, live)
            out[g * lay.cap + j] = matmul_beside(halves[lay.place(s // lay.width, me[0])], beside(tile))


def outgoing_kernel(lay, near_source, inverse, tiles, mate_tiles, out, lower, halves, near, done):
    held = (tiles, mate_tiles)
    outgoing_products(
        lay, inverse, near_source, near, done, halves, lambda g, k, s, live: jnp.where(live, held[g][s], 0.0), out
    )
    listed_tiles(lay, near.at[1], 1, tiles, lower)


def next_outgoing_kernel(lay, near_source, inverse, upper, mate_upper, out, halves, near, done):
    held = (upper, mate_upper)
    outgoing_products(lay, inverse, near_source, near, done, halves, lambda g, k, s, live: held[g][k], out)


def local_terms(lay, me, mine, inverse, diag, tiles, out):
    out[: lay.own_rows] = -diag[...]
    out[lay.own_rows :] = jnp.zeros((lay.rows - lay.own_rows,) + diag.shape[1:], F32)

    @pl.loop(0, lay.slots)
    def _(s):
        @pl.when(lay.is_local(mine, s, 1))
        def _():
            v = lay.link(mine, s)
            q = matmul(inverse[lay.place(v // lay.width, me[0])], tiles[v])
            out[lay.place(s // lay.width, me[0])] += matmul(tiles[s], q)


def local_pivot_kernel(
    lay, near, inverse, diag, tiles, mate_tiles, out, mate_lower, lower_local, upper, mate_upper, places
):
    me, mine, mates = near.at[0], near.at[1], near.at[2]
    local_terms(lay, me, mine, inverse, diag, tiles, out)
    listed_tiles(lay, mates, 1, mate_tiles, mate_lower)
    listed_tiles(lay, mates, 2, mate_tiles, mate_upper)
    listed_tiles(lay, mine, 2, tiles, upper)
    for side, target, start in ((1, lower_local, 0), (2, upper, 2 * lay.cap)):
        count = lay.scan(mine, side, places)
        for i in range(lay.pairs):
            live = i < count
            target[start + i] = jnp.where(live, tiles[jnp.where(live, places[i], 0)], 0.0)


def next_local_pivot_kernel(lay, near, inverse, diag, tiles, out):
    local_terms(lay, near.at[0], near.at[1], inverse, diag, tiles, out)


def incoming_kernel(lay, near_source, local, lower, mate_lower, arrived, keep, give, total, halves, near, done):
    fetch = pltpu.make_async_copy(near_source, near, done)
    fetch.start()
    total[...] = local[...]
    for k in range(2 * lay.cap):
        halves[k] = beside(arrived[k])
    fetch.wait()
    me, mine, mates = near.at[0], near.at[1], near.at[2]
    role = me[0] % 2
    places, terms = [], []
    for g, (meta, source) in enumerate(((mine, lower), (mates, mate_lower))):
        for j in range(lay.cap):
            s, _, v = lay.lookup(meta, 2 + role, 1, j)
            places.append(lay.place(s // lay.width, me[0]))
            terms.append(matmul_beside(beside(source[role * lay.cap + j]), halves[g * lay.cap + v]))
    for place, term in zip(places, terms):
        total[place] += term
    half = keep.shape[0]
    keep[...] = total[:half]
    give[...] = total[half:]


def newton_kernel(inverse, sums, out):
    for i in range(out.shape[0]):
        x = inverse[i]
        xh, xl = split(x)
        product = matmul_parts(xh, xl, *split(sums[i]))
        out[i] = 2.0 * x + matmul_parts(*split(product), xh, xl)


def vector_role(side, me):
    return (me + side) % 2


def table_kernel(lay, me, metas, peers_below, peers_above, out, *refs):
    masks, places = refs[:4], refs[4]
    out[2 * lay.table] = me[0]
    row = lax.broadcasted_iota(jnp.int32, masks[0].shape[1:], 0)
    for side in (1, 2):
        role = vector_role(side, me[0])
        start = (side - 1) * lay.table
        base, peers = ((2, peers_below), (0, peers_above))[side - 1]
        for q in range(lay.n_tile):
            a, meta, peer = q ^ me[0], metas.at[q], peers.at[q]
            for j in range(lay.cap):
                s, _, v = lay.lookup(meta, base + role, side, j)
                out[start + a * lay.cap + j] = s // lay.width
                source = lay.listed(peer, 2 - base + role, v) // lay.width
                masks[2 * side - 2][a * lay.cap + j] = (row == s // lay.width).astype(F32)
                masks[2 * side - 1][a * lay.cap + j] = (row == source).astype(F32)
        for q in range(0, lay.n_tile, 2):
            meta = metas.at[q]
            begin = start + lay.listed_slots + ((q ^ me[0]) >> 1) * lay.pairs
            count = lay.scan(meta, side, places)
            for i in range(lay.pairs):
                s = jnp.where(i < count, places[i], 0)
                out[begin + i] = s // lay.width
                v = jnp.where(i < count, lay.link(meta, s), 0)
                out[begin + lay.local_slots + i] = v // lay.width


def scaled_kernel(lay, side, table, inverse, *refs):
    sources, (listed, local) = refs[:-2], refs[-2:]
    me = table[2 * lay.table]
    role = vector_role(side, me)
    start = (side - 1) * lay.table

    def scaled(row, tile):
        return widen(matmul(inverse[lay.place(row, me)], tile))

    at = 0
    for q in range(lay.n_tile):
        lists = sources[at]
        for j in range(lay.cap):
            k = (q ^ me) * lay.cap + j
            listed[k] = scaled(table[start + k], lists[role * lay.cap + j])
        at += 1
        if q % 2 == 0:
            pairs, first = (lists, 2 * lay.cap) if side == 2 else (sources[at], 0)
            at += side == 1
            for i in range(lay.pairs):
                k = ((q ^ me) >> 1) * lay.pairs + i
                local[k] = scaled(table[start + lay.listed_slots + k], pairs[first + i])


def first_kernel(lay, me, base, inverse, out):
    count = out.shape[1]
    mine = pl.ds(pl.multiple_of((me[0] >> 1) * count, count), count)
    for r in range(lay.rows):
        out[r] = times_tile(base[r, mine], widen(inverse[lay.place(r, me[0])]))


def local_sum_kernel(lay, side, table, x, tiles, out):
    start = (side - 1) * lay.table + lay.listed_slots
    terms = [times_tile(x[table[start + lay.local_slots + k]], tiles[k]) for k in range(lay.local_slots)]
    out[...] = jnp.zeros_like(out)
    for k, value in enumerate(terms):
        out[table[start + k]] += value


def listed_sum_kernel(lay, tiles, picks, sources, local, arrived, out):
    rows = [arrived[r] for r in range(lay.rows)]
    terms = []
    for k in range(lay.listed_slots):
        x = sum(sources[k, r : r + 1] * rows[r] for r in range(lay.rows))
        terms.append(times_tile(x, tiles[k]))
    for r in range(lay.rows):
        out[r] = local[r] + sum(picks[k, r : r + 1] * terms[k] for k in range(lay.listed_slots))


def local(krylov_block, diag_block, inverse_prev, coupling_tiles, slot_kind, slot_link, send_slots):
    rows, width, n, _ = coupling_tiles.shape
    cap = send_slots.shape[3]
    n_dom, n_tile = lax.axis_size("dom"), lax.axis_size("tile")
    lay = Layout(rows, width, cap, n_tile)
    vectors = krylov_block.shape[1]
    upper_bits = [1 << b for b in range(1, n_tile.bit_length() - 1)]

    me = lax.axis_index("tile").astype(jnp.int32).reshape(1)
    mine = jnp.concatenate([slot_kind.reshape(-1), slot_link.reshape(-1), send_slots.reshape(-1)])
    tiles = coupling_tiles.reshape(lay.slots, n, n)

    def swap(x, bit):
        return lax.ppermute(x, "tile", [(i, i ^ bit) for i in range(n_tile)])

    def along(x, sign, swapped=0):
        route = []
        for d in range(n_dom):
            for t in range(n_tile):
                to = d + sign * (1 + (t + swapped) % 2)
                if 0 <= to < n_dom:
                    route.append((d * n_tile + t, to * n_tile + t))
        return lax.ppermute(x, ("dom", "tile"), route)

    def summed(x):
        for bit in upper_bits:
            got = swap(x, bit)
            near = bit // 2
            got = got.reshape((n_tile // 2 // (2 * near), 2, near * lay.own_rows) + x.shape[1:])
            x = x + jnp.concatenate([got[:, 1:], got[:, :1]], 1).reshape(x.shape)
        return x

    def shape(*dims, dtype=F32):
        return jax.ShapeDtypeStruct(dims, dtype)

    kernel = lambda body, *bound: functools.partial(body, lay, *bound)
    product = 8 * n**3

    def over_chips(x):
        held = [x]
        for bit in upper_bits:
            held += [swap(one, bit) for one in held]
        return held

    mate_tiles = swap(tiles, 1)
    arriving = over_chips(inverse_prev)
    mates = swap(mine, 1)
    given = swap(inverse_prev, 1)
    arriving, mine, mates, given = lax.optimization_barrier((arriving, mine, mates, given))
    near = jnp.stack([jnp.broadcast_to(me, mine.shape), mine, mates])
    kept = jnp.concatenate(arriving, 0)
    mated = jnp.concatenate([given] + [swap(x, 1) for x in arriving[1:]], 0)
    half = rows // 2
    lists, local_list = shape(2 * cap, n, n), shape(lay.pairs, n, n)
    places = pltpu.SMEM((lay.slots + 1,), jnp.int32)
    fetching = (pltpu.SMEM(near.shape, jnp.int32), pltpu.SemaphoreType.DMA)
    split_rows, whole_rows = pltpu.VMEM((rows, n, 2 * n), BF16), pltpu.VMEM((rows, n, n), F32)
    for sweep in range(FSWEEPS):
        inverse = jnp.concatenate([kept, mated], 0)
        early, later = [], []
        if sweep == 0:
            out, lower = call(
                kernel(outgoing_kernel),
                [lists] * 2,
                (),
                (inverse, tiles, mate_tiles),
                scratch=(split_rows, *fetching),
                fetched=(near,),
            )
            arrived = along(out, 1)
            lowers = over_chips(lower)
            here, mate_lower, lower_local, upper, mate_upper = call(
                kernel(local_pivot_kernel),
                [shape(rows, n, n), lists, local_list, shape(2 * cap + lay.pairs, n, n), lists],
                (near,),
                (inverse, diag_block, tiles, mate_tiles),
                flops=product * rows,
                scratch=(places,),
            )
            early += lowers[1:]
            metas = jnp.concatenate(over_chips(near[1:]), 0)
            later += [metas]
        else:
            (out,) = call(
                kernel(next_outgoing_kernel),
                [lists],
                (),
                (inverse, upper, mate_upper),
                scratch=(split_rows, *fetching),
                fetched=(near,),
            )
            arrived = along(out, 1)
            (here,) = call(
                kernel(next_local_pivot_kernel),
                [shape(rows, n, n)],
                (near,),
                (inverse, diag_block, tiles),
                flops=product * rows,
            )
        if sweep == FSWEEPS - 1:
            lower_locals = over_chips(lower_local)
            mate_lowers = [mate_lower] + [swap(x, 1) for x in lowers[1:]]
            below, above = along(metas, 1, 1), along(metas, -1)
            mask = shape(lay.listed_slots, rows, n)
            table, *masks = call(
                kernel(table_kernel),
                [shape(2 * lay.table + 1, dtype=jnp.int32)] + [mask] * 4,
                (me, metas, below, above),
                (),
                scratch=(places,),
                to_smem=1,
            )
            early += [*lower_locals[1:], *mate_lowers[1:], below, above]
            later += [table]
        keep, give = call(
            kernel(incoming_kernel),
            [shape(half, n, n)] * 2,
            (),
            (here, lower, mate_lower, arrived),
            scratch=(whole_rows, pltpu.VMEM((2 * cap, n, 2 * n), BF16), *fetching),
            fetched=(near,),
            early=early,
        )
        sums = summed(keep + swap(give, 1))
        (kept,) = call(newton_kernel, [shape(half, n, n)], (), (kept, sums), early=later)
        mated = swap(kept, 1)
    inverse = jnp.concatenate([kept, mated], 0)

    def scale(side, sources):
        return call(
            kernel(scaled_kernel, side),
            [
                shape(lay.listed_slots, 2 * n, n, dtype=BF16),
                shape(lay.local_slots, 2 * n, n, dtype=BF16),
            ],
            (table,),
            (inverse, *sources),
            flops=product * 24,
        )

    share = vectors // (n_tile // 2)
    block = shape(rows, share, n)
    (first,) = call(kernel(first_kernel), [block], (me,), (krylov_block, inverse))

    def sweeps(x, side, count, listed, local, early=()):
        base = x
        for sweep in range(count):
            arrived = along(x, 1, 1) if side == 1 else along(x, -1)
            (here,) = call(
                kernel(local_sum_kernel, side), [block], (table,), (x, local), flops=8 * n**2 * vectors * rows
            )
            (part,) = call(
                kernel(listed_sum_kernel),
                [block],
                (),
                (listed, *masks[2 * side - 2 : 2 * side], here, arrived),
                early=early if sweep == count - 1 else (),
            )
            x = base - (part + swap(part, 1))
        return x

    uppers = over_chips(upper)
    mate_uppers = [mate_upper] + [swap(x, 1) for x in uppers[1:]]
    low = [x for three in zip(lowers, lower_locals, mate_lowers) for x in three]
    up = [x for pair in zip(uppers, mate_uppers) for x in pair]
    solved = sweeps(first, 1, LSWEEPS, *scale(1, low), early=uppers[1:])
    solved = sweeps(solved, 2, USWEEPS, *scale(2, up))
    for bit in upper_bits:
        got = swap(solved, bit)
        solved = jnp.where(
            (me[0] & bit) == 0, jnp.concatenate([solved, got], 1), jnp.concatenate([got, solved], 1)
        )
    return (kept[: lay.own_rows], solved)


def solution(mesh):
    placed = (
        P("dom", None, None),
        P(("dom", "tile"), None, None),
        P(("dom", "tile"), None, None),
        P("dom", "tile", None, None),
        P("dom", "tile"),
        P("dom", "tile"),
        P("dom", "tile", None, None),
    )
    return jax.shard_map(
        local,
        mesh=mesh,
        in_specs=placed,
        out_specs=(P(("dom", "tile"), None, None), P("dom", None, None)),
        check_vma=False,
    )
```

```python
import functools

import jax
import jax.numpy as jnp
from jax import lax
from jax.experimental import pallas as pl
from jax.experimental.pallas import tpu as pltpu
from jax.sharding import PartitionSpec as P

FSWEEPS = 2
LSWEEPS = 3
USWEEPS = 3
F32 = jnp.float32
BF16 = jnp.bfloat16


def split(a):
    hi = a.astype(BF16)
    return hi, (a - hi.astype(F32)).astype(BF16)


def beside(a):
    return jnp.concatenate(split(a), 1)


def matmul_beside(lhs, pair):
    out = jnp.dot(lhs, jnp.concatenate([pair, pair], 0), preferred_element_type=F32)
    n = pair.shape[1] // 2
    return out[:, :n] + out[:, n:]


def matmul_parts(ah, al, bh, bl):
    return matmul_beside(jnp.concatenate([ah, al], 1), jnp.concatenate([bh, bl], 1))


def matmul(a, b):
    return matmul_parts(*split(a), *split(b))


def times_tile(x, wide):
    v, n = x.shape
    stacked = jnp.concatenate(split(x), 0)
    out = lax.dot_general(stacked, wide, (((1,), (1,)), ((), ())), preferred_element_type=F32)
    return out[:v, :n] + (out[v:, :n] + out[:v, n:])


def widen(a):
    return jnp.concatenate(split(a), 0)


class Layout:
    def __init__(self, rows, width, cap, n_tile):
        self.rows, self.width, self.cap, self.n_tile = rows, width, cap, n_tile
        self.slots = rows * width
        self.own_rows = rows // n_tile
        self.pairs = max(1, (self.slots - 4 * cap) // 2)
        self.listed_slots = n_tile * cap
        self.local_slots = n_tile // 2 * self.pairs
        self.table = self.listed_slots + 2 * self.local_slots

    def kind(self, meta, s):
        return meta[s]

    def link(self, meta, s):
        return meta[self.slots + s]

    def listed(self, meta, which, j):
        return meta[2 * self.slots + which * self.cap + j]

    def place(self, r, me):
        far = (r // self.own_rows) ^ me
        return ((far & 1) * (self.n_tile // 2) + (far >> 1)) * self.own_rows + r % self.own_rows

    def lookup(self, meta, which, side, j):
        s = self.listed(meta, which, j)
        v = self.link(meta, s) - self.slots - (which % 2) * self.cap
        live = (self.kind(meta, s) == side) & (v >= 0) & (v < self.cap)
        return s, live, jnp.clip(v, 0, self.cap - 1)

    def is_local(self, meta, s, side):
        return (self.kind(meta, s) == side) & (self.link(meta, s) < self.slots)

    def scan(self, meta, side, places):
        count = jnp.int32(0)
        for s in range(self.slots):
            places[count] = s
            count = count + self.is_local(meta, s, side).astype(jnp.int32)
        return count


def smem():
    return pl.BlockSpec(memory_space=pltpu.SMEM)


def vmem():
    return pl.BlockSpec(memory_space=pltpu.VMEM)


def call(body, outs, scalars, arrays, flops=0, scratch=(), early=(), to_smem=0, fetched=()):
    moved = sum(a.size * a.dtype.itemsize for a in arrays) + sum(o.size * o.dtype.itemsize for o in outs)
    return pl.pallas_call(
        body if not early else lambda *refs: body(*refs[len(early) :]),
        out_shape=outs,
        in_specs=[pl.BlockSpec(memory_space=pl.ANY)] * (len(early) + len(fetched)) + [smem()] * len(scalars) + [vmem()] * len(arrays),
        out_specs=[smem()] * to_smem + [vmem()] * (len(outs) - to_smem),
        scratch_shapes=list(scratch),
        compiler_params=pltpu.CompilerParams(vmem_limit_bytes=8 << 20),
        cost_estimate=pl.CostEstimate(flops=flops, bytes_accessed=moved, transcendentals=0),
    )(*early, *fetched, *scalars, *arrays)


def listed_tiles(lay, meta, side, tiles, out):
    for which in range(2):
        for j in range(lay.cap):
            s, live, _ = lay.lookup(meta, 4 - 2 * side + which, side, j)
            out[which * lay.cap + j] = jnp.where(live, tiles[s], 0.0)


def outgoing_products(lay, inverse, near_source, near, done, halves, tile_of, out):
    fetch = pltpu.make_async_copy(near_source, near, done)
    fetch.start()
    for r in range(lay.rows):
        halves[r] = beside(inverse[r])
    fetch.wait()
    me, metas = near.at[0], (near.at[1], near.at[2])
    for g, meta in enumerate(metas):
        for j in range(lay.cap):
            s, live, _ = lay.lookup(meta, me[0] % 2, 2, j)
            tile = tile_of(g, me[0] % 2 * lay.cap + j, s, live)
            out[g * lay.cap + j] = matmul_beside(halves[lay.place(s // lay.width, me[0])], beside(tile))


def outgoing_kernel(lay, near_source, inverse, tiles, mate_tiles, out, lower, halves, near, done):
    held = (tiles, mate_tiles)
    outgoing_products(
        lay, inverse, near_source, near, done, halves, lambda g, k, s, live: jnp.where(live, held[g][s], 0.0), out
    )
    listed_tiles(lay, near.at[1], 1, tiles, lower)


def next_outgoing_kernel(lay, near_source, inverse, upper, mate_upper, out, halves, near, done):
    held = (upper, mate_upper)
    outgoing_products(lay, inverse, near_source, near, done, halves, lambda g, k, s, live: held[g][k], out)


def local_terms(lay, me, mine, inverse, diag, tiles, out):
    out[: lay.own_rows] = -diag[...]
    out[lay.own_rows :] = jnp.zeros((lay.rows - lay.own_rows,) + diag.shape[1:], F32)

    @pl.loop(0, lay.slots)
    def _(s):
        @pl.when(lay.is_local(mine, s, 1))
        def _():
            v = lay.link(mine, s)
            q = matmul(inverse[lay.place(v // lay.width, me[0])], tiles[v])
            out[lay.place(s // lay.width, me[0])] += matmul(tiles[s], q)


def local_pivot_kernel(
    lay, near, inverse, diag, tiles, mate_tiles, out, mate_lower, lower_local, upper, mate_upper, places
):
    me, mine, mates = near.at[0], near.at[1], near.at[2]
    local_terms(lay, me, mine, inverse, diag, tiles, out)
    listed_tiles(lay, mates, 1, mate_tiles, mate_lower)
    listed_tiles(lay, mates, 2, mate_tiles, mate_upper)
    listed_tiles(lay, mine, 2, tiles, upper)
    for side, target, start in ((1, lower_local, 0), (2, upper, 2 * lay.cap)):
        count = lay.scan(mine, side, places)
        for i in range(lay.pairs):
            live = i < count
            target[start + i] = jnp.where(live, tiles[jnp.where(live, places[i], 0)], 0.0)


def next_local_pivot_kernel(lay, near, inverse, diag, tiles, out):
    local_terms(lay, near.at[0], near.at[1], inverse, diag, tiles, out)


def incoming_kernel(lay, near_source, local, lower, mate_lower, arrived, *refs):
    *outs, total, halves, near, done = refs
    fetch = pltpu.make_async_copy(near_source, near, done)
    fetch.start()
    total[...] = local[...]
    for k in range(2 * lay.cap):
        halves[k] = beside(arrived[k])
    fetch.wait()
    me, mine, mates = near.at[0], near.at[1], near.at[2]
    role = me[0] % 2
    places, terms = [], []
    for g, (meta, source) in enumerate(((mine, lower), (mates, mate_lower))):
        for j in range(lay.cap):
            s, _, v = lay.lookup(meta, 2 + role, 1, j)
            places.append(lay.place(s // lay.width, me[0]))
            terms.append(matmul_beside(beside(source[role * lay.cap + j]), halves[g * lay.cap + v]))
    for place, term in zip(places, terms):
        total[place] += term
    for c, out in enumerate(outs):
        out[...] = total[c * lay.own_rows : (c + 1) * lay.own_rows]


def newton_kernel(inverse, sums, out):
    for i in range(out.shape[0]):
        x = inverse[i]
        xh, xl = split(x)
        product = matmul_parts(xh, xl, *split(sums[i]))
        out[i] = 2.0 * x + matmul_parts(*split(product), xh, xl)


def vector_role(side, me):
    return (me + side) % 2


def table_kernel(lay, me, metas, peers_below, peers_above, out, *refs):
    masks, places = refs[:4], refs[4]
    out[2 * lay.table] = me[0]
    row = lax.broadcasted_iota(jnp.int32, masks[0].shape[1:], 0)
    for side in (1, 2):
        role = vector_role(side, me[0])
        start = (side - 1) * lay.table
        base, peers = ((2, peers_below), (0, peers_above))[side - 1]
        for q in range(lay.n_tile):
            a, meta, peer = q ^ me[0], metas.at[q], peers.at[q]
            for j in range(lay.cap):
                s, _, v = lay.lookup(meta, base + role, side, j)
                out[start + a * lay.cap + j] = s // lay.width
                source = lay.listed(peer, 2 - base + role, v) // lay.width
                masks[2 * side - 2][a * lay.cap + j] = (row == s // lay.width).astype(F32)
                masks[2 * side - 1][a * lay.cap + j] = (row == source).astype(F32)
        for q in range(0, lay.n_tile, 2):
            meta = metas.at[q]
            begin = start + lay.listed_slots + ((q ^ me[0]) >> 1) * lay.pairs
            count = lay.scan(meta, side, places)
            for i in range(lay.pairs):
                s = jnp.where(i < count, places[i], 0)
                out[begin + i] = s // lay.width
                v = jnp.where(i < count, lay.link(meta, s), 0)
                out[begin + lay.local_slots + i] = v // lay.width


def scaled_kernel(lay, side, table, inverse, *refs):
    sources, (listed, local) = refs[:-2], refs[-2:]
    me = table[2 * lay.table]
    role = vector_role(side, me)
    start = (side - 1) * lay.table

    def scaled(row, tile):
        return widen(matmul(inverse[lay.place(row, me)], tile))

    at = 0
    for q in range(lay.n_tile):
        lists = sources[at]
        for j in range(lay.cap):
            k = (q ^ me) * lay.cap + j
            listed[k] = scaled(table[start + k], lists[role * lay.cap + j])
        at += 1
        if q % 2 == 0:
            pairs, first = (lists, 2 * lay.cap) if side == 2 else (sources[at], 0)
            at += side == 1
            for i in range(lay.pairs):
                k = ((q ^ me) >> 1) * lay.pairs + i
                local[k] = scaled(table[start + lay.listed_slots + k], pairs[first + i])


def first_kernel(lay, me, base, inverse, out):
    count = out.shape[1]
    mine = pl.ds(pl.multiple_of((me[0] >> 1) * count, count), count)
    for r in range(lay.rows):
        out[r] = times_tile(base[r, mine], widen(inverse[lay.place(r, me[0])]))


def local_sum_kernel(lay, side, table, x, tiles, out):
    start = (side - 1) * lay.table + lay.listed_slots
    terms = [times_tile(x[table[start + lay.local_slots + k]], tiles[k]) for k in range(lay.local_slots)]
    out[...] = jnp.zeros_like(out)
    for k, value in enumerate(terms):
        out[table[start + k]] += value


def listed_sum_kernel(lay, tiles, picks, sources, local, arrived, out):
    rows = [arrived[r] for r in range(lay.rows)]
    terms = []
    for k in range(lay.listed_slots):
        x = sum(sources[k, r : r + 1] * rows[r] for r in range(lay.rows))
        terms.append(times_tile(x, tiles[k]))
    for r in range(lay.rows):
        out[r] = local[r] + sum(picks[k, r : r + 1] * terms[k] for k in range(lay.listed_slots))


def local(krylov_block, diag_block, inverse_prev, coupling_tiles, slot_kind, slot_link, send_slots):
    rows, width, n, _ = coupling_tiles.shape
    cap = send_slots.shape[3]
    n_dom, n_tile = lax.axis_size("dom"), lax.axis_size("tile")
    lay = Layout(rows, width, cap, n_tile)
    vectors = krylov_block.shape[1]
    upper_bits = [1 << b for b in range(1, n_tile.bit_length() - 1)]

    me = lax.axis_index("tile").astype(jnp.int32).reshape(1)
    mine = jnp.concatenate([slot_kind.reshape(-1), slot_link.reshape(-1), send_slots.reshape(-1)])
    tiles = coupling_tiles.reshape(lay.slots, n, n)

    def swap(x, bit):
        return lax.ppermute(x, "tile", [(i, i ^ bit) for i in range(n_tile)])

    def along(x, sign, swapped=0):
        route = []
        for d in range(n_dom):
            for t in range(n_tile):
                to = d + sign * (1 + (t + swapped) % 2)
                if 0 <= to < n_dom:
                    route.append((d * n_tile + t, to * n_tile + t))
        return lax.ppermute(x, ("dom", "tile"), route)

    def summed(parts):
        for bit in upper_bits:
            parts = [part + swap(parts[u ^ (bit // 2)], bit) for u, part in enumerate(parts)]
        return parts

    def shape(*dims, dtype=F32):
        return jax.ShapeDtypeStruct(dims, dtype)

    kernel = lambda body, *bound: functools.partial(body, lay, *bound)
    product = 8 * n**3

    def over_chips(x):
        held = [x]
        for bit in upper_bits:
            held += [swap(one, bit) for one in held]
        return held

    mate_tiles = swap(tiles, 1)
    arriving = over_chips(inverse_prev)
    mates = swap(mine, 1)
    given = swap(inverse_prev, 1)
    arriving, mine, mates, given = lax.optimization_barrier((arriving, mine, mates, given))
    near = jnp.stack([jnp.broadcast_to(me, mine.shape), mine, mates])
    kept = arriving
    mated = [given] + [swap(x, 1) for x in arriving[1:]]
    chunk = shape(lay.own_rows, n, n)
    lists, local_list = shape(2 * cap, n, n), shape(lay.pairs, n, n)
    places = pltpu.SMEM((lay.slots + 1,), jnp.int32)
    fetching = (pltpu.SMEM(near.shape, jnp.int32), pltpu.SemaphoreType.DMA)
    split_rows, whole_rows = pltpu.VMEM((rows, n, 2 * n), BF16), pltpu.VMEM((rows, n, n), F32)
    for sweep in range(FSWEEPS):
        inverse = jnp.concatenate(kept + mated, 0)
        early, later = [], []
        if sweep == 0:
            out, lower = call(
                kernel(outgoing_kernel),
                [lists] * 2,
                (),
                (inverse, tiles, mate_tiles),
                scratch=(split_rows, *fetching),
                fetched=(near,),
            )
            arrived = along(out, 1)
            lowers = over_chips(lower)
            here, mate_lower, lower_local, upper, mate_upper = call(
                kernel(local_pivot_kernel),
                [shape(rows, n, n), lists, local_list, shape(2 * cap + lay.pairs, n, n), lists],
                (near,),
                (inverse, diag_block, tiles, mate_tiles),
                flops=product * rows,
                scratch=(places,),
            )
            early += lowers[1:]
            metas = jnp.concatenate(over_chips(near[1:]), 0)
            later += [metas]
        else:
            (out,) = call(
                kernel(next_outgoing_kernel),
                [lists],
                (),
                (inverse, upper, mate_upper),
                scratch=(split_rows, *fetching),
                fetched=(near,),
            )
            arrived = along(out, 1)
            (here,) = call(
                kernel(next_local_pivot_kernel),
                [shape(rows, n, n)],
                (near,),
                (inverse, diag_block, tiles),
                flops=product * rows,
            )
        if sweep == FSWEEPS - 1:
            lower_locals = over_chips(lower_local)
            mate_lowers = [mate_lower] + [swap(x, 1) for x in lowers[1:]]
            below, above = along(metas, 1, 1), along(metas, -1)
            mask = shape(lay.listed_slots, rows, n)
            table, *masks = call(
                kernel(table_kernel),
                [shape(2 * lay.table + 1, dtype=jnp.int32)] + [mask] * 4,
                (me, metas, below, above),
                (),
                scratch=(places,),
                to_smem=1,
            )
            early += [*lower_locals[1:], *mate_lowers[1:], below, above]
            later += [table]
        parts = call(
            kernel(incoming_kernel),
            [chunk] * n_tile,
            (),
            (here, lower, mate_lower, arrived),
            scratch=(whole_rows, pltpu.VMEM((2 * cap, n, 2 * n), BF16), *fetching),
            fetched=(near,),
            early=early,
        )
        keep, give = parts[: n_tile // 2], parts[n_tile // 2 :]
        sums = summed([lax.optimization_barrier(x + swap(y, 1)) for x, y in zip(keep, give)])
        kept = [
            call(newton_kernel, [chunk], (), (x, y), early=later if x is kept[0] else ())[0]
            for x, y in zip(kept, sums)
        ]
        mated = [swap(x, 1) for x in kept]
    inverse = lax.optimization_barrier(jnp.concatenate(kept + mated, 0))

    def scale(side, sources):
        return call(
            kernel(scaled_kernel, side),
            [
                shape(lay.listed_slots, 2 * n, n, dtype=BF16),
                shape(lay.local_slots, 2 * n, n, dtype=BF16),
            ],
            (table,),
            (inverse, *sources),
            flops=product * 24,
        )

    share = vectors // (n_tile // 2)
    block = shape(rows, share, n)
    (first,) = call(kernel(first_kernel), [block], (me,), (krylov_block, inverse))

    def sweeps(x, side, count, listed, local, early=()):
        base = x
        for sweep in range(count):
            arrived = along(x, 1, 1) if side == 1 else along(x, -1)
            (here,) = call(
                kernel(local_sum_kernel, side), [block], (table,), (x, local), flops=8 * n**2 * vectors * rows
            )
            (part,) = call(
                kernel(listed_sum_kernel),
                [block],
                (),
                (listed, *masks[2 * side - 2 : 2 * side], here, arrived),
                early=early if sweep == count - 1 else (),
            )
            x = base - (part + swap(part, 1))
        return x

    uppers = over_chips(upper)
    mate_uppers = [mate_upper] + [swap(x, 1) for x in uppers[1:]]
    low = [x for three in zip(lowers, lower_locals, mate_lowers) for x in three]
    up = [x for pair in zip(uppers, mate_uppers) for x in pair]
    solved = sweeps(first, 1, LSWEEPS, *scale(1, low), early=uppers[1:])
    solved = sweeps(solved, 2, USWEEPS, *scale(2, up))
    for bit in upper_bits:
        got = swap(solved, bit)
        solved = jnp.where(
            (me[0] & bit) == 0, jnp.concatenate([solved, got], 1), jnp.concatenate([got, solved], 1)
        )
    return (inverse[: lay.own_rows], solved)


def solution(mesh):
    placed = (
        P("dom", None, None),
        P(("dom", "tile"), None, None),
        P(("dom", "tile"), None, None),
        P("dom", "tile", None, None),
        P("dom", "tile"),
        P("dom", "tile"),
        P("dom", "tile", None, None),
    )
    return jax.shard_map(
        local,
        mesh=mesh,
        in_specs=placed,
        out_specs=(P(("dom", "tile"), None, None), P("dom", None, None)),
        check_vma=False,
    )
```

```python
import functools

import jax
import jax.numpy as jnp
from jax import lax
from jax.experimental import pallas as pl
from jax.experimental.pallas import tpu as pltpu
from jax.sharding import PartitionSpec as P

FSWEEPS = 2
LSWEEPS = 3
USWEEPS = 3
F32 = jnp.float32
BF16 = jnp.bfloat16


def split(a):
    hi = a.astype(BF16)
    return hi, (a - hi.astype(F32)).astype(BF16)


def beside(a):
    return jnp.concatenate(split(a), 1)


def matmul_beside(lhs, pair):
    out = jnp.dot(lhs, jnp.concatenate([pair, pair], 0), preferred_element_type=F32)
    n = pair.shape[1] // 2
    return out[:, :n] + out[:, n:]


def matmul_parts(ah, al, bh, bl):
    return matmul_beside(jnp.concatenate([ah, al], 1), jnp.concatenate([bh, bl], 1))


def matmul(a, b):
    return matmul_parts(*split(a), *split(b))


def times_tile(x, wide):
    v, n = x.shape
    stacked = jnp.concatenate(split(x), 0)
    out = lax.dot_general(stacked, wide, (((1,), (1,)), ((), ())), preferred_element_type=F32)
    return out[:v, :n] + (out[v:, :n] + out[:v, n:])


def widen(a):
    return jnp.concatenate(split(a), 0)


class Layout:
    def __init__(self, rows, width, cap, n_tile):
        self.rows, self.width, self.cap, self.n_tile = rows, width, cap, n_tile
        self.slots = rows * width
        self.own_rows = rows // n_tile
        self.pairs = max(1, (self.slots - 4 * cap) // 2)
        self.listed_slots = n_tile * cap
        self.local_slots = n_tile // 2 * self.pairs
        self.table = self.listed_slots + 2 * self.local_slots

    def kind(self, meta, s):
        return meta[s]

    def link(self, meta, s):
        return meta[self.slots + s]

    def listed(self, meta, which, j):
        return meta[2 * self.slots + which * self.cap + j]

    def place(self, r, me):
        far = (r // self.own_rows) ^ me
        return ((far & 1) * (self.n_tile // 2) + (far >> 1)) * self.own_rows + r % self.own_rows

    def lookup(self, meta, which, side, j):
        s = self.listed(meta, which, j)
        v = self.link(meta, s) - self.slots - (which % 2) * self.cap
        live = (self.kind(meta, s) == side) & (v >= 0) & (v < self.cap)
        return s, live, jnp.clip(v, 0, self.cap - 1)

    def is_local(self, meta, s, side):
        return (self.kind(meta, s) == side) & (self.link(meta, s) < self.slots)

    def scan(self, meta, side, places):
        count = jnp.int32(0)
        for s in range(self.slots):
            places[count] = s
            count = count + self.is_local(meta, s, side).astype(jnp.int32)
        return count


def smem():
    return pl.BlockSpec(memory_space=pltpu.SMEM)


def vmem():
    return pl.BlockSpec(memory_space=pltpu.VMEM)


def call(body, outs, scalars, arrays, flops=0, scratch=(), early=(), to_smem=0, fetched=()):
    moved = sum(a.size * a.dtype.itemsize for a in arrays) + sum(o.size * o.dtype.itemsize for o in outs)
    return pl.pallas_call(
        body if not early else lambda *refs: body(*refs[len(early) :]),
        out_shape=outs,
        in_specs=[pl.BlockSpec(memory_space=pl.ANY)] * (len(early) + len(fetched)) + [smem()] * len(scalars) + [vmem()] * len(arrays),
        out_specs=[smem()] * to_smem + [vmem()] * (len(outs) - to_smem),
        scratch_shapes=list(scratch),
        compiler_params=pltpu.CompilerParams(vmem_limit_bytes=8 << 20),
        cost_estimate=pl.CostEstimate(flops=flops, bytes_accessed=moved, transcendentals=0),
    )(*early, *fetched, *scalars, *arrays)


def listed_tiles(lay, meta, side, tiles, out):
    for which in range(2):
        for j in range(lay.cap):
            s, live, _ = lay.lookup(meta, 4 - 2 * side + which, side, j)
            out[which * lay.cap + j] = jnp.where(live, tiles[s], 0.0)


def outgoing_products(lay, inverse, near_source, near, done, halves, tile_of, out):
    fetch = pltpu.make_async_copy(near_source, near, done)
    fetch.start()
    for r in range(lay.rows):
        halves[r] = beside(inverse[r])
    fetch.wait()
    me, metas = near.at[0], (near.at[1], near.at[2])
    for g, meta in enumerate(metas):
        for j in range(lay.cap):
            s, live, _ = lay.lookup(meta, me[0] % 2, 2, j)
            tile = tile_of(g, me[0] % 2 * lay.cap + j, s, live)
            out[g * lay.cap + j] = matmul_beside(halves[lay.place(s // lay.width, me[0])], beside(tile))


def outgoing_kernel(lay, near_source, inverse, tiles, mate_tiles, out, lower, halves, near, done):
    held = (tiles, mate_tiles)
    outgoing_products(
        lay, inverse, near_source, near, done, halves, lambda g, k, s, live: jnp.where(live, held[g][s], 0.0), out
    )
    listed_tiles(lay, near.at[1], 1, tiles, lower)


def next_outgoing_kernel(lay, near_source, inverse, upper, mate_upper, out, halves, near, done):
    held = (upper, mate_upper)
    outgoing_products(lay, inverse, near_source, near, done, halves, lambda g, k, s, live: held[g][k], out)


def local_terms(lay, me, mine, inverse, diag, tiles, out):
    out[: lay.own_rows] = -diag[...]
    out[lay.own_rows :] = jnp.zeros((lay.rows - lay.own_rows,) + diag.shape[1:], F32)

    @pl.loop(0, lay.slots)
    def _(s):
        @pl.when(lay.is_local(mine, s, 1))
        def _():
            v = lay.link(mine, s)
            q = matmul(inverse[lay.place(v // lay.width, me[0])], tiles[v])
            out[lay.place(s // lay.width, me[0])] += matmul(tiles[s], q)


def local_pivot_kernel(
    lay, near, inverse, diag, tiles, mate_tiles, out, mate_lower, lower_local, upper, mate_upper, places
):
    me, mine, mates = near.at[0], near.at[1], near.at[2]
    local_terms(lay, me, mine, inverse, diag, tiles, out)
    listed_tiles(lay, mates, 1, mate_tiles, mate_lower)
    listed_tiles(lay, mates, 2, mate_tiles, mate_upper)
    listed_tiles(lay, mine, 2, tiles, upper)
    for side, target, start in ((1, lower_local, 0), (2, upper, 2 * lay.cap)):
        count = lay.scan(mine, side, places)
        for i in range(lay.pairs):
            live = i < count
            target[start + i] = jnp.where(live, tiles[jnp.where(live, places[i], 0)], 0.0)


def next_local_pivot_kernel(lay, near, inverse, diag, tiles, out):
    local_terms(lay, near.at[0], near.at[1], inverse, diag, tiles, out)


def incoming_kernel(lay, near_source, local, lower, mate_lower, arrived, *refs):
    *outs, total, halves, near, done = refs
    fetch = pltpu.make_async_copy(near_source, near, done)
    fetch.start()
    total[...] = local[...]
    for k in range(2 * lay.cap):
        halves[k] = beside(arrived[k])
    fetch.wait()
    me, mine, mates = near.at[0], near.at[1], near.at[2]
    role = me[0] % 2
    places, terms = [], []
    for g, (meta, source) in enumerate(((mine, lower), (mates, mate_lower))):
        for j in range(lay.cap):
            s, _, v = lay.lookup(meta, 2 + role, 1, j)
            places.append(lay.place(s // lay.width, me[0]))
            terms.append(matmul_beside(beside(source[role * lay.cap + j]), halves[g * lay.cap + v]))
    for place, term in zip(places, terms):
        total[place] += term
    for c, out in enumerate(outs):
        out[...] = total[c * lay.own_rows : (c + 1) * lay.own_rows]


def newton_kernel(inverse, sums, out):
    for i in range(out.shape[0]):
        x = inverse[i]
        xh, xl = split(x)
        product = matmul_parts(xh, xl, *split(sums[i]))
        out[i] = 2.0 * x + matmul_parts(*split(product), xh, xl)


def vector_role(side, me):
    return (me + side) % 2


def table_kernel(lay, me, metas, peers_below, peers_above, out, *refs):
    masks, places = refs[:4], refs[4]
    out[2 * lay.table] = me[0]
    row = lax.broadcasted_iota(jnp.int32, masks[0].shape[1:], 0)
    for side in (1, 2):
        role = vector_role(side, me[0])
        start = (side - 1) * lay.table
        base, peers = ((2, peers_below), (0, peers_above))[side - 1]
        for q in range(lay.n_tile):
            a, meta, peer = q ^ me[0], metas.at[q], peers.at[q]
            for j in range(lay.cap):
                s, _, v = lay.lookup(meta, base + role, side, j)
                out[start + a * lay.cap + j] = s // lay.width
                source = lay.listed(peer, 2 - base + role, v) // lay.width
                masks[2 * side - 2][a * lay.cap + j] = (row == s // lay.width).astype(F32)
                masks[2 * side - 1][a * lay.cap + j] = (row == source).astype(F32)
        for q in range(0, lay.n_tile, 2):
            meta = metas.at[q]
            begin = start + lay.listed_slots + ((q ^ me[0]) >> 1) * lay.pairs
            count = lay.scan(meta, side, places)
            for i in range(lay.pairs):
                s = jnp.where(i < count, places[i], 0)
                out[begin + i] = s // lay.width
                v = jnp.where(i < count, lay.link(meta, s), 0)
                out[begin + lay.local_slots + i] = v // lay.width


def scaled_kernel(lay, side, table, inverse, *refs):
    sources, (listed, local) = refs[:-2], refs[-2:]
    me = table[2 * lay.table]
    role = vector_role(side, me)
    start = (side - 1) * lay.table

    def scaled(row, tile):
        return widen(matmul(inverse[lay.place(row, me)], tile))

    at = 0
    for q in range(lay.n_tile):
        lists = sources[at]
        for j in range(lay.cap):
            k = (q ^ me) * lay.cap + j
            listed[k] = scaled(table[start + k], lists[role * lay.cap + j])
        at += 1
        if q % 2 == 0:
            pairs, first = (lists, 2 * lay.cap) if side == 2 else (sources[at], 0)
            at += side == 1
            for i in range(lay.pairs):
                k = ((q ^ me) >> 1) * lay.pairs + i
                local[k] = scaled(table[start + lay.listed_slots + k], pairs[first + i])


def first_kernel(lay, me, base, inverse, out):
    count = out.shape[1]
    mine = pl.ds(pl.multiple_of((me[0] >> 1) * count, count), count)
    for r in range(lay.rows):
        out[r] = times_tile(base[r, mine], widen(inverse[lay.place(r, me[0])]))


def local_sum_kernel(lay, side, table, x, tiles, out):
    start = (side - 1) * lay.table + lay.listed_slots
    terms = [times_tile(x[table[start + lay.local_slots + k]], tiles[k]) for k in range(lay.local_slots)]
    out[...] = jnp.zeros_like(out)
    for k, value in enumerate(terms):
        out[table[start + k]] += value


def listed_sum_kernel(lay, tiles, picks, sources, local, arrived, out):
    rows = [arrived[r] for r in range(lay.rows)]
    terms = []
    for k in range(lay.listed_slots):
        x = sum(sources[k, r : r + 1] * rows[r] for r in range(lay.rows))
        terms.append(times_tile(x, tiles[k]))
    for r in range(lay.rows):
        out[r] = local[r] + sum(picks[k, r : r + 1] * terms[k] for k in range(lay.listed_slots))


def local(krylov_block, diag_block, inverse_prev, coupling_tiles, slot_kind, slot_link, send_slots):
    rows, width, n, _ = coupling_tiles.shape
    cap = send_slots.shape[3]
    n_dom, n_tile = lax.axis_size("dom"), lax.axis_size("tile")
    lay = Layout(rows, width, cap, n_tile)
    vectors = krylov_block.shape[1]
    upper_bits = [1 << b for b in range(1, n_tile.bit_length() - 1)]

    me = lax.axis_index("tile").astype(jnp.int32).reshape(1)
    mine = jnp.concatenate([slot_kind.reshape(-1), slot_link.reshape(-1), send_slots.reshape(-1)])
    tiles = coupling_tiles.reshape(lay.slots, n, n)

    def swap(x, bit):
        return lax.ppermute(x, "tile", [(i, i ^ bit) for i in range(n_tile)])

    def along(x, sign, swapped=0):
        route = []
        for d in range(n_dom):
            for t in range(n_tile):
                to = d + sign * (1 + (t + swapped) % 2)
                if 0 <= to < n_dom:
                    route.append((d * n_tile + t, to * n_tile + t))
        return lax.ppermute(x, ("dom", "tile"), route)

    def summed(parts):
        for bit in upper_bits:
            parts = [part + swap(parts[u ^ (bit // 2)], bit) for u, part in enumerate(parts)]
        return parts

    def shape(*dims, dtype=F32):
        return jax.ShapeDtypeStruct(dims, dtype)

    kernel = lambda body, *bound: functools.partial(body, lay, *bound)
    product = 8 * n**3

    def over_chips(x):
        held = [x]
        for bit in upper_bits:
            held += [swap(one, bit) for one in held]
        return held

    mate_tiles = swap(tiles, 1)
    arriving = over_chips(inverse_prev)
    mates = swap(mine, 1)
    given = swap(inverse_prev, 1)
    arriving, mine, mates, given = lax.optimization_barrier((arriving, mine, mates, given))
    near = jnp.stack([jnp.broadcast_to(me, mine.shape), mine, mates])
    kept = arriving
    mated = [given] + [swap(x, 1) for x in arriving[1:]]
    chunk = shape(lay.own_rows, n, n)
    lists, local_list = shape(2 * cap, n, n), shape(lay.pairs, n, n)
    places = pltpu.SMEM((lay.slots + 1,), jnp.int32)
    fetching = (pltpu.SMEM(near.shape, jnp.int32), pltpu.SemaphoreType.DMA)
    split_rows, whole_rows = pltpu.VMEM((rows, n, 2 * n), BF16), pltpu.VMEM((rows, n, n), F32)
    for sweep in range(FSWEEPS):
        inverse = jnp.concatenate(kept + mated, 0)
        early, later = [], []
        if sweep == 0:
            out, lower = call(
                kernel(outgoing_kernel),
                [lists] * 2,
                (),
                (inverse, tiles, mate_tiles),
                scratch=(split_rows, *fetching),
                fetched=(near,),
            )
            arrived = along(out, 1)
            lowers = over_chips(lower)
            here, mate_lower, lower_local, upper, mate_upper = call(
                kernel(local_pivot_kernel),
                [shape(rows, n, n), lists, local_list, shape(2 * cap + lay.pairs, n, n), lists],
                (near,),
                (inverse, diag_block, tiles, mate_tiles),
                flops=product * rows,
                scratch=(places,),
            )
            early += lowers[1:]
            later = over_chips(near[1:])
        else:
            (out,) = call(
                kernel(next_outgoing_kernel),
                [lists],
                (),
                (inverse, upper, mate_upper),
                scratch=(split_rows, *fetching),
                fetched=(near,),
            )
            arrived = along(out, 1)
            (here,) = call(
                kernel(next_local_pivot_kernel),
                [shape(rows, n, n)],
                (near,),
                (inverse, diag_block, tiles),
                flops=product * rows,
            )
        if sweep == FSWEEPS - 1:
            lower_locals = over_chips(lower_local)
            mate_lowers = [mate_lower] + [swap(x, 1) for x in lowers[1:]]
            below, above = along(metas, 1, 1), along(metas, -1)
            mask = shape(lay.listed_slots, rows, n)
            table, *masks = call(
                kernel(table_kernel),
                [shape(2 * lay.table + 1, dtype=jnp.int32)] + [mask] * 4,
                (me, metas, below, above),
                (),
                scratch=(places,),
                to_smem=1,
            )
            early += [*lower_locals[1:], *mate_lowers[1:], below, above]
            later += [table]
        parts = call(
            kernel(incoming_kernel),
            [chunk] * n_tile,
            (),
            (here, lower, mate_lower, arrived),
            scratch=(whole_rows, pltpu.VMEM((2 * cap, n, 2 * n), BF16), *fetching),
            fetched=(near,),
            early=early,
        )
        keep, give = parts[: n_tile // 2], parts[n_tile // 2 :]
        sums = summed([lax.optimization_barrier(x + swap(y, 1)) for x, y in zip(keep, give)])
        fresh = [call(newton_kernel, [chunk], (), (x, y))[0] for x, y in zip(kept[1:], sums[1:])]
        if sweep == 0:
            metas = jnp.concatenate(lax.optimization_barrier((later, fresh))[0], 0)
            later = [metas]
        kept = [*call(newton_kernel, [chunk], (), (kept[0], sums[0]), early=later), *fresh]
        mated = [swap(x, 1) for x in kept]
    inverse = lax.optimization_barrier(jnp.concatenate(kept + mated, 0))

    def scale(side, sources):
        return call(
            kernel(scaled_kernel, side),
            [
                shape(lay.listed_slots, 2 * n, n, dtype=BF16),
                shape(lay.local_slots, 2 * n, n, dtype=BF16),
            ],
            (table,),
            (inverse, *sources),
            flops=product * 24,
        )

    share = vectors // (n_tile // 2)
    block = shape(rows, share, n)
    (first,) = call(kernel(first_kernel), [block], (me,), (krylov_block, inverse))

    def sweeps(x, side, count, listed, local, early=()):
        base = x
        for sweep in range(count):
            arrived = along(x, 1, 1) if side == 1 else along(x, -1)
            (here,) = call(
                kernel(local_sum_kernel, side), [block], (table,), (x, local), flops=8 * n**2 * vectors * rows
            )
            (part,) = call(
                kernel(listed_sum_kernel),
                [block],
                (),
                (listed, *masks[2 * side - 2 : 2 * side], here, arrived),
                early=early if sweep == count - 1 else (),
            )
            x = base - (part + swap(part, 1))
        return x

    uppers = over_chips(upper)
    mate_uppers = [mate_upper] + [swap(x, 1) for x in uppers[1:]]
    low = [x for three in zip(lowers, lower_locals, mate_lowers) for x in three]
    up = [x for pair in zip(uppers, mate_uppers) for x in pair]
    solved = sweeps(first, 1, LSWEEPS, *scale(1, low), early=uppers[1:])
    solved = sweeps(solved, 2, USWEEPS, *scale(2, up))
    for bit in upper_bits:
        got = swap(solved, bit)
        solved = jnp.where(
            (me[0] & bit) == 0, jnp.concatenate([solved, got], 1), jnp.concatenate([got, solved], 1)
        )
    return (inverse[: lay.own_rows], solved)


def solution(mesh):
    placed = (
        P("dom", None, None),
        P(("dom", "tile"), None, None),
        P(("dom", "tile"), None, None),
        P("dom", "tile", None, None),
        P("dom", "tile"),
        P("dom", "tile"),
        P("dom", "tile", None, None),
    )
    return jax.shard_map(
        local,
        mesh=mesh,
        in_specs=placed,
        out_specs=(P(("dom", "tile"), None, None), P("dom", None, None)),
        check_vma=False,
    )
```

```python
import functools

import jax
import jax.numpy as jnp
from jax import lax
from jax.experimental import pallas as pl
from jax.experimental.pallas import tpu as pltpu
from jax.sharding import PartitionSpec as P

FSWEEPS = 2
LSWEEPS = 3
USWEEPS = 3
F32 = jnp.float32
BF16 = jnp.bfloat16


def split(a):
    hi = a.astype(BF16)
    return hi, (a - hi.astype(F32)).astype(BF16)


def beside(a):
    return jnp.concatenate(split(a), 1)


def matmul_beside(lhs, pair):
    out = jnp.dot(lhs, jnp.concatenate([pair, pair], 0), preferred_element_type=F32)
    n = pair.shape[1] // 2
    return out[:, :n] + out[:, n:]


def matmul_parts(ah, al, bh, bl):
    return matmul_beside(jnp.concatenate([ah, al], 1), jnp.concatenate([bh, bl], 1))


def matmul(a, b):
    return matmul_parts(*split(a), *split(b))


def times_tile(x, wide):
    v, n = x.shape
    stacked = jnp.concatenate(split(x), 0)
    out = lax.dot_general(stacked, wide, (((1,), (1,)), ((), ())), preferred_element_type=F32)
    return out[:v, :n] + (out[v:, :n] + out[:v, n:])


def widen(a):
    return jnp.concatenate(split(a), 0)


class Layout:
    def __init__(self, rows, width, cap, n_tile):
        self.rows, self.width, self.cap, self.n_tile = rows, width, cap, n_tile
        self.slots = rows * width
        self.own_rows = rows // n_tile
        self.pairs = max(1, (self.slots - 4 * cap) // 2)
        self.listed_slots = n_tile * cap
        self.local_slots = n_tile // 2 * self.pairs
        self.table = self.listed_slots + 2 * self.local_slots

    def kind(self, meta, s):
        return meta[s]

    def link(self, meta, s):
        return meta[self.slots + s]

    def listed(self, meta, which, j):
        return meta[2 * self.slots + which * self.cap + j]

    def place(self, r, me):
        far = (r // self.own_rows) ^ me
        return ((far & 1) * (self.n_tile // 2) + (far >> 1)) * self.own_rows + r % self.own_rows

    def lookup(self, meta, which, side, j):
        s = self.listed(meta, which, j)
        v = self.link(meta, s) - self.slots - (which % 2) * self.cap
        live = (self.kind(meta, s) == side) & (v >= 0) & (v < self.cap)
        return s, live, jnp.clip(v, 0, self.cap - 1)

    def is_local(self, meta, s, side):
        return (self.kind(meta, s) == side) & (self.link(meta, s) < self.slots)

    def scan(self, meta, side, places):
        count = jnp.int32(0)
        for s in range(self.slots):
            places[count] = s
            count = count + self.is_local(meta, s, side).astype(jnp.int32)
        return count


def smem():
    return pl.BlockSpec(memory_space=pltpu.SMEM)


def vmem():
    return pl.BlockSpec(memory_space=pltpu.VMEM)


def call(body, outs, scalars, arrays, flops=0, scratch=(), early=(), to_smem=0, fetched=()):
    moved = sum(a.size * a.dtype.itemsize for a in arrays) + sum(o.size * o.dtype.itemsize for o in outs)
    return pl.pallas_call(
        body if not early else lambda *refs: body(*refs[len(early) :]),
        out_shape=outs,
        in_specs=[pl.BlockSpec(memory_space=pl.ANY)] * (len(early) + len(fetched)) + [smem()] * len(scalars) + [vmem()] * len(arrays),
        out_specs=[smem()] * to_smem + [vmem()] * (len(outs) - to_smem),
        scratch_shapes=list(scratch),
        compiler_params=pltpu.CompilerParams(vmem_limit_bytes=8 << 20),
        cost_estimate=pl.CostEstimate(flops=flops, bytes_accessed=moved, transcendentals=0),
    )(*early, *fetched, *scalars, *arrays)


def listed_tiles(lay, meta, side, tiles, out):
    for which in range(2):
        for j in range(lay.cap):
            s, live, _ = lay.lookup(meta, 4 - 2 * side + which, side, j)
            out[which * lay.cap + j] = jnp.where(live, tiles[s], 0.0)


def outgoing_products(lay, inverse, near_source, near, done, halves, tile_of, out):
    fetch = pltpu.make_async_copy(near_source, near, done)
    fetch.start()
    for r in range(lay.rows):
        halves[r] = beside(inverse[r])
    fetch.wait()
    me, metas = near.at[0], (near.at[1], near.at[2])
    for g, meta in enumerate(metas):
        for j in range(lay.cap):
            s, live, _ = lay.lookup(meta, me[0] % 2, 2, j)
            tile = tile_of(g, me[0] % 2 * lay.cap + j, s, live)
            out[g * lay.cap + j] = matmul_beside(halves[lay.place(s // lay.width, me[0])], beside(tile))


def outgoing_kernel(lay, near_source, inverse, tiles, mate_tiles, out, lower, halves, near, done):
    held = (tiles, mate_tiles)
    outgoing_products(
        lay, inverse, near_source, near, done, halves, lambda g, k, s, live: jnp.where(live, held[g][s], 0.0), out
    )
    listed_tiles(lay, near.at[1], 1, tiles, lower)


def next_outgoing_kernel(lay, near_source, inverse, upper, mate_upper, out, halves, near, done):
    held = (upper, mate_upper)
    outgoing_products(lay, inverse, near_source, near, done, halves, lambda g, k, s, live: held[g][k], out)


def local_terms(lay, me, mine, inverse, diag, tiles, out):
    out[: lay.own_rows] = -diag[...]
    out[lay.own_rows :] = jnp.zeros((lay.rows - lay.own_rows,) + diag.shape[1:], F32)

    @pl.loop(0, lay.slots)
    def _(s):
        @pl.when(lay.is_local(mine, s, 1))
        def _():
            v = lay.link(mine, s)
            q = matmul(inverse[lay.place(v // lay.width, me[0])], tiles[v])
            out[lay.place(s // lay.width, me[0])] += matmul(tiles[s], q)


def local_pivot_kernel(
    lay, near, inverse, diag, tiles, mate_tiles, out, mate_lower, lower_local, upper, mate_upper, places
):
    me, mine, mates = near.at[0], near.at[1], near.at[2]
    local_terms(lay, me, mine, inverse, diag, tiles, out)
    listed_tiles(lay, mates, 1, mate_tiles, mate_lower)
    listed_tiles(lay, mates, 2, mate_tiles, mate_upper)
    listed_tiles(lay, mine, 2, tiles, upper)
    for side, target, start in ((1, lower_local, 0), (2, upper, 2 * lay.cap)):
        count = lay.scan(mine, side, places)
        for i in range(lay.pairs):
            live = i < count
            target[start + i] = jnp.where(live, tiles[jnp.where(live, places[i], 0)], 0.0)


def next_local_pivot_kernel(lay, near, inverse, diag, tiles, out):
    local_terms(lay, near.at[0], near.at[1], inverse, diag, tiles, out)


def incoming_kernel(lay, near_source, local, lower, mate_lower, arrived, *refs):
    *outs, total, halves, near, done = refs
    fetch = pltpu.make_async_copy(near_source, near, done)
    fetch.start()
    total[...] = local[...]
    for k in range(2 * lay.cap):
        halves[k] = beside(arrived[k])
    fetch.wait()
    me, mine, mates = near.at[0], near.at[1], near.at[2]
    role = me[0] % 2
    for g, (meta, source) in enumerate(((mine, lower), (mates, mate_lower))):
        for j in range(lay.cap):
            s, _, v = lay.lookup(meta, 2 + role, 1, j)
            place = lay.place(s // lay.width, me[0])
            total[place] += matmul_beside(beside(source[role * lay.cap + j]), halves[g * lay.cap + v])
    for c, out in enumerate(outs):
        out[...] = total[c * lay.own_rows : (c + 1) * lay.own_rows]


def newton_kernel(inverse, sums, out):
    for i in range(out.shape[0]):
        x = inverse[i]
        xh, xl = split(x)
        product = matmul_parts(xh, xl, *split(sums[i]))
        out[i] = 2.0 * x + matmul_parts(*split(product), xh, xl)


def vector_role(side, me):
    return (me + side) % 2


def table_kernel(lay, me, metas, peers_below, peers_above, out, *refs):
    masks, places = refs[:4], refs[4]
    out[2 * lay.table] = me[0]
    row = lax.broadcasted_iota(jnp.int32, masks[0].shape[1:], 0)
    for side in (1, 2):
        role = vector_role(side, me[0])
        start = (side - 1) * lay.table
        base, peers = ((2, peers_below), (0, peers_above))[side - 1]
        for q in range(lay.n_tile):
            a, meta, peer = q ^ me[0], metas.at[q], peers.at[q]
            for j in range(lay.cap):
                s, _, v = lay.lookup(meta, base + role, side, j)
                out[start + a * lay.cap + j] = s // lay.width
                source = lay.listed(peer, 2 - base + role, v) // lay.width
                masks[2 * side - 2][a * lay.cap + j] = (row == s // lay.width).astype(F32)
                masks[2 * side - 1][a * lay.cap + j] = (row == source).astype(F32)
        for q in range(0, lay.n_tile, 2):
            meta = metas.at[q]
            begin = start + lay.listed_slots + ((q ^ me[0]) >> 1) * lay.pairs
            count = lay.scan(meta, side, places)
            for i in range(lay.pairs):
                s = jnp.where(i < count, places[i], 0)
                out[begin + i] = s // lay.width
                v = jnp.where(i < count, lay.link(meta, s), 0)
                out[begin + lay.local_slots + i] = v // lay.width


def scaled_kernel(lay, side, table, inverse, *refs):
    sources, (listed, local) = refs[:-2], refs[-2:]
    me = table[2 * lay.table]
    role = vector_role(side, me)
    start = (side - 1) * lay.table

    def scaled(row, tile):
        return widen(matmul(inverse[lay.place(row, me)], tile))

    at = 0
    for q in range(lay.n_tile):
        lists = sources[at]
        for j in range(lay.cap):
            k = (q ^ me) * lay.cap + j
            listed[k] = scaled(table[start + k], lists[role * lay.cap + j])
        at += 1
        if q % 2 == 0:
            pairs, first = (lists, 2 * lay.cap) if side == 2 else (sources[at], 0)
            at += side == 1
            for i in range(lay.pairs):
                k = ((q ^ me) >> 1) * lay.pairs + i
                local[k] = scaled(table[start + lay.listed_slots + k], pairs[first + i])


def first_kernel(lay, me, base, inverse, out):
    count = out.shape[1]
    mine = pl.ds(pl.multiple_of((me[0] >> 1) * count, count), count)
    for r in range(lay.rows):
        out[r] = times_tile(base[r, mine], widen(inverse[lay.place(r, me[0])]))


def local_sum_kernel(lay, side, table, x, tiles, out):
    start = (side - 1) * lay.table + lay.listed_slots
    terms = [times_tile(x[table[start + lay.local_slots + k]], tiles[k]) for k in range(lay.local_slots)]
    out[...] = jnp.zeros_like(out)
    for k, value in enumerate(terms):
        out[table[start + k]] += value


def listed_sum_kernel(lay, tiles, picks, sources, local, arrived, out):
    rows = [arrived[r] for r in range(lay.rows)]
    terms = []
    for k in range(lay.listed_slots):
        x = sum(sources[k, r : r + 1] * rows[r] for r in range(lay.rows))
        terms.append(times_tile(x, tiles[k]))
    for r in range(lay.rows):
        out[r] = local[r] + sum(picks[k, r : r + 1] * terms[k] for k in range(lay.listed_slots))


def local(krylov_block, diag_block, inverse_prev, coupling_tiles, slot_kind, slot_link, send_slots):
    rows, width, n, _ = coupling_tiles.shape
    cap = send_slots.shape[3]
    n_dom, n_tile = lax.axis_size("dom"), lax.axis_size("tile")
    lay = Layout(rows, width, cap, n_tile)
    vectors = krylov_block.shape[1]
    upper_bits = [1 << b for b in range(1, n_tile.bit_length() - 1)]

    me = lax.axis_index("tile").astype(jnp.int32).reshape(1)
    mine = jnp.concatenate([slot_kind.reshape(-1), slot_link.reshape(-1), send_slots.reshape(-1)])
    tiles = coupling_tiles.reshape(lay.slots, n, n)

    def swap(x, bit):
        return lax.ppermute(x, "tile", [(i, i ^ bit) for i in range(n_tile)])

    def along(x, sign, swapped=0):
        route = []
        for d in range(n_dom):
            for t in range(n_tile):
                to = d + sign * (1 + (t + swapped) % 2)
                if 0 <= to < n_dom:
                    route.append((d * n_tile + t, to * n_tile + t))
        return lax.ppermute(x, ("dom", "tile"), route)

    def summed(parts):
        for bit in upper_bits:
            parts = [part + swap(parts[u ^ (bit // 2)], bit) for u, part in enumerate(parts)]
        return parts

    def shape(*dims, dtype=F32):
        return jax.ShapeDtypeStruct(dims, dtype)

    kernel = lambda body, *bound: functools.partial(body, lay, *bound)
    product = 8 * n**3

    def over_chips(x):
        held = [x]
        for bit in upper_bits:
            held += [swap(one, bit) for one in held]
        return held

    mate_tiles = swap(tiles, 1)
    arriving = over_chips(inverse_prev)
    mates = swap(mine, 1)
    given = swap(inverse_prev, 1)
    arriving, mine, mates, given = lax.optimization_barrier((arriving, mine, mates, given))
    near = jnp.stack([jnp.broadcast_to(me, mine.shape), mine, mates])
    kept = arriving
    mated = [given] + [swap(x, 1) for x in arriving[1:]]
    chunk = shape(lay.own_rows, n, n)
    lists, local_list = shape(2 * cap, n, n), shape(lay.pairs, n, n)
    places = pltpu.SMEM((lay.slots + 1,), jnp.int32)
    fetching = (pltpu.SMEM(near.shape, jnp.int32), pltpu.SemaphoreType.DMA)
    split_rows, whole_rows = pltpu.VMEM((rows, n, 2 * n), BF16), pltpu.VMEM((rows, n, n), F32)
    for sweep in range(FSWEEPS):
        inverse = jnp.concatenate(kept + mated, 0)
        early, later = [], []
        if sweep == 0:
            out, lower = call(
                kernel(outgoing_kernel),
                [lists] * 2,
                (),
                (inverse, tiles, mate_tiles),
                scratch=(split_rows, *fetching),
                fetched=(near,),
            )
            arrived = along(out, 1)
            lowers = over_chips(lower)
            here, mate_lower, lower_local, upper, mate_upper = call(
                kernel(local_pivot_kernel),
                [shape(rows, n, n), lists, local_list, shape(2 * cap + lay.pairs, n, n), lists],
                (near,),
                (inverse, diag_block, tiles, mate_tiles),
                flops=product * rows,
                scratch=(places,),
            )
            early += lowers[1:]
            later = over_chips(near[1:])
        else:
            (out,) = call(
                kernel(next_outgoing_kernel),
                [lists],
                (),
                (inverse, upper, mate_upper),
                scratch=(split_rows, *fetching),
                fetched=(near,),
            )
            arrived = along(out, 1)
            (here,) = call(
                kernel(next_local_pivot_kernel),
                [shape(rows, n, n)],
                (near,),
                (inverse, diag_block, tiles),
                flops=product * rows,
            )
        if sweep == FSWEEPS - 1:
            lower_locals = over_chips(lower_local)
            mate_lowers = [mate_lower] + [swap(x, 1) for x in lowers[1:]]
            below, above = along(metas, 1, 1), along(metas, -1)
            mask = shape(lay.listed_slots, rows, n)
            table, *masks = call(
                kernel(table_kernel),
                [shape(2 * lay.table + 1, dtype=jnp.int32)] + [mask] * 4,
                (me, metas, below, above),
                (),
                scratch=(places,),
                to_smem=1,
            )
            early += [*lower_locals[1:], *mate_lowers[1:], below, above]
            later += [table]
        parts = call(
            kernel(incoming_kernel),
            [chunk] * n_tile,
            (),
            (here, lower, mate_lower, arrived),
            scratch=(whole_rows, pltpu.VMEM((2 * cap, n, 2 * n), BF16), *fetching),
            fetched=(near,),
            early=early,
        )
        keep, give = parts[: n_tile // 2], parts[n_tile // 2 :]
        sums = summed([lax.optimization_barrier(x + swap(y, 1)) for x, y in zip(keep, give)])
        fresh = [call(newton_kernel, [chunk], (), (x, y))[0] for x, y in zip(kept[1:], sums[1:])]
        if sweep == 0:
            metas = jnp.concatenate(lax.optimization_barrier((later, fresh))[0], 0)
            later = [metas]
        kept = [*call(newton_kernel, [chunk], (), (kept[0], sums[0]), early=later), *fresh]
        mated = [swap(x, 1) for x in kept]
    inverse = lax.optimization_barrier(jnp.concatenate(kept + mated, 0))

    def scale(side, sources):
        return call(
            kernel(scaled_kernel, side),
            [
                shape(lay.listed_slots, 2 * n, n, dtype=BF16),
                shape(lay.local_slots, 2 * n, n, dtype=BF16),
            ],
            (table,),
            (inverse, *sources),
            flops=product * 24,
        )

    share = vectors // (n_tile // 2)
    block = shape(rows, share, n)
    (first,) = call(kernel(first_kernel), [block], (me,), (krylov_block, inverse))

    def sweeps(x, side, count, listed, local, early=()):
        base = x
        for sweep in range(count):
            arrived = along(x, 1, 1) if side == 1 else along(x, -1)
            (here,) = call(
                kernel(local_sum_kernel, side), [block], (table,), (x, local), flops=8 * n**2 * vectors * rows
            )
            (part,) = call(
                kernel(listed_sum_kernel),
                [block],
                (),
                (listed, *masks[2 * side - 2 : 2 * side], here, arrived),
                early=early if sweep == count - 1 else (),
            )
            x = base - (part + swap(part, 1))
        return x

    uppers = over_chips(upper)
    mate_uppers = [mate_upper] + [swap(x, 1) for x in uppers[1:]]
    low = [x for three in zip(lowers, lower_locals, mate_lowers) for x in three]
    up = [x for pair in zip(uppers, mate_uppers) for x in pair]
    solved = sweeps(first, 1, LSWEEPS, *scale(1, low), early=uppers[1:])
    solved = sweeps(solved, 2, USWEEPS, *scale(2, up))
    for bit in upper_bits:
        got = swap(solved, bit)
        solved = jnp.where(
            (me[0] & bit) == 0, jnp.concatenate([solved, got], 1), jnp.concatenate([got, solved], 1)
        )
    return (inverse[: lay.own_rows], solved)


def solution(mesh):
    placed = (
        P("dom", None, None),
        P(("dom", "tile"), None, None),
        P(("dom", "tile"), None, None),
        P("dom", "tile", None, None),
        P("dom", "tile"),
        P("dom", "tile"),
        P("dom", "tile", None, None),
    )
    return jax.shard_map(
        local,
        mesh=mesh,
        in_specs=placed,
        out_specs=(P(("dom", "tile"), None, None), P("dom", None, None)),
        check_vma=False,
    )
```
